32 devices in a mesh: groups: 1, ep: 32 (over z, y, x, core), section: 1.
Axes of the slice: x: 2, y: 2, z: 4, core: 2. Of those that a mesh axis runs over, the one named last changes fastest.
Arguments:
- moe_rows: bfloat16 [2, 1024, 7168], P('section', ('groups', 'ep')), may hold values from -6 to 6
- routes: int32 [2, 1024, 2], P('section', ('groups', 'ep')), may hold values from 0 to 3, all different within a row; in each aligned block of 32 rows (0 to 31, 32 to 63, ..., all dimensions but the last counted through in order) at most 24 rows name the same one
- route_gates: float32 [2, 1024, 2], P('section', ('groups', 'ep')), may hold values from 0.1 to 1
- gate_proj: bfloat16 [7168, 4096], P(None, 'ep'), may hold values from -0.0625 to 0.0625
- up_proj: bfloat16 [7168, 4096], P(None, 'ep'), may hold values from -0.0625 to 0.0625
- down_proj: bfloat16 [4096, 7168], P('ep'), may hold values from -0.1875 to 0.1875
- queries: bfloat16 [256, 128, 576], P(('groups', 'ep')), may hold values from -400 to 400
- cache_latents: bfloat16 [256, 256, 576], P(('groups', 'ep')), may hold values from -5 to 5
- cache_lens: int32 [256], P(('groups', 'ep')), may hold values from 1 to 256, 32768 in all
- prompt_latents: bfloat16 [4096, 576], P(('groups', 'ep')), may hold values from -5 to 5
- kv_owner: int32 [4096, 1], P(('groups', 'ep')), may hold values from 0 to 31; in each aligned block of 128 rows (0 to 127, 128 to 255, ...) at most 8 rows name the same one
- kv_request: int32 [4096], P(('groups', 'ep')), may hold values from 0 to 7
Outputs:
- expert_out: bfloat16 [2, 1024, 7168], P('section', ('groups', 'ep'))
- attended: bfloat16 [256, 128, 512], P(('groups', 'ep'))
The draws below stay inside these ranges and needn't reach their ends.
Inputs may be any that keep to these rules, and one draw needn't show every extreme that they name: `routes`: within each block of 32 rows of one section index and one ep index no expert is named by more than 24 rows, a bound that some block reaches. `kv_owner`: among the 128 rows of one ep index no owner is named by more than 8 rows, a bound that some block reaches.
All inputs are finite; a program needn't handle non-finite values. No bound on the sum of `cache_lens` on one device may be relied on, other than what follows from the above.
Results may differ from the reference program's by a relative error of at most 0.0057.
Values may be sent and summed in bfloat16 or wider, within the bound.
No kernel may reach another device: no remote copies, remote signals or barrier semaphores. Data moves between devices by JAX's collectives and lax.ppermute only.
A program may use at most 128 MiB of HBM per device.

```python
import math
import jax
import jax.numpy as jnp
import numpy as np
from jax import lax

D = 7168
HEADS = 128
VDIM = 512
LAT = 576
FF_WIN = 1024
HID_DEV = 128
EXPERTS_W = 4
TOPW = 2
ROWS = 32
CAP = 24
ROW_TOTAL = 1024
REQ = 8
CACHE = 256
STRETCH = 128
SENDCAP = 8
REQUESTS = 256
PROMPT_ROWS = 4096
N_EP = 32


def cache_base(key):
    return jnp.clip(jax.random.normal(key, (N_EP * REQ, CACHE, LAT), jnp.float32), -5.0, 5.0)


def draw_cache_latents(key, part):
    base = cache_base(key)
    return base.astype(jnp.bfloat16)


def draw_queries(key, part):
    key = jax.random.fold_in(key, 7)
    first_key = jax.random.fold_in(key, 0)
    query = jnp.clip(jax.random.normal(first_key, (N_EP * REQ, HEADS, LAT), jnp.float32), -5.0, 5.0)
    return query.astype(jnp.bfloat16)


def touch_ends(drawn, key, low, largest):
    extent = drawn.shape
    place = [jax.random.randint(jax.random.fold_in(key, axis), (), 0, extent[axis]) for axis in range(len(extent))]
    drawn = drawn.at[tuple(place)].set(low)
    longest = extent.index(max(extent))
    place[longest] = (place[longest] + 1) % extent[longest]
    return drawn.at[tuple(place)].set(largest)


def level_of(rng, extent, pieces, smallest, high):
    loudness, own = 1.0, jax.random.fold_in(rng, 6)
    for axis_at, shards_of in pieces:
        heights = jnp.exp(jax.random.uniform(jax.random.fold_in(own, axis_at), (shards_of,), jnp.float32, smallest / len(pieces), high / len(pieces)))
        loudness = loudness * jnp.repeat(heights, extent[axis_at] // shards_of).reshape([-1 if axis == axis_at else 1 for axis in range(len(extent))])
    return loudness


def split_up(amount, total, reach, skew):
    weights = [(1 << 20) // math.isqrt(rank ** skew) + 1 for rank in range(2, amount + 1)]
    spare, holding = total - reach - (amount - 1), [1] * (amount - 1)
    while spare > 0:
        free = [i for i in range(amount - 1) if holding[i] < reach]
        whole, left = sum([weights[i] for i in free]), spare
        for i in free:
            addition = min(reach - holding[i], max(1, left * weights[i] // whole), spare)
            holding[i] = holding[i] + addition
            spare = spare - addition
    return np.array([reach] + holding)


def uneven_parts(own_key, count, total, most, lean):
    if count == 2:
        one = jax.random.randint(own_key, (), max(1, total - most), min(most, total - 1) + 1)
        return jnp.stack([one, total - one])
    tallies = jnp.asarray(split_up(count, total, most, lean), jnp.int32)
    twos = (count - 1) // 2
    donor, receiver = tallies[1:1 + 2 * twos:2], tallies[2:2 + 2 * twos:2]
    margin = jnp.minimum(donor - 1, most - receiver)
    moved = jax.random.randint(jax.random.fold_in(own_key, 1), (twos,), 0, 1 << 20) % (margin + 1)
    tallies = tallies.at[1:1 + 2 * twos:2].set(donor - moved).at[2:2 + 2 * twos:2].set(receiver + moved)
    return tallies[jax.random.permutation(jax.random.fold_in(own_key, 2), count)]


def assign_block(stream_key, own, number, rows, amount, top, limit, lean):
    sequence = jax.random.permutation(stream_key, amount)
    crowded, ordinary = shares(amount, rows * top, limit, lean, True), shares(amount, rows * top, limit, lean, False)
    places = jnp.arange(amount)

    def named(lengths, turn):
        used = int((lengths > 0).sum())
        fixed = max(1, used // 4)
        moved = fixed + (places - fixed + turn * (used - fixed)) % max(1, amount - fixed)
        return jnp.zeros((amount,), jnp.int32).at[sequence[jnp.where(places < fixed, places, moved)]].set(jnp.asarray(lengths, jnp.int32))

    lengths = jnp.where(number % 4 == 0, named(crowded, number // 4), named(ordinary, number - number // 4 - 1))
    mixed = jax.random.permutation(jax.random.fold_in(own, 3), amount)
    donor, sink = mixed[0:amount // 2 * 2:2], mixed[1:amount // 2 * 2:2]
    room = jnp.minimum(lengths[donor] - 1, limit - lengths[sink]) // 2
    room = jnp.where((donor == sequence[0]) | (sink == sequence[0]) | (lengths[sink] == 0), 0, jnp.maximum(room, 0))
    moved = jax.random.randint(jax.random.fold_in(own, 4), (amount // 2,), 0, 1 << 20) % (room + 1)
    lengths = lengths.at[donor].add(-moved).at[sink].add(moved)
    members = jnp.searchsorted(jnp.cumsum(lengths), jnp.arange(rows * top), side="right").astype(jnp.int32)
    table = members.reshape(top, rows).T
    table = table[jax.random.permutation(jax.random.fold_in(own, 1), rows)]
    turn = jax.random.randint(jax.random.fold_in(own, 2), (rows, 1), 0, top)
    return jnp.take_along_axis(table, (jnp.arange(top)[None, :] + turn) % top, axis=1)


def shares(count, total, bound, slope, full):
    weights = [(1 << 20) // math.isqrt(grade ** slope) + 1 for grade in range(1, count + 1)]
    largest = bound if full else min(bound, max(-(-total // count), total * weights[0] // sum(weights)))
    least = 1 if total - largest >= count - 1 else 0
    given, rest = [largest] + [least] * (count - 1), total - largest - least * (count - 1)
    while rest > 0:
        movable = [i for i in range(1, count) if given[i] < largest] or [i for i in range(1, count) if given[i] < bound]
        pool, left = sum([weights[i] for i in movable]), rest
        for i in movable:
            extra = min(bound - given[i], max(1, left * weights[i] // pool), rest)
            given[i] = given[i] + extra
            rest = rest - extra
    return np.array(given)


def bell_draw(key, shape, width, reach, cuts=(), kind=jnp.bfloat16):
    values = width * jax.random.normal(key, shape, jnp.float32)
    if cuts:
        values = values * level_of(key, shape, cuts, -0.22, 0.18)
    return jnp.clip(values, -reach, reach).astype(kind)


def setup_inputs(seed: int = 0, part: int = 0) -> dict:
    arg_keys = jax.random.split(jax.random.key(seed), 13)
    part_splits = jax.random.split(jax.random.fold_in(arg_keys[12], part), 13)
    moe_rows = bell_draw(part_splits[0], (2, ROW_TOTAL, D), 1.0, 6.0, ((1, 32),))
    routes_keys = jax.random.split(jax.random.fold_in(part_splits[1], 1), 2 * ROW_TOTAL // ROWS)
    routes_turns = jax.random.permutation(jax.random.fold_in(part_splits[1], 3), 2 * ROW_TOTAL // ROWS)
    routes = jax.vmap(lambda own, number: assign_block(jax.random.fold_in(part_splits[1], 2), own, number, ROWS, EXPERTS_W, TOPW, CAP, 2))(routes_keys, routes_turns).reshape((2, ROW_TOTAL, TOPW))
    route_gates = jnp.clip(jnp.exp(math.log(1.0) - 2.3025851 * jax.random.uniform(part_splits[2], (2, ROW_TOTAL, TOPW), jnp.float32) ** level_of(part_splits[2], (2, ROW_TOTAL, TOPW), ((1, 32),), -0.2, 0.2)), 0.1, 1.0)
    gate_proj = bell_draw(arg_keys[3], (D, EXPERTS_W * FF_WIN), D ** -0.5, 0.0625, ((1, 32),))
    up_proj = bell_draw(arg_keys[4], (D, EXPERTS_W * FF_WIN), D ** -0.5, 0.0625, ((1, 32),))
    down_proj = bell_draw(arg_keys[5], (EXPERTS_W * FF_WIN, D), FF_WIN ** -0.5, 0.1875, ((0, 32),))
    queries = draw_queries(jax.random.fold_in(jax.random.fold_in(arg_keys[12], part), 71), part)
    cache_latents = draw_cache_latents(jax.random.fold_in(jax.random.fold_in(arg_keys[12], part), 71), part)
    cache_lens = uneven_parts(part_splits[8], REQUESTS, REQUESTS * CACHE // 2, CACHE, 1).astype(jnp.int32)
    prompt_latents = bell_draw(part_splits[9], (PROMPT_ROWS, LAT), 1.0, 5.0, ((0, 32),))
    kv_owner_keys = jax.random.split(jax.random.fold_in(part_splits[10], 1), PROMPT_ROWS // STRETCH)
    kv_owner_turns = jax.random.permutation(jax.random.fold_in(part_splits[10], 3), PROMPT_ROWS // STRETCH)
    kv_owner = jax.vmap(lambda own, number: assign_block(jax.random.fold_in(part_splits[10], 2), own, number, STRETCH, N_EP, 1, SENDCAP, 2))(kv_owner_keys, kv_owner_turns).reshape((PROMPT_ROWS, 1))
    kv_request = touch_ends(jax.random.randint(part_splits[11], (PROMPT_ROWS,), 0, REQ), jax.random.fold_in(part_splits[11], 1), 0, REQ - 1).astype(jnp.int32)
    return dict(moe_rows=moe_rows, routes=routes, route_gates=route_gates, gate_proj=gate_proj, up_proj=up_proj, down_proj=down_proj, queries=queries, cache_latents=cache_latents, cache_lens=cache_lens, prompt_latents=prompt_latents, kv_owner=kv_owner, kv_request=kv_request)


score_scale = 0.07216878364870323


def attend_owner(query_block, cache_block, lens_block, handed, handed_id):
    query_wide = query_block.astype(jnp.float32)
    cache_wide = cache_block.astype(jnp.float32)
    handed_wide = handed.astype(jnp.float32)
    cache_scores = jnp.einsum("qhl,qcl->qhc", query_wide, cache_wide) * score_scale
    hand_scores = jnp.einsum("qhl,rl->qhr", query_wide, handed_wide) * score_scale
    cache_mask = (jnp.arange(cache_block.shape[1], dtype=jnp.int32)[None, :] < lens_block[:, None])[:, None, :]
    hand_mask = (handed_id[None, :] == jnp.arange(query_block.shape[0], dtype=jnp.int32)[:, None])[:, None, :]
    scores = jnp.concatenate([cache_scores, hand_scores], axis=2)
    masks = jnp.concatenate([jnp.broadcast_to(cache_mask, cache_scores.shape), jnp.broadcast_to(hand_mask, hand_scores.shape)], axis=2)
    scores = jnp.where(masks, scores, -jnp.inf)
    top = jnp.max(scores, axis=2, keepdims=True)
    expo = jnp.exp(scores - top)
    probs = (expo / jnp.sum(expo, axis=2, keepdims=True)).astype(jnp.bfloat16).astype(jnp.float32)
    count = cache_block.shape[1]
    result = jnp.einsum("qhc,qcv->qhv", probs[:, :, :count], cache_wide[:, :, :VDIM])
    result = result + jnp.einsum("qhr,rv->qhv", probs[:, :, count:], handed_wide[:, :VDIM])
    return result.astype(jnp.bfloat16)


def reference(moe_rows, routes, route_gates, gate_proj, up_proj, down_proj, queries, cache_latents, cache_lens, prompt_latents, kv_owner, kv_request):
    rows = moe_rows.reshape(-1, D)
    picks = routes.reshape(-1, TOPW)
    gates = route_gates.reshape(-1, TOPW)
    total = jnp.zeros((rows.shape[0], D), jnp.float32)
    for expert in range(EXPERTS_W):
        first = expert * FF_WIN
        gate_val = jnp.dot(rows, gate_proj[:, first:first + FF_WIN], preferred_element_type=jnp.float32)
        up_val = jnp.dot(rows, up_proj[:, first:first + FF_WIN], preferred_element_type=jnp.float32)
        hidden = (jax.nn.silu(gate_val) * up_val).astype(jnp.bfloat16)
        value = jnp.zeros((rows.shape[0], D), jnp.float32)
        for piece in range(FF_WIN // HID_DEV):
            start = piece * HID_DEV
            partial_value = jnp.dot(hidden[:, start:start + HID_DEV], down_proj[first + start:first + start + HID_DEV], preferred_element_type=jnp.float32).astype(jnp.bfloat16)
            value = value + lax.optimization_barrier(partial_value).astype(jnp.float32)
        weight = jnp.sum(jnp.where(picks == expert, gates, jnp.zeros_like(gates)), axis=1)
        total = total + weight[:, None] * value
    expert_out = total.astype(jnp.bfloat16).reshape(moe_rows.shape)

    owners = kv_owner[:, 0]
    order = jnp.argsort(owners, stable=True)
    span = 2 * STRETCH
    padded_lat = jnp.concatenate([prompt_latents[order], jnp.zeros((span, LAT), prompt_latents.dtype)], axis=0)
    padded_owner = jnp.concatenate([owners[order], jnp.full((span,), -1, jnp.int32)], axis=0)
    padded_req = jnp.concatenate([kv_request[order], jnp.full((span,), -1, jnp.int32)], axis=0)
    starts = jnp.sum((owners[None, :] < jnp.arange(N_EP, dtype=jnp.int32)[:, None]).astype(jnp.int32), axis=1).astype(jnp.int32)

    def per_owner(index):
        start = starts[index].astype(jnp.int32)
        handed = lax.dynamic_slice_in_dim(padded_lat, start, span, 0)
        owner_rows = lax.dynamic_slice_in_dim(padded_owner, start, span, 0)
        req_rows = lax.dynamic_slice_in_dim(padded_req, start, span, 0)
        handed_id = jnp.where(owner_rows == index, req_rows, -1).astype(jnp.int32)
        first = (index * REQ).astype(jnp.int32)
        query_block = lax.dynamic_slice_in_dim(queries, first, REQ, 0)
        cache_block = lax.dynamic_slice_in_dim(cache_latents, first, REQ, 0)
        lens_block = lax.dynamic_slice_in_dim(cache_lens, first, REQ, 0)
        return attend_owner(query_block, cache_block, lens_block, handed, handed_id)

    attended = lax.map(per_owner, jnp.arange(N_EP, dtype=jnp.int32)).reshape(N_EP * REQ, HEADS, VDIM)
    return expert_out, attended
```

```python
from functools import partial

import jax
import jax.numpy as jnp
from jax import lax
from jax.experimental import pallas as pl
from jax.experimental.pallas import tpu as pltpu
from jax.sharding import PartitionSpec as P

VDIM = 512
FF_WIN = 1024
SLOT_ROWS = 8
CORE, XBIT, YBIT = 1, 2, 4
VMEM_BYTES = 48 * 1024 * 1024


score_scale = 0.07216878364870323


def swap(value, bit):
    count = lax.axis_size("ep")
    return lax.ppermute(value, "ep", [(i, i ^ bit) for i in range(count)])


def shift(value, step):
    count = lax.axis_size("ep")
    return lax.ppermute(value, "ep", [(i, (i + step) % count) for i in range(count)])


def hidden_kernel(*refs):
    units, blocks, (mine, theirs, acc) = refs[:8], refs[8:12], refs[12:]
    step = pl.program_id(0)

    @pl.when(step == 0)
    def _():
        acc[...] = jnp.zeros_like(acc)

    rows = jnp.concatenate([unit[...] for unit in units], axis=0)
    wide = blocks[0].shape[1]
    for at, block in enumerate(blocks):
        acc[:, at * wide : (at + 1) * wide] += jnp.dot(
            rows, block[...], preferred_element_type=jnp.float32
        )

    @pl.when(step == pl.num_programs(0) - 1)
    def _():
        half = wide // 2
        count = mine.shape[0]
        for at in range(len(blocks)):
            gate = acc[:, at * wide : at * wide + half]
            up = acc[:, at * wide + half : (at + 1) * wide]
            hidden = (gate / (1.0 + jnp.exp(-gate)) * up).astype(jnp.bfloat16)
            mine[:, at * half : (at + 1) * half] = hidden[:count]
            theirs[:, at * half : (at + 1) * half] = hidden[count:]


def hidden_units(units, blocks):
    rows, width = units[0].shape
    wide = blocks[0].shape[1]
    chunk = 1024
    count = rows * len(units) // 2
    out = jax.ShapeDtypeStruct((count, len(blocks) * wide // 2), jnp.bfloat16)
    return pl.pallas_call(
        hidden_kernel,
        grid=(width // chunk,),
        in_specs=[pl.BlockSpec((rows, chunk), lambda k: (0, k)) for _ in units]
        + [pl.BlockSpec((chunk, wide), lambda k: (k, 0)) for _ in blocks],
        out_specs=[pl.BlockSpec(out.shape, lambda k: (0, 0))] * 2,
        out_shape=[out, out],
        scratch_shapes=[pltpu.VMEM((2 * count, len(blocks) * wide), jnp.float32)],
        compiler_params=pltpu.CompilerParams(vmem_limit_bytes=VMEM_BYTES),
        cost_estimate=pl.CostEstimate(
            flops=2 * 2 * count * width * len(blocks) * wide,
            bytes_accessed=2 * (2 * count * width + len(blocks) * wide * width),
            transcendentals=0,
        ),
    )(*units, *blocks)


def down_kernel(planes, *refs):
    mine, other, weight, blocks, outs = refs[0], refs[1], refs[2], refs[3:-planes], refs[-planes:]
    hidden = jnp.concatenate([mine[...], other[...]], axis=1)
    table = jnp.concatenate([block[...] for block in blocks], axis=0)
    value = jnp.dot(hidden, table, preferred_element_type=jnp.float32) * weight[...]
    rows = outs[0].shape[0]
    for at, out in enumerate(outs):
        out[...] = value[at * rows : (at + 1) * rows].astype(out.dtype)


def down_values(mine, other, weight, blocks, planes):
    count, inner = mine.shape
    width = blocks[0].shape[1]
    rows = count // planes
    chunk = 1024 if width % 1024 == 0 else 512
    kinds = [jnp.float32] * (planes - 1) + [jnp.bfloat16]
    return pl.pallas_call(
        partial(down_kernel, planes),
        grid=(width // chunk,),
        in_specs=[
            pl.BlockSpec((count, inner), lambda k: (0, 0)),
            pl.BlockSpec((count, inner), lambda k: (0, 0)),
            pl.BlockSpec((count, 1), lambda k: (0, 0)),
        ]
        + [pl.BlockSpec((block.shape[0], chunk), lambda k: (0, k)) for block in blocks],
        out_specs=[pl.BlockSpec((rows, chunk), lambda k: (0, k)) for _ in kinds],
        out_shape=[jax.ShapeDtypeStruct((rows, width), kind) for kind in kinds],
        compiler_params=pltpu.CompilerParams(vmem_limit_bytes=VMEM_BYTES),
        cost_estimate=pl.CostEstimate(
            flops=2 * count * 2 * inner * width,
            bytes_accessed=2 * 2 * inner * width + 4 * count * width,
            transcendentals=0,
        ),
    )(mine, other, weight, *blocks)


def after(value, *others):
    return lax.optimization_barrier((value, *others))[0]


def expert_rows(rows, weight, gate_proj, up_proj, down_proj):
    n_ep = lax.axis_size("ep")
    split = FF_WIN // gate_proj.shape[1]
    planes = n_ep // split
    gate_up = jnp.concatenate([gate_proj, up_proj], axis=1)
    units = [rows]
    for _ in range(planes - 1):
        units.append(shift(units[-1], split))
    peers = [swap(unit, YBIT) for unit in units]
    block_x = swap(gate_up, XBIT)
    blocks = [gate_up, swap(gate_up, CORE), block_x, swap(block_x, CORE)]
    mine, theirs = hidden_units(units + peers, blocks)
    other = swap(theirs, YBIT)

    down = after(down_proj, block_x, peers[-1])
    half = down.shape[0] // 2
    down_x, down_y = swap(down, XBIT), swap(down, YBIT)
    corner = jnp.concatenate([swap(down_x[:half], YBIT), swap(down_y[half:], XBIT)], axis=0)
    tables = []
    for own in (down, down_x, down_y, corner):
        tables += [own, swap(own, CORE)]
    values = down_values(mine, other, weight, tables, planes)
    total = values[-1]
    for at in range(planes - 2, -1, -1):
        total = (shift(total, n_ep - split).astype(jnp.float32) + values[at]).astype(jnp.bfloat16)
    return total


def attend(query_part, cache_latents, cache_lens, handed, handed_mark):
    requests = query_part.shape[0]
    cache_scores = (
        jnp.einsum("qhl,qcl->qhc", query_part, cache_latents, preferred_element_type=jnp.float32)
        * score_scale
    )
    hand_scores = (
        jnp.einsum("qhl,rl->qhr", query_part, handed, preferred_element_type=jnp.float32)
        * score_scale
    )
    cache_mask = (
        jnp.arange(cache_latents.shape[1], dtype=jnp.int32)[None, :] < cache_lens[:, None]
    )[:, None, :]
    marks = jnp.arange(1, requests + 1, dtype=jnp.int32).astype(jnp.float32)
    hand_mask = (handed_mark[None, :] == marks[:, None])[:, None, :]
    cache_scores = jnp.where(cache_mask, cache_scores, -jnp.inf)
    hand_scores = jnp.where(hand_mask, hand_scores, -jnp.inf)
    top = jnp.maximum(jnp.max(cache_scores, axis=2), jnp.max(hand_scores, axis=2))[:, :, None]
    cache_expo = jnp.exp(cache_scores - top)
    hand_expo = jnp.exp(hand_scores - top)
    denom = (jnp.sum(cache_expo, axis=2) + jnp.sum(hand_expo, axis=2))[:, :, None]
    cache_prob = (cache_expo / denom).astype(jnp.bfloat16)
    hand_prob = (hand_expo / denom).astype(jnp.bfloat16)
    result = jnp.einsum(
        "qhc,qcv->qhv", cache_prob, cache_latents[:, :, :VDIM], preferred_element_type=jnp.float32
    )
    result = result + jnp.einsum(
        "qhr,rv->qhv", hand_prob, handed[:, :VDIM], preferred_element_type=jnp.float32
    )
    return result.astype(jnp.bfloat16)


def pieces(value):
    parts = []
    for _ in range(3):
        part = lax.reduce_precision(value, 8, 7)
        parts.append(part.astype(jnp.bfloat16))
        value = value - part
    return parts


def hand_over(prompt_latents, owners, requests, picks, gates, split):
    n_ep = lax.axis_size("ep")
    stretch, lat = prompt_latents.shape
    cap = 2 * stretch // n_ep
    places = jnp.arange(stretch, dtype=jnp.int32)
    earlier = (owners[:, None] == owners[None, :]) & (places[None, :] < places[:, None])
    target = owners * cap + jnp.sum(earlier.astype(jnp.int32), axis=1)
    slots = jnp.arange(n_ep * cap, dtype=jnp.int32)
    chosen = slots[:, None] == target[None, :]
    packed = jnp.dot(
        chosen.astype(jnp.bfloat16), prompt_latents, preferred_element_type=jnp.float32
    ).astype(jnp.bfloat16)
    mark = jnp.sum(jnp.where(chosen, requests[None, :] + 1, 0), axis=1).astype(jnp.bfloat16)
    planes = n_ep // split
    experts = jnp.arange(planes, dtype=jnp.int32)
    weights = jnp.sum(
        jnp.where(picks[None] == experts[:, None, None], gates[None], jnp.zeros_like(gates)[None]),
        axis=2,
    )
    lanes = weights.shape[1] // cap
    table = jnp.concatenate(
        [part.reshape(planes, 1, cap, lanes) for part in pieces(weights)], axis=3
    )
    table = jnp.broadcast_to(table, (planes, split, cap, 3 * lanes)).reshape(n_ep, cap, 3 * lanes)
    fill = -(lat + 1 + 3 * lanes) % 128
    outgoing = jnp.concatenate(
        [
            packed.reshape(n_ep, cap, lat),
            mark.reshape(n_ep, cap, 1),
            table,
            jnp.zeros((n_ep, cap, fill), jnp.bfloat16),
        ],
        axis=2,
    )
    incoming = lax.all_to_all(outgoing, "ep", split_axis=0, concat_axis=0, tiled=True)
    handed = incoming[:, :, :lat].reshape(n_ep * cap, lat)
    handed_mark = incoming[:, :, lat].reshape(n_ep * cap).astype(jnp.float32)
    here = lax.axis_index("ep")
    found = []
    for step in range(planes):
        source = (here - step * split + n_ep) % n_ep
        tile = lax.dynamic_index_in_dim(incoming, source, 0, keepdims=False)
        tile = tile[:, lat + 1 : lat + 1 + 3 * lanes].astype(jnp.float32)
        tile = tile.reshape(cap, 3, lanes)
        found.append((tile[:, 0] + tile[:, 1] + tile[:, 2]).reshape(cap * lanes, 1))
    return handed, handed_mark, jnp.concatenate(found, axis=0)


def on_device(
    moe_rows,
    routes,
    route_gates,
    gate_proj,
    up_proj,
    down_proj,
    queries,
    cache_latents,
    cache_lens,
    prompt_latents,
    kv_owner,
    kv_request,
):
    sections, count, width = moe_rows.shape
    top = routes.shape[2]
    split = FF_WIN // gate_proj.shape[1]
    handed, handed_mark, weight = hand_over(
        prompt_latents,
        kv_owner[:, 0],
        kv_request,
        routes.reshape(sections * count, top),
        route_gates.reshape(sections * count, top),
        split,
    )
    expert_out = expert_rows(
        moe_rows.reshape(sections * count, width), weight, gate_proj, up_proj, down_proj
    ).reshape(moe_rows.shape)
    attended = attend(queries, cache_latents, cache_lens, handed, handed_mark)
    return (expert_out, attended)


def solution(mesh):
    placed = (
        P("section", ("groups", "ep"), None),
        P("section", ("groups", "ep"), None),
        P("section", ("groups", "ep"), None),
        P(None, "ep"),
        P(None, "ep"),
        P("ep", None),
        P(("groups", "ep"), None, None),
        P(("groups", "ep"), None, None),
        P(("groups", "ep")),
        P(("groups", "ep"), None),
        P(("groups", "ep"), None),
        P(("groups", "ep")),
    )
    return jax.shard_map(
        on_device,
        mesh=mesh,
        in_specs=placed,
        out_specs=(P("section", ("groups", "ep"), None), P(("groups", "ep"), None, None)),
        check_vma=False,
    )
```

```python
from functools import partial

import jax
import jax.numpy as jnp
from jax import lax
from jax.experimental import pallas as pl
from jax.experimental.pallas import tpu as pltpu
from jax.sharding import PartitionSpec as P

VDIM = 512
FF_WIN = 1024
SLOT_ROWS = 8
CORE, XBIT, YBIT = 1, 2, 4
VMEM_BYTES = 48 * 1024 * 1024


score_scale = 0.07216878364870323


def swap(value, bit):
    count = lax.axis_size("ep")
    return lax.ppermute(value, "ep", [(i, i ^ bit) for i in range(count)])


def shift(value, step):
    count = lax.axis_size("ep")
    return lax.ppermute(value, "ep", [(i, (i + step) % count) for i in range(count)])


def together(*values):
    return lax.optimization_barrier(values)


def hidden_kernel(lead, *refs):
    units, firsts, seconds, (mine, theirs, acc) = refs[:8], refs[8:12], refs[12:16], refs[16:]
    step = pl.program_id(0)

    @pl.when(step == 0)
    def _():
        acc[...] = jnp.zeros_like(acc)

    wide = firsts[0].shape[1]

    def add(blocks):
        rows = jnp.concatenate([unit[...] for unit in units], axis=0)
        for at, block in enumerate(blocks):
            acc[:, at * wide : (at + 1) * wide] += jnp.dot(
                rows, block[...], preferred_element_type=jnp.float32
            )

    @pl.when(step < lead)
    def _():
        add(firsts)

    @pl.when(step >= lead)
    def _():
        add(seconds)

    @pl.when(step == pl.num_programs(0) - 1)
    def _():
        half = wide // 2
        count = mine.shape[0]
        for at in range(len(firsts)):
            gate = acc[:, at * wide : at * wide + half]
            up = acc[:, at * wide + half : (at + 1) * wide]
            hidden = (gate / (1.0 + jnp.exp(-gate)) * up).astype(jnp.bfloat16)
            mine[:, at * half : (at + 1) * half] = hidden[:count]
            theirs[:, at * half : (at + 1) * half] = hidden[count:]


def hidden_units(units, firsts, seconds, chunk):
    rows, width = units[0].shape
    lead, wide = firsts[0].shape[0] // chunk, firsts[0].shape[1]
    count = rows * len(units) // 2
    across = len(firsts) * wide
    out = jax.ShapeDtypeStruct((count, across // 2), jnp.bfloat16)
    return pl.pallas_call(
        partial(hidden_kernel, lead),
        grid=(width // chunk,),
        in_specs=[pl.BlockSpec((rows, chunk), lambda k: (0, k)) for _ in units]
        + [pl.BlockSpec((chunk, wide), lambda k: (jnp.minimum(k, lead - 1), 0)) for _ in firsts]
        + [pl.BlockSpec((chunk, wide), lambda k: (jnp.maximum(k - lead, 0), 0)) for _ in seconds],
        out_specs=[pl.BlockSpec(out.shape, lambda k: (0, 0))] * 2,
        out_shape=[out, out],
        scratch_shapes=[pltpu.VMEM((2 * count, across), jnp.float32)],
        compiler_params=pltpu.CompilerParams(vmem_limit_bytes=VMEM_BYTES),
        cost_estimate=pl.CostEstimate(
            flops=2 * 2 * count * width * across,
            bytes_accessed=2 * (2 * count * width + across * width),
            transcendentals=0,
        ),
    )(*units, *firsts, *seconds)


def down_kernel(planes, *refs):
    mine, other, weight, blocks, outs = refs[0], refs[1], refs[2], refs[3:-planes], refs[-planes:]
    hidden = jnp.concatenate([mine[...], other[...]], axis=1)
    table = jnp.concatenate([block[...] for block in blocks], axis=0)
    value = jnp.dot(hidden, table, preferred_element_type=jnp.float32) * weight[...]
    rows = outs[0].shape[0]
    for at, out in enumerate(outs):
        out[...] = value[at * rows : (at + 1) * rows].astype(out.dtype)


def down_values(mine, other, weight, blocks, planes):
    count, inner = mine.shape
    width = blocks[0].shape[1]
    rows = count // planes
    chunk = 896 if width % 896 == 0 else 512
    kinds = [jnp.float32] * (planes - 1) + [jnp.bfloat16]
    return pl.pallas_call(
        partial(down_kernel, planes),
        grid=(width // chunk,),
        in_specs=[
            pl.BlockSpec((count, inner), lambda k: (0, 0)),
            pl.BlockSpec((count, inner), lambda k: (0, 0)),
            pl.BlockSpec((count, 1), lambda k: (0, 0)),
        ]
        + [pl.BlockSpec((block.shape[0], chunk), lambda k: (0, k)) for block in blocks],
        out_specs=[pl.BlockSpec((rows, chunk), lambda k: (0, k)) for _ in kinds],
        out_shape=[jax.ShapeDtypeStruct((rows, width), kind) for kind in kinds],
        compiler_params=pltpu.CompilerParams(vmem_limit_bytes=VMEM_BYTES),
        cost_estimate=pl.CostEstimate(
            flops=2 * count * 2 * inner * width,
            bytes_accessed=2 * 2 * inner * width + 4 * count * width,
            transcendentals=0,
        ),
    )(mine, other, weight, *blocks)


def expert_rows(rows, weight, gate_proj, up_proj, down_proj):
    n_ep = lax.axis_size("ep")
    split = FF_WIN // gate_proj.shape[1]
    planes = n_ep // split
    width = rows.shape[1]
    chunk = width // 7
    cut = 5 * chunk
    first = jnp.concatenate([gate_proj[:cut], up_proj[:cut]], axis=1)
    second = jnp.concatenate([gate_proj[cut:], up_proj[cut:]], axis=1)
    first_x = swap(first, XBIT)
    second, first_x = together(second, first_x)
    second_x = swap(second, XBIT)
    firsts = [first, swap(first, CORE), first_x, swap(first_x, CORE)]
    seconds = [second, swap(second, CORE), second_x, swap(second_x, CORE)]

    units, peers = [], []
    unit = rows
    for at in range(planes):
        units.append(unit)
        peer = swap(unit, YBIT)
        if at < planes - 1:
            unit, peer = together(shift(unit, split), peer)
        peers.append(peer)
    mine, theirs = hidden_units(units + peers, firsts, seconds, chunk)
    other = swap(theirs, YBIT)

    half = down_proj.shape[0] // 2
    span = width // 2
    ready = (second_x, peers[-1])
    values = []
    for at in range(2):
        down = together(down_proj[:, at * span : (at + 1) * span], *ready)[0]
        down_x, down_y = together(swap(down, XBIT), swap(down, YBIT))
        upper, lower = swap(down_x[:half], YBIT), swap(down_y[half:], XBIT)
        ready = (upper, lower)
        tables = []
        for own in (down, down_x, down_y):
            tables += [own, swap(own, CORE)]
        tables += [upper, lower, swap(upper, CORE), swap(lower, CORE)]
        values.append(down_values(mine, other, weight, tables, planes))
    outs = []
    for value in values:
        total = value[-1]
        for at in range(planes - 2, -1, -1):
            total = (shift(total, n_ep - split).astype(jnp.float32) + value[at]).astype(jnp.bfloat16)
        outs.append(total)
    return jnp.concatenate(outs, axis=1)


def attend(query_part, cache_latents, cache_lens, handed, handed_mark):
    requests = query_part.shape[0]
    cache_scores = (
        jnp.einsum("qhl,qcl->qhc", query_part, cache_latents, preferred_element_type=jnp.float32)
        * score_scale
    )
    hand_scores = (
        jnp.einsum("qhl,rl->qhr", query_part, handed, preferred_element_type=jnp.float32)
        * score_scale
    )
    cache_mask = (
        jnp.arange(cache_latents.shape[1], dtype=jnp.int32)[None, :] < cache_lens[:, None]
    )[:, None, :]
    marks = jnp.arange(1, requests + 1, dtype=jnp.int32).astype(jnp.float32)
    hand_mask = (handed_mark[None, :] == marks[:, None])[:, None, :]
    cache_scores = jnp.where(cache_mask, cache_scores, -jnp.inf)
    hand_scores = jnp.where(hand_mask, hand_scores, -jnp.inf)
    top = jnp.maximum(jnp.max(cache_scores, axis=2), jnp.max(hand_scores, axis=2))[:, :, None]
    cache_expo = jnp.exp(cache_scores - top)
    hand_expo = jnp.exp(hand_scores - top)
    denom = (jnp.sum(cache_expo, axis=2) + jnp.sum(hand_expo, axis=2))[:, :, None]
    cache_prob = (cache_expo / denom).astype(jnp.bfloat16)
    hand_prob = (hand_expo / denom).astype(jnp.bfloat16)
    result = jnp.einsum(
        "qhc,qcv->qhv", cache_prob, cache_latents[:, :, :VDIM], preferred_element_type=jnp.float32
    )
    result = result + jnp.einsum(
        "qhr,rv->qhv", hand_prob, handed[:, :VDIM], preferred_element_type=jnp.float32
    )
    return result.astype(jnp.bfloat16)


def pieces(value):
    parts = []
    for _ in range(3):
        part = lax.reduce_precision(value, 8, 7)
        parts.append(part.astype(jnp.bfloat16))
        value = value - part
    return parts


def hand_over(prompt_latents, owners, requests, picks, gates, split):
    n_ep = lax.axis_size("ep")
    stretch, lat = prompt_latents.shape
    cap = 2 * stretch // n_ep
    places = jnp.arange(stretch, dtype=jnp.int32)
    earlier = (owners[:, None] == owners[None, :]) & (places[None, :] < places[:, None])
    target = owners * cap + jnp.sum(earlier.astype(jnp.int32), axis=1)
    slots = jnp.arange(n_ep * cap, dtype=jnp.int32)
    chosen = slots[:, None] == target[None, :]
    packed = jnp.dot(
        chosen.astype(jnp.bfloat16), prompt_latents, preferred_element_type=jnp.float32
    ).astype(jnp.bfloat16)
    mark = jnp.sum(jnp.where(chosen, requests[None, :] + 1, 0), axis=1).astype(jnp.bfloat16)
    planes = n_ep // split
    experts = jnp.arange(planes, dtype=jnp.int32)
    weights = jnp.sum(
        jnp.where(picks[None] == experts[:, None, None], gates[None], jnp.zeros_like(gates)[None]),
        axis=2,
    )
    lanes = weights.shape[1] // cap
    table = jnp.concatenate(
        [part.reshape(planes, 1, cap, lanes) for part in pieces(weights)], axis=3
    )
    table = jnp.broadcast_to(table, (planes, split, cap, 3 * lanes)).reshape(n_ep, cap, 3 * lanes)
    fill = -(lat + 1 + 3 * lanes) % 128
    outgoing = jnp.concatenate(
        [
            packed.reshape(n_ep, cap, lat),
            mark.reshape(n_ep, cap, 1),
            table,
            jnp.zeros((n_ep, cap, fill), jnp.bfloat16),
        ],
        axis=2,
    )
    incoming = lax.all_to_all(outgoing, "ep", split_axis=0, concat_axis=0, tiled=True)
    handed = incoming[:, :, :lat].reshape(n_ep * cap, lat)
    handed_mark = incoming[:, :, lat].reshape(n_ep * cap).astype(jnp.float32)
    here = lax.axis_index("ep")
    found = []
    for step in range(planes):
        source = (here - step * split + n_ep) % n_ep
        tile = lax.dynamic_index_in_dim(incoming, source, 0, keepdims=False)
        tile = tile[:, lat + 1 : lat + 1 + 3 * lanes].astype(jnp.float32)
        tile = tile.reshape(cap, 3, lanes)
        found.append((tile[:, 0] + tile[:, 1] + tile[:, 2]).reshape(cap * lanes, 1))
    return handed, handed_mark, jnp.concatenate(found, axis=0)


def on_device(
    moe_rows,
    routes,
    route_gates,
    gate_proj,
    up_proj,
    down_proj,
    queries,
    cache_latents,
    cache_lens,
    prompt_latents,
    kv_owner,
    kv_request,
):
    sections, count, width = moe_rows.shape
    top = routes.shape[2]
    split = FF_WIN // gate_proj.shape[1]
    handed, handed_mark, weight = hand_over(
        prompt_latents,
        kv_owner[:, 0],
        kv_request,
        routes.reshape(sections * count, top),
        route_gates.reshape(sections * count, top),
        split,
    )
    expert_out = expert_rows(
        moe_rows.reshape(sections * count, width), weight, gate_proj, up_proj, down_proj
    ).reshape(moe_rows.shape)
    attended = attend(queries, cache_latents, cache_lens, handed, handed_mark)
    return (expert_out, attended)


def solution(mesh):
    placed = (
        P("section", ("groups", "ep"), None),
        P("section", ("groups", "ep"), None),
        P("section", ("groups", "ep"), None),
        P(None, "ep"),
        P(None, "ep"),
        P("ep", None),
        P(("groups", "ep"), None, None),
        P(("groups", "ep"), None, None),
        P(("groups", "ep")),
        P(("groups", "ep"), None),
        P(("groups", "ep"), None),
        P(("groups", "ep")),
    )
    return jax.shard_map(
        on_device,
        mesh=mesh,
        in_specs=placed,
        out_specs=(P("section", ("groups", "ep"), None), P(("groups", "ep"), None, None)),
        check_vma=False,
    )
```

```python
from functools import partial

import jax
import jax.numpy as jnp
from jax import lax
from jax.experimental import pallas as pl
from jax.experimental.pallas import tpu as pltpu
from jax.sharding import PartitionSpec as P

VDIM = 512
FF_WIN = 1024
SLOT_ROWS = 8
CORE, XBIT, YBIT = 1, 2, 4
VMEM_BYTES = 48 * 1024 * 1024


score_scale = 0.07216878364870323


def swap(value, bit):
    count = lax.axis_size("ep")
    return lax.ppermute(value, "ep", [(i, i ^ bit) for i in range(count)])


def shift(value, step):
    count = lax.axis_size("ep")
    return lax.ppermute(value, "ep", [(i, (i + step) % count) for i in range(count)])


def together(*values):
    return lax.optimization_barrier(values)


def pair_dot(rows, left, right):
    both = jnp.concatenate([left[...], right[...]], axis=1)
    return jnp.dot(rows, both, preferred_element_type=jnp.float32)


def gated(gate, up):
    return (gate / (1.0 + jnp.exp(-gate)) * up).astype(jnp.bfloat16)


def early_kernel(count, *refs):
    units, (gate_o, gate_c, gate_x, gate_xc, up_o, up_c) = refs[:count], refs[count : count + 6]
    near, far, acc_near, acc_up = refs[count + 6 :]
    step = pl.program_id(0)

    @pl.when(step == 0)
    def _():
        far[...] = jnp.zeros_like(far)
        acc_near[...] = jnp.zeros_like(acc_near)
        acc_up[...] = jnp.zeros_like(acc_up)

    rows = jnp.concatenate([unit[...] for unit in units], axis=0)
    far[...] += pair_dot(rows, gate_x, gate_xc)
    acc_near[...] += pair_dot(rows, gate_o, gate_c)
    acc_up[...] += pair_dot(rows, up_o, up_c)

    @pl.when(step == pl.num_programs(0) - 1)
    def _():
        near[...] = gated(acc_near[...], acc_up[...])


def early_hidden(units, weights, chunk):
    rows, width = units[0].shape
    wide = weights[0].shape[1]
    count = rows * len(units)
    return pl.pallas_call(
        partial(early_kernel, len(units)),
        grid=(width // chunk,),
        in_specs=[pl.BlockSpec((rows, chunk), lambda k: (0, k)) for _ in units]
        + [pl.BlockSpec((chunk, wide), lambda k: (k, 0)) for _ in weights],
        out_specs=[pl.BlockSpec((count, 2 * wide), lambda k: (0, 0))] * 2,
        out_shape=[
            jax.ShapeDtypeStruct((count, 2 * wide), jnp.bfloat16),
            jax.ShapeDtypeStruct((count, 2 * wide), jnp.float32),
        ],
        scratch_shapes=[pltpu.VMEM((count, 2 * wide), jnp.float32)] * 2,
        compiler_params=pltpu.CompilerParams(vmem_limit_bytes=VMEM_BYTES),
        cost_estimate=pl.CostEstimate(
            flops=2 * count * width * wide * len(weights),
            bytes_accessed=2 * width * (count + wide * len(weights)),
            transcendentals=0,
        ),
    )(*units, *weights)


def late_kernel(lead, count, *refs):
    units, last, (near, far) = refs[:count], refs[count : count + 2], refs[count + 2 : count + 4]
    gate_o, gate_c, gate_x, gate_xc, up_o, up_c = refs[count + 4 : count + 10]
    up_xa, up_xca, up_xb, up_xcb = refs[count + 10 : count + 14]
    out, acc, acc_last = refs[count + 14 :]
    step = pl.program_id(0)
    two = acc.shape[1]

    @pl.when(step == 0)
    def _():
        acc[...] = jnp.zeros_like(acc)
        acc_last[...] = jnp.zeros_like(acc_last)

    tail = jnp.concatenate([part[...] for part in last], axis=0)
    acc_last[:, :two] += pair_dot(tail, gate_o, gate_c)
    acc_last[:, two : 2 * two] += pair_dot(tail, gate_x, gate_xc)
    acc_last[:, 2 * two : 3 * two] += pair_dot(tail, up_o, up_c)

    def add(left, right):
        rows = jnp.concatenate([unit[...] for unit in units] + [tail], axis=0)
        acc[...] += pair_dot(rows, left, right)

    @pl.when(step < lead)
    def _():
        add(up_xa, up_xca)

    @pl.when(step >= lead)
    def _():
        add(up_xb, up_xcb)

    @pl.when(step == pl.num_programs(0) - 1)
    def _():
        early = far.shape[0]
        out[:early, :two] = near[...]
        out[:early, two:] = gated(far[...], acc[:early, :])
        out[early:, :two] = gated(acc_last[:, :two], acc_last[:, 2 * two : 3 * two])
        out[early:, two:] = gated(acc_last[:, two : 2 * two], acc[early:, :])


def late_hidden(units, last, near, far, weights, leads, rests, chunk):
    rows, width = units[0].shape
    wide = weights[0].shape[1]
    lead = leads[0].shape[0] // chunk
    early = rows * len(units)
    total = early + rows
    out = jax.ShapeDtypeStruct((total, 4 * wide), jnp.bfloat16)
    return pl.pallas_call(
        partial(late_kernel, lead, len(units)),
        grid=(width // chunk,),
        in_specs=[pl.BlockSpec((rows, chunk), lambda k: (0, k)) for _ in units]
        + [pl.BlockSpec((part.shape[0], chunk), lambda k: (0, k)) for part in last]
        + [pl.BlockSpec((early, 2 * wide), lambda k: (0, 0))] * 2
        + [pl.BlockSpec((chunk, wide), lambda k: (k, 0)) for _ in weights]
        + [pl.BlockSpec((chunk, wide), lambda k: (jnp.minimum(k, lead - 1), 0)) for _ in leads]
        + [pl.BlockSpec((chunk, wide), lambda k: (jnp.maximum(k - lead, 0), 0)) for _ in rests],
        out_specs=pl.BlockSpec(out.shape, lambda k: (0, 0)),
        out_shape=out,
        scratch_shapes=[
            pltpu.VMEM((total, 2 * wide), jnp.float32),
            pltpu.VMEM((rows, 6 * wide), jnp.float32),
        ],
        compiler_params=pltpu.CompilerParams(vmem_limit_bytes=VMEM_BYTES),
        cost_estimate=pl.CostEstimate(
            flops=2 * width * wide * (2 * total + 6 * rows),
            bytes_accessed=2 * width * (total + 8 * wide),
            transcendentals=0,
        ),
    )(*units, *last, near, far, *weights, *leads, *rests)


def down_kernel(planes, mine, other, weight, *refs):
    blocks, outs = refs[:-planes], refs[-planes:]
    table = jnp.concatenate([block[...] for block in blocks], axis=0)
    count = mine.shape[0] // 2
    rows = count // planes
    for part in range(2):
        here = slice(part * count, (part + 1) * count)
        there = slice((1 - part) * count, (2 - part) * count)
        joined = jnp.concatenate([mine[here, :], other[there, :]], axis=1)
        value = jnp.dot(joined, table, preferred_element_type=jnp.float32) * weight[here, :]
        for at, out in enumerate(outs):
            out[part * rows : (part + 1) * rows, :] = value[at * rows : (at + 1) * rows].astype(
                out.dtype
            )


def down_values(mine, other, weight, own, blocks, planes, chunk, offset):
    count, inner = mine.shape
    depth, width = blocks[0].shape
    rows = count // planes
    kinds = [jnp.float32] * (planes - 1) + [jnp.bfloat16]
    return pl.pallas_call(
        partial(down_kernel, planes),
        grid=(width // chunk,),
        in_specs=[pl.BlockSpec((count, inner), lambda k: (0, 0))] * 2
        + [pl.BlockSpec((count, 1), lambda k: (0, 0))]
        + [pl.BlockSpec((depth, chunk), lambda k: (0, k + offset)) for _ in own]
        + [pl.BlockSpec((depth, chunk), lambda k: (0, k)) for _ in blocks],
        out_specs=[pl.BlockSpec((rows, chunk), lambda k: (0, k)) for _ in kinds],
        out_shape=[jax.ShapeDtypeStruct((rows, width), kind) for kind in kinds],
        compiler_params=pltpu.CompilerParams(vmem_limit_bytes=VMEM_BYTES),
        cost_estimate=pl.CostEstimate(
            flops=2 * count * 2 * inner * width,
            bytes_accessed=2 * 2 * inner * width + 4 * count * width,
            transcendentals=0,
        ),
    )(mine, other, weight, *own, *blocks)


def expert_rows(rows, outgoing, gate_proj, up_proj, down_proj):
    n_ep = lax.axis_size("ep")
    split = FF_WIN // gate_proj.shape[1]
    planes = n_ep // split
    count, width = rows.shape
    chunk = width // 7
    cut = 5 * chunk

    upper = lax.axis_index("ep") // YBIT % 2
    span = width // 4
    keep = lax.dynamic_slice_in_dim(down_proj, 2 * upper * span, 2 * span, 1)
    send = lax.dynamic_slice_in_dim(down_proj, (2 - 2 * upper) * span, 2 * span, 1)
    keep_0, keep_1, send_0, send_1 = keep[:, :span], keep[:, span:], send[:, :span], send[:, span:]
    up_a, up_b = up_proj[:cut], up_proj[cut:]

    gate_x, gate_c = swap(gate_proj, XBIT), swap(gate_proj, CORE)
    unit_1, peer_0 = shift(rows, split), swap(rows, YBIT)
    unit_1, peer_0, gate_c = together(unit_1, peer_0, gate_c)
    up_c = swap(up_proj, CORE)
    unit_2, peer_1 = shift(unit_1, split), swap(unit_1, YBIT)
    unit_2, peer_1, gate_x, up_c, up_a, keep, outgoing = together(
        unit_2, peer_1, gate_x, up_c, up_a, keep, outgoing
    )
    up_xa, gate_xc, keep_c = swap(up_a, XBIT), swap(gate_x, CORE), swap(keep, CORE)
    incoming = lax.all_to_all(outgoing, "ep", split_axis=0, concat_axis=0, tiled=True)
    unit_3, peer_2 = shift(unit_2, split), swap(unit_2, YBIT)
    unit_3, peer_2, up_xa, gate_xc, keep_c, up_b, incoming = together(
        unit_3, peer_2, up_xa, gate_xc, keep_c, up_b, incoming
    )
    up_xb, up_xca = swap(up_b, XBIT), swap(up_xa, CORE)
    half = count // 2
    last = (shift(peer_2[:half], split), swap(unit_3[half:], YBIT))
    early = (rows, unit_1, unit_2, unit_3, peer_0, peer_1, peer_2)
    weights = (gate_proj, gate_c, gate_x, gate_xc, up_proj, up_c)
    near, far = early_hidden(early, weights, chunk)
    up_xb, up_xca, near, keep_0, send_0, *last = together(
        up_xb, up_xca, near, keep_0, send_0, *last
    )
    up_xcb = swap(up_xb, CORE)
    down_x, down_y = swap(keep_0, XBIT), swap(send_0, YBIT)
    hidden = late_hidden(
        early, last, near, far, weights, (up_xa, up_xca), (up_xb, up_xcb), chunk
    )
    other = swap(hidden, YBIT)
    down_x, down_y, hidden, incoming = together(down_x, down_y, hidden, incoming)
    weight = row_weights(incoming, count, planes, split)
    down_yx = swap(down_y, XBIT)
    first = (down_x, swap(down_x, CORE), down_y, swap(down_y, CORE), down_yx, swap(down_yx, CORE))
    keep_1, send_1, down_yx, other = together(keep_1, send_1, down_yx, other)
    down_x, down_y = swap(keep_1, XBIT), swap(send_1, YBIT)
    down_yx = swap(down_y, XBIT)
    second = (down_x, swap(down_x, CORE), down_y, swap(down_y, CORE), down_yx, swap(down_yx, CORE))

    outs, others = [], []
    for at, parts in enumerate((first, second)):
        values = down_values(
            hidden, other, weight, (keep, keep_c), parts, planes, span // 2, 2 * at
        )
        total = values[-1]
        for step in range(planes - 2, -1, -1):
            total = shift(total, n_ep - split).astype(jnp.float32) + values[step]
            total = total.astype(jnp.bfloat16)
        outs.append(total[:count])
        others.append(swap(total[count:], YBIT))
    low = jnp.concatenate(outs + others, axis=1)
    high = jnp.concatenate(others + outs, axis=1)
    return jnp.where(upper == 0, low, high), incoming


def attend(query_part, cache_latents, cache_lens, handed, handed_mark):
    requests = query_part.shape[0]
    cache_scores = (
        jnp.einsum("qhl,qcl->qhc", query_part, cache_latents, preferred_element_type=jnp.float32)
        * score_scale
    )
    hand_scores = (
        jnp.einsum("qhl,rl->qhr", query_part, handed, preferred_element_type=jnp.float32)
        * score_scale
    )
    cache_mask = (
        jnp.arange(cache_latents.shape[1], dtype=jnp.int32)[None, :] < cache_lens[:, None]
    )[:, None, :]
    marks = jnp.arange(1, requests + 1, dtype=jnp.int32).astype(jnp.float32)
    hand_mask = (handed_mark[None, :] == marks[:, None])[:, None, :]
    cache_scores = jnp.where(cache_mask, cache_scores, -jnp.inf)
    hand_scores = jnp.where(hand_mask, hand_scores, -jnp.inf)
    top = jnp.maximum(jnp.max(cache_scores, axis=2), jnp.max(hand_scores, axis=2))[:, :, None]
    cache_expo = jnp.exp(cache_scores - top)
    hand_expo = jnp.exp(hand_scores - top)
    denom = (jnp.sum(cache_expo, axis=2) + jnp.sum(hand_expo, axis=2))[:, :, None]
    cache_prob = (cache_expo / denom).astype(jnp.bfloat16)
    hand_prob = (hand_expo / denom).astype(jnp.bfloat16)
    result = jnp.einsum(
        "qhc,qcv->qhv", cache_prob, cache_latents[:, :, :VDIM], preferred_element_type=jnp.float32
    )
    result = result + jnp.einsum(
        "qhr,rv->qhv", hand_prob, handed[:, :VDIM], preferred_element_type=jnp.float32
    )
    return result.astype(jnp.bfloat16)


def pieces(value):
    parts = []
    for _ in range(3):
        part = lax.reduce_precision(value, 8, 7)
        parts.append(part.astype(jnp.bfloat16))
        value = value - part
    return parts


def hand_over(prompt_latents, owners, requests, picks, gates, split):
    n_ep = lax.axis_size("ep")
    stretch, lat = prompt_latents.shape
    cap = 2 * stretch // n_ep
    places = jnp.arange(stretch, dtype=jnp.int32)
    earlier = (owners[:, None] == owners[None, :]) & (places[None, :] < places[:, None])
    target = owners * cap + jnp.sum(earlier.astype(jnp.int32), axis=1)
    slots = jnp.arange(n_ep * cap, dtype=jnp.int32)
    chosen = slots[:, None] == target[None, :]
    packed = jnp.dot(
        chosen.astype(jnp.bfloat16), prompt_latents, preferred_element_type=jnp.float32
    ).astype(jnp.bfloat16)
    mark = jnp.sum(jnp.where(chosen, requests[None, :] + 1, 0), axis=1).astype(jnp.bfloat16)
    planes = n_ep // split
    experts = jnp.arange(planes, dtype=jnp.int32)
    weights = jnp.sum(
        jnp.where(picks[None] == experts[:, None, None], gates[None], jnp.zeros_like(gates)[None]),
        axis=2,
    )
    lanes = weights.shape[1] // cap
    table = jnp.concatenate(
        [part.reshape(planes, 1, cap, lanes) for part in pieces(weights)], axis=3
    )
    table = jnp.broadcast_to(table, (planes, split, cap, 3 * lanes)).reshape(n_ep, cap, 3 * lanes)
    fill = -(lat + 1 + 3 * lanes) % 128
    outgoing = jnp.concatenate(
        [
            packed.reshape(n_ep, cap, lat),
            mark.reshape(n_ep, cap, 1),
            jnp.zeros((n_ep, cap, fill), jnp.bfloat16),
            table,
        ],
        axis=2,
    )
    return outgoing


def row_weights(incoming, count, planes, split):
    n_ep, cap, width = incoming.shape
    lanes = count // cap
    start = width - 3 * lanes
    here = lax.axis_index("ep")
    found = []
    for place in (here, here ^ YBIT):
        for step in range(planes):
            source = (place - step * split + n_ep) % n_ep
            tile = lax.dynamic_slice(incoming, (source, 0, start), (1, cap, 3 * lanes))
            tile = tile.astype(jnp.float32).reshape(cap, 3, lanes)
            found.append((tile[:, 0] + tile[:, 1] + tile[:, 2]).reshape(count, 1))
    return jnp.concatenate(found, axis=0)


def on_device(
    moe_rows,
    routes,
    route_gates,
    gate_proj,
    up_proj,
    down_proj,
    queries,
    cache_latents,
    cache_lens,
    prompt_latents,
    kv_owner,
    kv_request,
):
    sections, count, width = moe_rows.shape
    top = routes.shape[2]
    split = FF_WIN // gate_proj.shape[1]
    outgoing = hand_over(
        prompt_latents,
        kv_owner[:, 0],
        kv_request,
        routes.reshape(sections * count, top),
        route_gates.reshape(sections * count, top),
        split,
    )
    expert_out, incoming = expert_rows(
        moe_rows.reshape(sections * count, width), outgoing, gate_proj, up_proj, down_proj
    )
    expert_out = expert_out.reshape(moe_rows.shape)
    lat = prompt_latents.shape[1]
    handed = incoming[:, :, :lat].reshape(-1, lat)
    handed_mark = incoming[:, :, lat].reshape(-1).astype(jnp.float32)
    attended = attend(queries, cache_latents, cache_lens, handed, handed_mark)
    return (expert_out, attended)


def solution(mesh):
    placed = (
        P("section", ("groups", "ep"), None),
        P("section", ("groups", "ep"), None),
        P("section", ("groups", "ep"), None),
        P(None, "ep"),
        P(None, "ep"),
        P("ep", None),
        P(("groups", "ep"), None, None),
        P(("groups", "ep"), None, None),
        P(("groups", "ep")),
        P(("groups", "ep"), None),
        P(("groups", "ep"), None),
        P(("groups", "ep")),
    )
    return jax.shard_map(
        on_device,
        mesh=mesh,
        in_specs=placed,
        out_specs=(P("section", ("groups", "ep"), None), P(("groups", "ep"), None, None)),
        check_vma=False,
    )
```

```python
from functools import partial

import jax
import jax.numpy as jnp
from jax import lax
from jax.experimental import pallas as pl
from jax.experimental.pallas import tpu as pltpu
from jax.sharding import PartitionSpec as P

VDIM = 512
FF_WIN = 1024
SLOT_ROWS = 8
CORE, XBIT, YBIT = 1, 2, 4
VMEM_BYTES = 14 * 1024 * 1024


score_scale = 0.07216878364870323


def swap(value, bit):
    count = lax.axis_size("ep")
    return lax.ppermute(value, "ep", [(i, i ^ bit) for i in range(count)])


def shift(value, step):
    count = lax.axis_size("ep")
    return lax.ppermute(value, "ep", [(i, (i + step) % count) for i in range(count)])


def together(*values):
    return lax.optimization_barrier(values)


def pair_dot(rows, left, right):
    both = jnp.concatenate([left[...], right[...]], axis=1)
    return jnp.dot(rows, both, preferred_element_type=jnp.float32)


def gated(gate, up):
    return (gate / (1.0 + jnp.exp(-gate)) * up).astype(jnp.bfloat16)


def early_kernel(count, *refs):
    units, (gate_o, gate_c, gate_x, gate_xc, up_o, up_c) = refs[:count], refs[count : count + 6]
    near, far, acc_near, acc_up = refs[count + 6 :]
    step = pl.program_id(0)

    @pl.when(step == 0)
    def _():
        far[...] = jnp.zeros_like(far)
        acc_near[...] = jnp.zeros_like(acc_near)
        acc_up[...] = jnp.zeros_like(acc_up)

    rows = jnp.concatenate([unit[...] for unit in units], axis=0)
    far[...] += pair_dot(rows, gate_x, gate_xc)
    acc_near[...] += pair_dot(rows, gate_o, gate_c)
    acc_up[...] += pair_dot(rows, up_o, up_c)

    @pl.when(step == pl.num_programs(0) - 1)
    def _():
        near[...] = gated(acc_near[...], acc_up[...])


def early_hidden(units, weights, chunk):
    rows, width = units[0].shape
    wide = weights[0].shape[1]
    count = rows * len(units)
    return pl.pallas_call(
        partial(early_kernel, len(units)),
        grid=(width // chunk,),
        in_specs=[pl.BlockSpec((rows, chunk), lambda k: (0, k)) for _ in units]
        + [pl.BlockSpec((chunk, wide), lambda k: (k, 0)) for _ in weights],
        out_specs=[pl.BlockSpec((count, 2 * wide), lambda k: (0, 0))] * 2,
        out_shape=[
            jax.ShapeDtypeStruct((count, 2 * wide), jnp.bfloat16),
            jax.ShapeDtypeStruct((count, 2 * wide), jnp.float32),
        ],
        scratch_shapes=[pltpu.VMEM((count, 2 * wide), jnp.float32)] * 2,
        compiler_params=pltpu.CompilerParams(vmem_limit_bytes=VMEM_BYTES),
        cost_estimate=pl.CostEstimate(
            flops=2 * count * width * wide * len(weights),
            bytes_accessed=2 * width * (count + wide * len(weights)),
            transcendentals=0,
        ),
    )(*units, *weights)


def late_kernel(lead, count, *refs):
    units, last, (near, far) = refs[:count], refs[count : count + 2], refs[count + 2 : count + 4]
    gate_o, gate_c, gate_x, gate_xc, up_o, up_c = refs[count + 4 : count + 10]
    up_xa, up_xca, up_xb, up_xcb = refs[count + 10 : count + 14]
    out, acc, acc_last = refs[count + 14 :]
    step = pl.program_id(0)
    two = acc.shape[1]

    @pl.when(step == 0)
    def _():
        acc[...] = jnp.zeros_like(acc)
        acc_last[...] = jnp.zeros_like(acc_last)

    tail = jnp.concatenate([part[...] for part in last], axis=0)
    acc_last[:, :two] += pair_dot(tail, gate_o, gate_c)
    acc_last[:, two : 2 * two] += pair_dot(tail, gate_x, gate_xc)
    acc_last[:, 2 * two : 3 * two] += pair_dot(tail, up_o, up_c)

    def add(left, right):
        rows = jnp.concatenate([unit[...] for unit in units] + [tail], axis=0)
        acc[...] += pair_dot(rows, left, right)

    @pl.when(step < lead)
    def _():
        add(up_xa, up_xca)

    @pl.when(step >= lead)
    def _():
        add(up_xb, up_xcb)

    @pl.when(step == pl.num_programs(0) - 1)
    def _():
        early = far.shape[0]
        out[:early, :two] = near[...]
        out[:early, two:] = gated(far[...], acc[:early, :])
        out[early:, :two] = gated(acc_last[:, :two], acc_last[:, 2 * two : 3 * two])
        out[early:, two:] = gated(acc_last[:, two : 2 * two], acc[early:, :])


def late_hidden(units, last, near, far, weights, leads, rests, chunk):
    rows, width = units[0].shape
    wide = weights[0].shape[1]
    lead = leads[0].shape[0] // chunk
    early = rows * len(units)
    total = early + rows
    out = jax.ShapeDtypeStruct((total, 4 * wide), jnp.bfloat16)
    return pl.pallas_call(
        partial(late_kernel, lead, len(units)),
        grid=(width // chunk,),
        in_specs=[pl.BlockSpec((rows, chunk), lambda k: (0, k)) for _ in units]
        + [pl.BlockSpec((part.shape[0], chunk), lambda k: (0, k)) for part in last]
        + [pl.BlockSpec((early, 2 * wide), lambda k: (0, 0))] * 2
        + [pl.BlockSpec((chunk, wide), lambda k: (k, 0)) for _ in weights]
        + [pl.BlockSpec((chunk, wide), lambda k: (jnp.minimum(k, lead - 1), 0)) for _ in leads]
        + [pl.BlockSpec((chunk, wide), lambda k: (jnp.maximum(k - lead, 0), 0)) for _ in rests],
        out_specs=pl.BlockSpec(out.shape, lambda k: (0, 0)),
        out_shape=out,
        scratch_shapes=[
            pltpu.VMEM((total, 2 * wide), jnp.float32),
            pltpu.VMEM((rows, 6 * wide), jnp.float32),
        ],
        compiler_params=pltpu.CompilerParams(vmem_limit_bytes=VMEM_BYTES),
        cost_estimate=pl.CostEstimate(
            flops=2 * width * wide * (2 * total + 6 * rows),
            bytes_accessed=2 * width * (total + 8 * wide),
            transcendentals=0,
        ),
    )(*units, *last, near, far, *weights, *leads, *rests)


def down_kernel(planes, mine, other, weight, *refs):
    blocks, outs = refs[:-planes], refs[-planes:]
    table = jnp.concatenate([block[...] for block in blocks], axis=0)
    count = mine.shape[0] // 2
    rows = count // planes
    for part in range(2):
        here = slice(part * count, (part + 1) * count)
        there = slice((1 - part) * count, (2 - part) * count)
        joined = jnp.concatenate([mine[here, :], other[there, :]], axis=1)
        value = jnp.dot(joined, table, preferred_element_type=jnp.float32) * weight[here, :]
        for at, out in enumerate(outs):
            out[part * rows : (part + 1) * rows, :] = value[at * rows : (at + 1) * rows].astype(
                out.dtype
            )


def down_values(mine, other, weight, own, blocks, planes, chunk, offset):
    count, inner = mine.shape
    depth, width = blocks[0].shape
    rows = count // planes
    kinds = [jnp.float32] * (planes - 1) + [jnp.bfloat16]
    return pl.pallas_call(
        partial(down_kernel, planes),
        grid=(width // chunk,),
        in_specs=[pl.BlockSpec((count, inner), lambda k: (0, 0))] * 2
        + [pl.BlockSpec((count, 1), lambda k: (0, 0))]
        + [pl.BlockSpec((depth, chunk), lambda k: (0, k + offset)) for _ in own]
        + [pl.BlockSpec((depth, chunk), lambda k: (0, k)) for _ in blocks],
        out_specs=[pl.BlockSpec((rows, chunk), lambda k: (0, k)) for _ in kinds],
        out_shape=[jax.ShapeDtypeStruct((rows, width), kind) for kind in kinds],
        compiler_params=pltpu.CompilerParams(vmem_limit_bytes=VMEM_BYTES),
        cost_estimate=pl.CostEstimate(
            flops=2 * count * 2 * inner * width,
            bytes_accessed=2 * 2 * inner * width + 4 * count * width,
            transcendentals=0,
        ),
    )(mine, other, weight, *own, *blocks)


def expert_rows(rows, outgoing, gate_proj, up_proj, down_proj):
    n_ep = lax.axis_size("ep")
    split = FF_WIN // gate_proj.shape[1]
    planes = n_ep // split
    count, width = rows.shape
    chunk = width // 7
    cut = 5 * chunk

    upper = lax.axis_index("ep") // YBIT % 2
    span = width // 4
    keep = lax.dynamic_slice_in_dim(down_proj, 2 * upper * span, 2 * span, 1)
    send = lax.dynamic_slice_in_dim(down_proj, (2 - 2 * upper) * span, 2 * span, 1)
    keep_0, keep_1, send_0, send_1 = keep[:, :span], keep[:, span:], send[:, :span], send[:, span:]
    up_a, up_b = up_proj[:cut], up_proj[cut:]

    gate_x, gate_c = swap(gate_proj, XBIT), swap(gate_proj, CORE)
    unit_1, peer_0 = shift(rows, split), swap(rows, YBIT)
    unit_1, peer_0, gate_c, outgoing = together(unit_1, peer_0, gate_c, outgoing)
    up_c = swap(up_proj, CORE)
    unit_2, peer_1 = shift(unit_1, split), swap(unit_1, YBIT)
    unit_2, peer_1, gate_x, up_c, up_a, keep = together(
        unit_2, peer_1, gate_x, up_c, up_a, keep
    )
    up_xa, gate_xc, keep_c = swap(up_a, XBIT), swap(gate_x, CORE), swap(keep, CORE)
    incoming = lax.all_to_all(outgoing, "ep", split_axis=0, concat_axis=0, tiled=True)
    unit_3, peer_2 = shift(unit_2, split), swap(unit_2, YBIT)
    unit_3, peer_2, up_xa, gate_xc, keep_c, up_b, keep_0, send_0 = together(
        unit_3, peer_2, up_xa, gate_xc, keep_c, up_b, keep_0, send_0
    )
    up_xb, up_xca = swap(up_b, XBIT), swap(up_xa, CORE)
    half = count // 2
    last = (shift(peer_2[:half], split), swap(unit_3[half:], YBIT))
    early = (rows, unit_1, unit_2, unit_3, peer_0, peer_1, peer_2)
    weights = (gate_proj, gate_c, gate_x, gate_xc, up_proj, up_c)
    near, far = early_hidden(early, weights, chunk)
    up_xb, up_xca, near, keep_0, send_0, incoming, *last = together(
        up_xb, up_xca, near, keep_0, send_0, incoming, *last
    )
    up_xcb = swap(up_xb, CORE)
    down_x, down_y = swap(keep_0, XBIT), swap(send_0, YBIT)
    hidden = late_hidden(
        early, last, near, far, weights, (up_xa, up_xca), (up_xb, up_xcb), chunk
    )
    other = swap(hidden, YBIT)
    down_x, down_y, hidden, incoming = together(down_x, down_y, hidden, incoming)
    weight = row_weights(incoming, count, planes, split)
    down_yx = swap(down_y, XBIT)
    first = (down_x, swap(down_x, CORE), down_y, swap(down_y, CORE), down_yx, swap(down_yx, CORE))
    keep_1, down_yx = together(keep_1, down_yx)
    send_1, other = together(send_1, other)
    down_x, down_y = swap(keep_1, XBIT), swap(send_1, YBIT)
    down_yx = swap(down_y, XBIT)
    second = (down_x, swap(down_x, CORE), down_y, swap(down_y, CORE), down_yx, swap(down_yx, CORE))

    outs, others = [], []
    for at, parts in enumerate((first, second)):
        values = down_values(
            hidden, other, weight, (keep, keep_c), parts, planes, span // 2, 2 * at
        )
        total = values[-1]
        for step in range(planes - 2, -1, -1):
            total = shift(total, n_ep - split).astype(jnp.float32) + values[step]
            total = total.astype(jnp.bfloat16)
        outs.append(total[:count])
        others.append(swap(total[count:], YBIT))
    low = jnp.concatenate(outs + others, axis=1)
    high = jnp.concatenate(others + outs, axis=1)
    return jnp.where(upper == 0, low, high), incoming


def attend(query_part, cache_latents, cache_lens, handed, handed_mark):
    requests = query_part.shape[0]
    cache_scores = (
        jnp.einsum("qhl,qcl->qhc", query_part, cache_latents, preferred_element_type=jnp.float32)
        * score_scale
    )
    hand_scores = (
        jnp.einsum("qhl,rl->qhr", query_part, handed, preferred_element_type=jnp.float32)
        * score_scale
    )
    cache_mask = (
        jnp.arange(cache_latents.shape[1], dtype=jnp.int32)[None, :] < cache_lens[:, None]
    )[:, None, :]
    marks = jnp.arange(1, requests + 1, dtype=jnp.int32).astype(jnp.float32)
    hand_mask = (handed_mark[None, :] == marks[:, None])[:, None, :]
    cache_scores = jnp.where(cache_mask, cache_scores, -jnp.inf)
    hand_scores = jnp.where(hand_mask, hand_scores, -jnp.inf)
    top = jnp.maximum(jnp.max(cache_scores, axis=2), jnp.max(hand_scores, axis=2))[:, :, None]
    cache_expo = jnp.exp(cache_scores - top)
    hand_expo = jnp.exp(hand_scores - top)
    denom = (jnp.sum(cache_expo, axis=2) + jnp.sum(hand_expo, axis=2))[:, :, None]
    cache_prob = (cache_expo / denom).astype(jnp.bfloat16)
    hand_prob = (hand_expo / denom).astype(jnp.bfloat16)
    result = jnp.einsum(
        "qhc,qcv->qhv", cache_prob, cache_latents[:, :, :VDIM], preferred_element_type=jnp.float32
    )
    result = result + jnp.einsum(
        "qhr,rv->qhv", hand_prob, handed[:, :VDIM], preferred_element_type=jnp.float32
    )
    return result.astype(jnp.bfloat16)


def pieces(value):
    parts = []
    for _ in range(3):
        part = lax.reduce_precision(value, 8, 7)
        parts.append(part.astype(jnp.bfloat16))
        value = value - part
    return parts


def hand_over(prompt_latents, owners, requests, picks, gates, split):
    n_ep = lax.axis_size("ep")
    stretch, lat = prompt_latents.shape
    cap = 2 * stretch // n_ep
    places = jnp.arange(stretch, dtype=jnp.int32)
    earlier = (owners[:, None] == owners[None, :]) & (places[None, :] < places[:, None])
    target = owners * cap + jnp.sum(earlier.astype(jnp.int32), axis=1)
    slots = jnp.arange(n_ep * cap, dtype=jnp.int32)
    chosen = slots[:, None] == target[None, :]
    packed = jnp.dot(
        chosen.astype(jnp.bfloat16), prompt_latents, preferred_element_type=jnp.float32
    ).astype(jnp.bfloat16)
    mark = jnp.sum(jnp.where(chosen, requests[None, :] + 1, 0), axis=1).astype(jnp.bfloat16)
    planes = n_ep // split
    experts = jnp.arange(planes, dtype=jnp.int32)
    weights = jnp.sum(
        jnp.where(picks[None] == experts[:, None, None], gates[None], jnp.zeros_like(gates)[None]),
        axis=2,
    )
    lanes = weights.shape[1] // cap
    table = jnp.concatenate(
        [part.reshape(planes, 1, cap, lanes) for part in pieces(weights)], axis=3
    )
    table = jnp.broadcast_to(table, (planes, split, cap, 3 * lanes)).reshape(n_ep, cap, 3 * lanes)
    fill = -(lat + 1 + 3 * lanes) % 128
    outgoing = jnp.concatenate(
        [
            packed.reshape(n_ep, cap, lat),
            mark.reshape(n_ep, cap, 1),
            jnp.zeros((n_ep, cap, fill), jnp.bfloat16),
            table,
        ],
        axis=2,
    )
    return outgoing


def row_weights(incoming, count, planes, split):
    n_ep, cap, width = incoming.shape
    lanes = count // cap
    start = width - 3 * lanes
    here = lax.axis_index("ep")
    found = []
    for place in (here, here ^ YBIT):
        for step in range(planes):
            source = (place - step * split + n_ep) % n_ep
            tile = lax.dynamic_slice(incoming, (source, 0, start), (1, cap, 3 * lanes))
            tile = tile.astype(jnp.float32).reshape(cap, 3, lanes)
            found.append((tile[:, 0] + tile[:, 1] + tile[:, 2]).reshape(count, 1))
    return jnp.concatenate(found, axis=0)


def on_device(
    moe_rows,
    routes,
    route_gates,
    gate_proj,
    up_proj,
    down_proj,
    queries,
    cache_latents,
    cache_lens,
    prompt_latents,
    kv_owner,
    kv_request,
):
    sections, count, width = moe_rows.shape
    top = routes.shape[2]
    split = FF_WIN // gate_proj.shape[1]
    outgoing = hand_over(
        prompt_latents,
        kv_owner[:, 0],
        kv_request,
        routes.reshape(sections * count, top),
        route_gates.reshape(sections * count, top),
        split,
    )
    expert_out, incoming = expert_rows(
        moe_rows.reshape(sections * count, width), outgoing, gate_proj, up_proj, down_proj
    )
    expert_out = expert_out.reshape(moe_rows.shape)
    queries, incoming = together(queries, incoming)
    lat = prompt_latents.shape[1]
    handed = incoming[:, :, :lat].reshape(-1, lat)
    handed_mark = incoming[:, :, lat].reshape(-1).astype(jnp.float32)
    attended = attend(queries, cache_latents, cache_lens, handed, handed_mark)
    return (expert_out, attended)


def solution(mesh):
    placed = (
        P("section", ("groups", "ep"), None),
        P("section", ("groups", "ep"), None),
        P("section", ("groups", "ep"), None),
        P(None, "ep"),
        P(None, "ep"),
        P("ep", None),
        P(("groups", "ep"), None, None),
        P(("groups", "ep"), None, None),
        P(("groups", "ep")),
        P(("groups", "ep"), None),
        P(("groups", "ep"), None),
        P(("groups", "ep")),
    )
    return jax.shard_map(
        on_device,
        mesh=mesh,
        in_specs=placed,
        out_specs=(P("section", ("groups", "ep"), None), P(("groups", "ep"), None, None)),
        check_vma=False,
    )
```

```python
from functools import partial

import jax
import jax.numpy as jnp
from jax import lax
from jax.experimental import pallas as pl
from jax.experimental.pallas import tpu as pltpu
from jax.sharding import PartitionSpec as P

VDIM = 512
FF_WIN = 1024
CORE, XBIT, YBIT = 1, 2, 4
VMEM_BYTES = 16 * 1024 * 1024


score_scale = 0.07216878364870323


def swap(value, bit):
    count = lax.axis_size("ep")
    return lax.ppermute(value, "ep", [(i, i ^ bit) for i in range(count)])


def shift(value, step):
    count = lax.axis_size("ep")
    return lax.ppermute(value, "ep", [(i, (i + step) % count) for i in range(count)])


def together(*values):
    return lax.optimization_barrier(values)


def pair_dot(rows, left, right):
    both = jnp.concatenate([left[...], right[...]], axis=1)
    return jnp.dot(rows, both, preferred_element_type=jnp.float32)


def gated(gate, up):
    return (gate / (1.0 + jnp.exp(-gate)) * up).astype(jnp.bfloat16)


def pack_kernel(chosen, rows, *outs):
    picked = jnp.dot(chosen[...], rows[...], preferred_element_type=jnp.float32)
    picked = picked.astype(jnp.bfloat16)
    slots = outs[0].shape[0]
    for at, out in enumerate(outs):
        out[...] = picked[at * slots : (at + 1) * slots]


def packs(chosen, rows, planes, chunk):
    count, width = rows.shape
    slots = chosen.shape[0] // planes
    return pl.pallas_call(
        pack_kernel,
        grid=(width // chunk,),
        in_specs=[
            pl.BlockSpec(chosen.shape, lambda k: (0, 0)),
            pl.BlockSpec((count, chunk), lambda k: (0, k)),
        ],
        out_specs=[pl.BlockSpec((slots, chunk), lambda k: (0, k))] * planes,
        out_shape=[jax.ShapeDtypeStruct((slots, width), jnp.bfloat16)] * planes,
        compiler_params=pltpu.CompilerParams(vmem_limit_bytes=VMEM_BYTES),
        cost_estimate=pl.CostEstimate(
            flops=2 * chosen.size * width,
            bytes_accessed=2 * width * (count + planes * slots),
            transcendentals=0,
        ),
    )(chosen, rows)


def hidden_kernel(count, lead, *refs):
    units, weights = refs[:count], refs[count : count + 10]
    gate_o, gate_c, gate_x, gate_xc, up_o, up_c, up_xa, up_xca, up_xb, up_xcb = weights
    out, near_gate, far_gate, near_up, far_up = refs[count + 10 :]
    step = pl.program_id(0)

    @pl.when(step == 0)
    def _():
        for total in (near_gate, far_gate, near_up, far_up):
            total[...] = jnp.zeros_like(total)

    rows = jnp.concatenate([unit[...] for unit in units], axis=0)
    near_gate[...] += pair_dot(rows, gate_o, gate_c)
    far_gate[...] += pair_dot(rows, gate_x, gate_xc)
    near_up[...] += pair_dot(rows, up_o, up_c)

    @pl.when(step < lead)
    def _():
        far_up[...] += pair_dot(rows, up_xa, up_xca)

    @pl.when(step >= lead)
    def _():
        far_up[...] += pair_dot(rows, up_xb, up_xcb)

    @pl.when(step == pl.num_programs(0) - 1)
    def _():
        two = near_up.shape[1]
        out[:, :two] = gated(near_gate[...], near_up[...])
        out[:, two:] = gated(far_gate[...], far_up[...])


def hidden_units(units, weights, leads, rests, chunk):
    width = units[0].shape[1]
    wide = weights[0].shape[1]
    lead = leads[0].shape[0] // chunk
    count = sum(unit.shape[0] for unit in units)
    return pl.pallas_call(
        partial(hidden_kernel, len(units), lead),
        grid=(width // chunk,),
        in_specs=[pl.BlockSpec((unit.shape[0], chunk), lambda k: (0, k)) for unit in units]
        + [pl.BlockSpec((chunk, wide), lambda k: (k, 0)) for _ in weights]
        + [pl.BlockSpec((chunk, wide), lambda k: (jnp.minimum(k, lead - 1), 0)) for _ in leads]
        + [pl.BlockSpec((chunk, wide), lambda k: (jnp.maximum(k - lead, 0), 0)) for _ in rests],
        out_specs=pl.BlockSpec((count, 4 * wide), lambda k: (0, 0)),
        out_shape=jax.ShapeDtypeStruct((count, 4 * wide), jnp.bfloat16),
        scratch_shapes=[pltpu.VMEM((count, 2 * wide), jnp.float32)] * 4,
        compiler_params=pltpu.CompilerParams(vmem_limit_bytes=VMEM_BYTES),
        cost_estimate=pl.CostEstimate(
            flops=2 * count * width * wide * 8,
            bytes_accessed=2 * width * (count + wide * 8),
            transcendentals=0,
        ),
    )(*units, *weights, *leads, *rests)


def down_kernel(mine, other, *refs):
    (own, own_c, side, side_c, peer, peer_c), outs = refs[:6], refs[6:]
    deep = own.shape[0]
    table = jnp.concatenate(
        [own[...], own_c[...], side[:deep, :], side_c[:deep, :]]
        + [peer[...], peer_c[...], side[deep:, :], side_c[deep:, :]],
        axis=0,
    )
    count = mine.shape[0] // 2
    rows = count // len(outs)
    for part in range(2):
        here = slice(part * count, (part + 1) * count)
        there = slice((1 - part) * count, (2 - part) * count)
        joined = jnp.concatenate([mine[here, :], other[there, :]], axis=1)
        value = jnp.dot(joined, table, preferred_element_type=jnp.float32).astype(jnp.bfloat16)
        for at, out in enumerate(outs):
            out[part * rows : (part + 1) * rows, :] = value[at * rows : (at + 1) * rows]


def down_values(mine, other, own, side, peer, planes, chunk, offset):
    count, inner = mine.shape
    width = side[0].shape[1]
    rows = count // planes
    return pl.pallas_call(
        down_kernel,
        grid=(width // chunk,),
        in_specs=[pl.BlockSpec((count, inner), lambda k: (0, 0))] * 2
        + [pl.BlockSpec((block.shape[0], chunk), lambda k: (0, k + offset)) for block in own]
        + [pl.BlockSpec((block.shape[0], chunk), lambda k: (0, k)) for block in side]
        + [pl.BlockSpec((block.shape[0], chunk), lambda k: (0, k + offset)) for block in peer],
        out_specs=[pl.BlockSpec((rows, chunk), lambda k: (0, k))] * planes,
        out_shape=[jax.ShapeDtypeStruct((rows, width), jnp.bfloat16)] * planes,
        compiler_params=pltpu.CompilerParams(vmem_limit_bytes=VMEM_BYTES),
        cost_estimate=pl.CostEstimate(
            flops=2 * count * 2 * inner * width,
            bytes_accessed=2 * 2 * inner * width + 2 * count * width,
            transcendentals=0,
        ),
    )(mine, other, *own, *side, *peer)


def combine_kernel(high, low, *refs):
    parts, (mine, theirs) = refs[:-2], refs[-2:]
    values = jnp.concatenate([part[...] for part in parts], axis=0)
    total = jnp.dot(high[...], values, preferred_element_type=jnp.float32)
    total = total + jnp.dot(low[...], values, preferred_element_type=jnp.float32)
    rows = mine.shape[0]
    mine[...] = total[:rows].astype(jnp.bfloat16)
    theirs[...] = total[rows:].astype(jnp.bfloat16)


def combine(high, low, parts, chunk):
    rows, width = parts[0].shape
    count = high.shape[0] // 2
    out = jax.ShapeDtypeStruct((count, width), jnp.bfloat16)
    return pl.pallas_call(
        combine_kernel,
        grid=(width // chunk,),
        in_specs=[pl.BlockSpec(high.shape, lambda k: (0, 0))] * 2
        + [pl.BlockSpec((rows, chunk), lambda k: (0, k)) for _ in parts],
        out_specs=[pl.BlockSpec((count, chunk), lambda k: (0, k))] * 2,
        out_shape=[out, out],
        compiler_params=pltpu.CompilerParams(vmem_limit_bytes=VMEM_BYTES),
        cost_estimate=pl.CostEstimate(
            flops=4 * high.size * width,
            bytes_accessed=2 * width * (len(parts) * rows + 2 * count),
            transcendentals=0,
        ),
    )(high, low, *parts)


def places(picks, planes, split):
    count = picks.shape[0]
    plane = lax.axis_index("ep") // split
    experts = (plane + jnp.arange(planes, dtype=jnp.int32)) % planes
    named = jnp.any(picks[None] == experts[:, None, None], axis=2)
    order = jnp.arange(count, dtype=jnp.int32)
    before = order[:, None] < order[None, :]
    rank = jnp.sum((named[:, :, None] & before[None]).astype(jnp.int32), axis=1)
    return experts, named, rank


def gate_table(picks, gates, planes, split, slots):
    experts, named, rank = places(picks, planes, split)
    weight = jnp.sum(
        jnp.where(picks[None] == experts[:, None, None], gates[None], jnp.zeros_like(gates)[None]),
        axis=2,
    )
    at = jnp.arange(slots, dtype=jnp.int32)
    found = (rank.T[:, :, None] == at[None, None, :]) & named.T[:, :, None]
    return jnp.where(found, weight.T[:, :, None], 0.0)


def expert_rows(rows, picks, gates, latents, owners, requests, gate_proj, up_proj, down_proj):
    n_ep = lax.axis_size("ep")
    split = FF_WIN // gate_proj.shape[1]
    planes = n_ep // split
    count, width = rows.shape
    slots = -(-3 * count * picks.shape[1] // (2 * planes * 16)) * 16
    chunk = width // 4
    cut = 3 * chunk
    upper = lax.axis_index("ep") // YBIT % 2
    span = width // 4

    gate_x = swap(gate_proj, XBIT)
    _, named, rank = places(picks, planes, split)
    at = jnp.arange(slots, dtype=jnp.int32)
    chosen = (rank[:, None, :] == at[None, :, None]) & named[:, None, :]
    chosen = chosen.astype(jnp.bfloat16)

    own_0, out_1, out_2, out_3 = packs(chosen.reshape(planes * slots, count), rows, planes, span)
    own_0, out_1, out_3, latents, owners, requests, down_proj = together(
        own_0, out_1, out_3, latents, owners, requests, down_proj
    )
    own_1, own_3, peer_0 = shift(out_1, split), shift(out_3, 3 * split), swap(own_0, YBIT)
    keep = lax.dynamic_slice_in_dim(down_proj, 2 * upper * span, 2 * span, 1)
    send = lax.dynamic_slice_in_dim(down_proj, (2 - 2 * upper) * span, 2 * span, 1)
    down_y = swap(send, YBIT)
    outgoing = hand_over(latents, owners, requests)
    up_a, up_b = up_proj[:cut], up_proj[cut:]

    own_1, own_3, peer_0, down_y, gate_x, up_a, out_2, gate_proj, up_proj = together(
        own_1, own_3, peer_0, down_y, gate_x, up_a, out_2, gate_proj, up_proj
    )
    outgoing, keep, picks, gates, own_1 = together(outgoing, keep, picks, gates, own_1)
    own_2, peer_1, peer_3 = shift(out_2, 2 * split), swap(own_1, YBIT), swap(own_3, YBIT)
    up_xa, gate_xc = swap(up_a, XBIT), swap(gate_x, CORE)
    gate_c, up_c = swap(gate_proj, CORE), swap(up_proj, CORE)

    own_2, peer_1, peer_3, up_xa, gate_xc, gate_c, up_c, up_b = together(
        own_2, peer_1, peer_3, up_xa, gate_xc, gate_c, up_c, up_b
    )
    keep, down_y, picks, gates, outgoing, own_2 = together(
        keep, down_y, picks, gates, outgoing, own_2
    )
    peer_2, up_xb, up_xca = swap(own_2, YBIT), swap(up_b, XBIT), swap(up_xa, CORE)
    keep_c, down_yc = swap(keep, CORE), swap(down_y, CORE)
    incoming = lax.all_to_all(outgoing, "ep", split_axis=0, concat_axis=0, tiled=True)
    info = swap(jnp.concatenate([picks.astype(jnp.float32), gates], axis=1), YBIT)
    sides = [
        jnp.concatenate([part[:, at * span : (at + 1) * span] for part in (keep, down_y)], axis=0)
        for at in range(2)
    ]
    up_xb, sides[0] = together(up_xb, sides[0])
    up_xcb, side_0 = swap(up_xb, CORE), swap(sides[0], XBIT)

    units = (own_0, own_1, own_2, own_3, peer_0, peer_1, peer_2, peer_3)
    weights = (gate_proj, gate_c, gate_x, gate_xc, up_proj, up_c)
    hidden = hidden_units(units, weights, (up_xa, up_xca), (up_xb, up_xcb), chunk)
    other = swap(hidden, YBIT)
    side_0, sides[1] = together(side_0, sides[1])
    side_1 = swap(sides[1], XBIT)
    side = ((side_0, swap(side_0, CORE)), (side_1, swap(side_1, CORE)))

    top = picks.shape[1]
    tables = [
        gate_table(picks, gates, planes, split, slots),
        gate_table(info[:, :top].astype(jnp.int32), info[:, top:], planes, split, slots),
    ]
    tables = [
        jnp.pad(tables[0], ((0, 0), (0, 0), (0, slots))),
        jnp.pad(tables[1], ((0, 0), (0, 0), (slots, 0))),
    ]
    table = jnp.concatenate(tables, axis=0).reshape(2 * count, planes * 2 * slots)
    high = lax.reduce_precision(table, 8, 7)
    high, low = high.astype(jnp.bfloat16), (table - high).astype(jnp.bfloat16)

    outs, others = [], []
    for at in range(2):
        values = down_values(
            hidden, other, (keep, keep_c), side[at], (down_y, down_yc), planes, span // 2, 2 * at
        )
        back = [values[0]] + [shift(values[k], n_ep - k * split) for k in range(1, planes)]
        mine, theirs = combine(high, low, back, span // 2)
        outs.append(mine)
        others.append(swap(theirs, YBIT))
    low_first = jnp.concatenate(outs + others, axis=1)
    high_first = jnp.concatenate(others + outs, axis=1)
    return jnp.where(upper == 0, low_first, high_first), incoming, other


def attend(query_part, cache_latents, cache_lens, handed, handed_mark):
    requests = query_part.shape[0]
    cache_scores = (
        jnp.einsum("qhl,qcl->qhc", query_part, cache_latents, preferred_element_type=jnp.float32)
        * score_scale
    )
    hand_scores = (
        jnp.einsum("qhl,rl->qhr", query_part, handed, preferred_element_type=jnp.float32)
        * score_scale
    )
    cache_mask = (
        jnp.arange(cache_latents.shape[1], dtype=jnp.int32)[None, :] < cache_lens[:, None]
    )[:, None, :]
    marks = jnp.arange(1, requests + 1, dtype=jnp.int32).astype(jnp.float32)
    hand_mask = (handed_mark[None, :] == marks[:, None])[:, None, :]
    cache_scores = jnp.where(cache_mask, cache_scores, -jnp.inf)
    hand_scores = jnp.where(hand_mask, hand_scores, -jnp.inf)
    top = jnp.maximum(jnp.max(cache_scores, axis=2), jnp.max(hand_scores, axis=2))[:, :, None]
    cache_expo = jnp.exp(cache_scores - top)
    hand_expo = jnp.exp(hand_scores - top)
    denom = (jnp.sum(cache_expo, axis=2) + jnp.sum(hand_expo, axis=2))[:, :, None]
    cache_prob = (cache_expo / denom).astype(jnp.bfloat16)
    hand_prob = (hand_expo / denom).astype(jnp.bfloat16)
    result = jnp.einsum(
        "qhc,qcv->qhv", cache_prob, cache_latents[:, :, :VDIM], preferred_element_type=jnp.float32
    )
    result = result + jnp.einsum(
        "qhr,rv->qhv", hand_prob, handed[:, :VDIM], preferred_element_type=jnp.float32
    )
    return result.astype(jnp.bfloat16)


def hand_over(prompt_latents, owners, requests):
    n_ep = lax.axis_size("ep")
    stretch, lat = prompt_latents.shape
    cap = 2 * stretch // n_ep
    places_at = jnp.arange(stretch, dtype=jnp.int32)
    earlier = (owners[:, None] == owners[None, :]) & (places_at[None, :] < places_at[:, None])
    target = owners * cap + jnp.sum(earlier.astype(jnp.int32), axis=1)
    slots = jnp.arange(n_ep * cap, dtype=jnp.int32)
    chosen = slots[:, None] == target[None, :]
    packed = jnp.dot(
        chosen.astype(jnp.bfloat16), prompt_latents, preferred_element_type=jnp.float32
    ).astype(jnp.bfloat16)
    mark = jnp.sum(jnp.where(chosen, requests[None, :] + 1, 0), axis=1).astype(jnp.bfloat16)
    fill = -(lat + 1) % 128
    outgoing = jnp.concatenate(
        [packed, mark[:, None], jnp.zeros((n_ep * cap, fill), jnp.bfloat16)], axis=1
    )
    return outgoing.reshape(n_ep, cap, lat + 1 + fill)


def on_device(
    moe_rows,
    routes,
    route_gates,
    gate_proj,
    up_proj,
    down_proj,
    queries,
    cache_latents,
    cache_lens,
    prompt_latents,
    kv_owner,
    kv_request,
):
    sections, count, width = moe_rows.shape
    top = routes.shape[2]
    expert_out, incoming, other = expert_rows(
        moe_rows.reshape(sections * count, width),
        routes.reshape(sections * count, top),
        route_gates.reshape(sections * count, top),
        prompt_latents,
        kv_owner[:, 0],
        kv_request,
        gate_proj,
        up_proj,
        down_proj,
    )
    expert_out = expert_out.reshape(moe_rows.shape)
    queries, incoming, _ = together(queries, incoming, other)
    lat = prompt_latents.shape[1]
    handed = incoming[:, :, :lat].reshape(-1, lat)
    handed_mark = incoming[:, :, lat].reshape(-1).astype(jnp.float32)
    attended = attend(queries, cache_latents, cache_lens, handed, handed_mark)
    return (expert_out, attended)


def solution(mesh):
    placed = (
        P("section", ("groups", "ep"), None),
        P("section", ("groups", "ep"), None),
        P("section", ("groups", "ep"), None),
        P(None, "ep"),
        P(None, "ep"),
        P("ep", None),
        P(("groups", "ep"), None, None),
        P(("groups", "ep"), None, None),
        P(("groups", "ep")),
        P(("groups", "ep"), None),
        P(("groups", "ep"), None),
        P(("groups", "ep")),
    )
    return jax.shard_map(
        on_device,
        mesh=mesh,
        in_specs=placed,
        out_specs=(P("section", ("groups", "ep"), None), P(("groups", "ep"), None, None)),
        check_vma=False,
    )
```

```python
from functools import partial

import jax
import jax.numpy as jnp
from jax import lax
from jax.experimental import pallas as pl
from jax.experimental.pallas import tpu as pltpu
from jax.sharding import PartitionSpec as P

VDIM = 512
FF_WIN = 1024
CORE, XBIT, YBIT = 1, 2, 4
VMEM_BYTES = 16 * 1024 * 1024


score_scale = 0.07216878364870323


def swap(value, bit):
    count = lax.axis_size("ep")
    return lax.ppermute(value, "ep", [(i, i ^ bit) for i in range(count)])


def shift(value, step):
    count = lax.axis_size("ep")
    return lax.ppermute(value, "ep", [(i, (i + step) % count) for i in range(count)])


def together(*values):
    return lax.optimization_barrier(values)


def pair_dot(rows, left, right):
    both = jnp.concatenate([left[...], right[...]], axis=1)
    return jnp.dot(rows, both, preferred_element_type=jnp.float32)


def gated(gate, up):
    return (gate / (1.0 + jnp.exp(-gate)) * up).astype(jnp.bfloat16)


def pack_kernel(chosen, rows, *outs):
    picked = jnp.dot(chosen[...], rows[...], preferred_element_type=jnp.float32)
    picked = picked.astype(jnp.bfloat16)
    slots = outs[0].shape[0]
    for at, out in enumerate(outs):
        out[...] = picked[at * slots : (at + 1) * slots]


def packs(chosen, rows, planes, chunk):
    count, width = rows.shape
    slots = chosen.shape[0] // planes
    return pl.pallas_call(
        pack_kernel,
        grid=(width // chunk,),
        in_specs=[
            pl.BlockSpec(chosen.shape, lambda k: (0, 0)),
            pl.BlockSpec((count, chunk), lambda k: (0, k)),
        ],
        out_specs=[pl.BlockSpec((slots, chunk), lambda k: (0, k))] * planes,
        out_shape=[jax.ShapeDtypeStruct((slots, width), jnp.bfloat16)] * planes,
        compiler_params=pltpu.CompilerParams(vmem_limit_bytes=VMEM_BYTES),
        cost_estimate=pl.CostEstimate(
            flops=2 * chosen.size * width,
            bytes_accessed=2 * width * (count + planes * slots),
            transcendentals=0,
        ),
    )(chosen, rows)


def hidden_kernel(count, lead, *refs):
    units, weights = refs[:count], refs[count : count + 10]
    gate_o, up_o, gate_x, gate_c, up_c, gate_xc, up_xa, up_xca, up_xb, up_xcb = weights
    out, near_gate, far_gate, near_up, far_up = refs[count + 10 :]
    step = pl.program_id(0)

    @pl.when(step == 0)
    def _():
        for total in (near_gate, far_gate, near_up, far_up):
            total[...] = jnp.zeros_like(total)

    rows = jnp.concatenate([unit[...] for unit in units], axis=0)
    near_gate[...] += pair_dot(rows, gate_o, gate_c)
    far_gate[...] += pair_dot(rows, gate_x, gate_xc)
    near_up[...] += pair_dot(rows, up_o, up_c)

    @pl.when(step < lead)
    def _():
        far_up[...] += pair_dot(rows, up_xa, up_xca)

    @pl.when(step >= lead)
    def _():
        far_up[...] += pair_dot(rows, up_xb, up_xcb)

    @pl.when(step == pl.num_programs(0) - 1)
    def _():
        two = near_up.shape[1]
        out[:, :two] = gated(near_gate[...], near_up[...])
        out[:, two:] = gated(far_gate[...], far_up[...])


def hidden_units(units, weights, leads, rests, chunk):
    width = units[0].shape[1]
    wide = weights[0].shape[1]
    lead = leads[0].shape[0] // chunk
    count = sum(unit.shape[0] for unit in units)
    return pl.pallas_call(
        partial(hidden_kernel, len(units), lead),
        grid=(width // chunk,),
        in_specs=[pl.BlockSpec((unit.shape[0], chunk), lambda k: (0, k)) for unit in units]
        + [pl.BlockSpec((chunk, wide), lambda k: (k, 0)) for _ in weights]
        + [pl.BlockSpec((chunk, wide), lambda k: (jnp.minimum(k, lead - 1), 0)) for _ in leads]
        + [pl.BlockSpec((chunk, wide), lambda k: (jnp.maximum(k - lead, 0), 0)) for _ in rests],
        out_specs=pl.BlockSpec((count, 4 * wide), lambda k: (0, 0)),
        out_shape=jax.ShapeDtypeStruct((count, 4 * wide), jnp.bfloat16),
        scratch_shapes=[pltpu.VMEM((count, 2 * wide), jnp.float32)] * 4,
        compiler_params=pltpu.CompilerParams(vmem_limit_bytes=VMEM_BYTES),
        cost_estimate=pl.CostEstimate(
            flops=2 * count * width * wide * 8,
            bytes_accessed=2 * width * (count + wide * 8),
            transcendentals=0,
        ),
    )(*units, *weights, *leads, *rests)


def down_kernel(mine, other, *refs):
    (own, own_c, side, side_c, peer, peer_c), outs = refs[:6], refs[6:]
    deep = own.shape[0]
    table = jnp.concatenate(
        [own[...], own_c[...], side[:deep, :], side_c[:deep, :]]
        + [peer[...], peer_c[...], side[deep:, :], side_c[deep:, :]],
        axis=0,
    )
    count = mine.shape[0] // 2
    rows = count // len(outs)
    for part in range(2):
        here = slice(part * count, (part + 1) * count)
        there = slice((1 - part) * count, (2 - part) * count)
        joined = jnp.concatenate([mine[here, :], other[there, :]], axis=1)
        value = jnp.dot(joined, table, preferred_element_type=jnp.float32).astype(jnp.bfloat16)
        for at, out in enumerate(outs):
            out[part * rows : (part + 1) * rows, :] = value[at * rows : (at + 1) * rows]


def down_values(mine, other, own, side, peer, planes, chunk, offset):
    count, inner = mine.shape
    width = side[0].shape[1]
    rows = count // planes
    return pl.pallas_call(
        down_kernel,
        grid=(width // chunk,),
        in_specs=[pl.BlockSpec((count, inner), lambda k: (0, 0))] * 2
        + [pl.BlockSpec((block.shape[0], chunk), lambda k: (0, k + offset)) for block in own]
        + [pl.BlockSpec((block.shape[0], chunk), lambda k: (0, k)) for block in side]
        + [pl.BlockSpec((block.shape[0], chunk), lambda k: (0, k + offset)) for block in peer],
        out_specs=[pl.BlockSpec((rows, chunk), lambda k: (0, k))] * planes,
        out_shape=[jax.ShapeDtypeStruct((rows, width), jnp.bfloat16)] * planes,
        compiler_params=pltpu.CompilerParams(vmem_limit_bytes=VMEM_BYTES),
        cost_estimate=pl.CostEstimate(
            flops=2 * count * 2 * inner * width,
            bytes_accessed=2 * 2 * inner * width + 2 * count * width,
            transcendentals=0,
        ),
    )(mine, other, *own, *side, *peer)


def combine_kernel(high, low, *refs):
    parts, (mine, theirs) = refs[:-2], refs[-2:]
    values = jnp.concatenate([part[...] for part in parts], axis=0)
    total = jnp.dot(high[...], values, preferred_element_type=jnp.float32)
    total = total + jnp.dot(low[...], values, preferred_element_type=jnp.float32)
    rows = mine.shape[0]
    mine[...] = total[:rows].astype(jnp.bfloat16)
    theirs[...] = total[rows:].astype(jnp.bfloat16)


def combine(high, low, parts, chunk):
    rows, width = parts[0].shape
    count = high.shape[0] // 2
    out = jax.ShapeDtypeStruct((count, width), jnp.bfloat16)
    return pl.pallas_call(
        combine_kernel,
        grid=(width // chunk,),
        in_specs=[pl.BlockSpec(high.shape, lambda k: (0, 0))] * 2
        + [pl.BlockSpec((rows, chunk), lambda k: (0, k)) for _ in parts],
        out_specs=[pl.BlockSpec((count, chunk), lambda k: (0, k))] * 2,
        out_shape=[out, out],
        compiler_params=pltpu.CompilerParams(vmem_limit_bytes=VMEM_BYTES),
        cost_estimate=pl.CostEstimate(
            flops=4 * high.size * width,
            bytes_accessed=2 * width * (len(parts) * rows + 2 * count),
            transcendentals=0,
        ),
    )(high, low, *parts)


def places(picks, planes, split):
    count = picks.shape[0]
    plane = lax.axis_index("ep") // split
    experts = (plane + jnp.arange(planes, dtype=jnp.int32)) % planes
    named = jnp.any(picks[None] == experts[:, None, None], axis=2)
    order = jnp.arange(count, dtype=jnp.int32)
    before = order[:, None] < order[None, :]
    rank = jnp.sum((named[:, :, None] & before[None]).astype(jnp.int32), axis=1)
    return experts, named, rank


def gate_table(picks, gates, planes, split, slots):
    experts, named, rank = places(picks, planes, split)
    weight = jnp.sum(
        jnp.where(picks[None] == experts[:, None, None], gates[None], jnp.zeros_like(gates)[None]),
        axis=2,
    )
    at = jnp.arange(slots, dtype=jnp.int32)
    found = (rank.T[:, :, None] == at[None, None, :]) & named.T[:, :, None]
    return jnp.where(found, weight.T[:, :, None], 0.0)


def expert_rows(
    rows, picks, gates, latents, owners, requests, queries, gate_proj, up_proj, down_proj
):
    n_ep = lax.axis_size("ep")
    split = FF_WIN // gate_proj.shape[1]
    planes = n_ep // split
    count, width = rows.shape
    slots = -(-3 * count * picks.shape[1] // (2 * planes * 16)) * 16
    chunk = width // 4
    cut = 3 * chunk
    upper = lax.axis_index("ep") // YBIT % 2
    span = width // 4

    gate_x = swap(gate_proj, XBIT)
    _, named, rank = places(picks, planes, split)
    at = jnp.arange(slots, dtype=jnp.int32)
    chosen = (rank[:, None, :] == at[None, :, None]) & named[:, None, :]
    chosen = chosen.astype(jnp.bfloat16)

    own_0, out_1, out_2, out_3 = packs(chosen.reshape(planes * slots, count), rows, planes, span)
    own_0, out_1, out_3, latents, owners, requests, down_proj = together(
        own_0, out_1, out_3, latents, owners, requests, down_proj
    )
    own_1, own_3, peer_0 = shift(out_1, split), shift(out_3, 3 * split), swap(own_0, YBIT)
    send = lax.dynamic_slice_in_dim(down_proj, (2 - 2 * upper) * span, 2 * span, 1)
    down_y = swap(send, YBIT)
    outgoing = hand_over(latents, owners, requests)
    up_a, up_b = up_proj[:cut], up_proj[cut:]

    own_1, own_3, peer_0, down_y, gate_x, up_a, out_2, outgoing, down_proj, gate_proj = together(
        own_1, own_3, peer_0, down_y, gate_x, up_a, out_2, outgoing, down_proj, gate_proj
    )
    own_2, peer_1, peer_3 = shift(out_2, 2 * split), swap(own_1, YBIT), swap(own_3, YBIT)
    up_xa = swap(up_a, XBIT)
    gate_c = swap(gate_proj, CORE)
    incoming = lax.all_to_all(outgoing, "ep", split_axis=0, concat_axis=0, tiled=True)
    keep = lax.dynamic_slice_in_dim(down_proj, 2 * upper * span, 2 * span, 1)
    sides = [
        jnp.concatenate([part[:, at * span : (at + 1) * span] for part in (keep, down_y)], axis=0)
        for at in range(2)
    ]
    head = -(-slots // 32) * 16

    own_2, peer_1, peer_3, up_xa, gate_c, up_b, sides[0], up_proj = together(
        own_2, peer_1, peer_3, up_xa, gate_c, up_b, sides[0], up_proj
    )
    peer_2a, up_xb = swap(own_2[:head], YBIT), swap(up_b, XBIT)
    up_c, gate_xc, up_xca = swap(up_proj, CORE), swap(gate_x, CORE), swap(up_xa, CORE)
    away = own_2[head:]
    peer_2a, up_xb, up_c, gate_xc, up_xca, away, sides[0] = together(
        peer_2a, up_xb, up_c, gate_xc, up_xca, away, sides[0]
    )
    peer_2b, up_xcb, side_0 = swap(away, YBIT), swap(up_xb, CORE), swap(sides[0], XBIT)

    units = (own_0, own_1, own_2, own_3, peer_0, peer_1, peer_2a, peer_2b, peer_3)
    hidden = hidden_units(
        units,
        (gate_proj, up_proj, gate_x, gate_c, up_c, gate_xc),
        (up_xa, up_xca),
        (up_xb, up_xcb),
        chunk,
    )
    hidden, side_0, keep, down_y, picks, gates = together(
        hidden, side_0, keep, down_y, picks, gates
    )
    other, keep_c, down_yc = swap(hidden, YBIT), swap(keep, CORE), swap(down_y, CORE)
    info = swap(jnp.concatenate([picks.astype(jnp.float32), gates], axis=1), YBIT)

    own, peer = (keep, keep_c), (down_y, down_yc)
    values = down_values(
        hidden, other, own, (side_0, swap(side_0, CORE)), peer, planes, span // 2, 0
    )
    sides[1], *values = together(sides[1], *values)
    side_1 = swap(sides[1], XBIT)
    side_1, info, picks, gates = together(side_1, info, picks, gates)
    values_1 = down_values(
        hidden, other, own, (side_1, swap(side_1, CORE)), peer, planes, span // 2, 2
    )

    top = picks.shape[1]
    tables = [
        gate_table(picks, gates, planes, split, slots),
        gate_table(info[:, :top].astype(jnp.int32), info[:, top:], planes, split, slots),
    ]
    tables = [
        jnp.pad(tables[0], ((0, 0), (0, 0), (0, slots))),
        jnp.pad(tables[1], ((0, 0), (0, 0), (slots, 0))),
    ]
    table = jnp.concatenate(tables, axis=0).reshape(2 * count, planes * 2 * slots)
    high = lax.reduce_precision(table, 8, 7)
    high, low = high.astype(jnp.bfloat16), (table - high).astype(jnp.bfloat16)

    def returned(part):
        return [part[0]] + [shift(part[k], n_ep - k * split) for k in range(1, planes)]

    backs = [returned(values), returned(values_1)]
    backs[1][0], incoming, queries, *backs[0] = together(
        backs[1][0], incoming, queries, *backs[0]
    )
    outs, others = [], []
    for back in backs:
        mine, theirs = combine(high, low, back, span // 2)
        outs.append(mine)
        others.append(swap(theirs, YBIT))
    low_first = jnp.concatenate(outs + others, axis=1)
    high_first = jnp.concatenate(others + outs, axis=1)
    return jnp.where(upper == 0, low_first, high_first), incoming, queries


def attend(query_part, cache_latents, cache_lens, handed, handed_mark):
    requests = query_part.shape[0]
    cache_scores = (
        jnp.einsum("qhl,qcl->qhc", query_part, cache_latents, preferred_element_type=jnp.float32)
        * score_scale
    )
    hand_scores = (
        jnp.einsum("qhl,rl->qhr", query_part, handed, preferred_element_type=jnp.float32)
        * score_scale
    )
    cache_mask = (
        jnp.arange(cache_latents.shape[1], dtype=jnp.int32)[None, :] < cache_lens[:, None]
    )[:, None, :]
    marks = jnp.arange(1, requests + 1, dtype=jnp.int32).astype(jnp.float32)
    hand_mask = (handed_mark[None, :] == marks[:, None])[:, None, :]
    cache_scores = jnp.where(cache_mask, cache_scores, -jnp.inf)
    hand_scores = jnp.where(hand_mask, hand_scores, -jnp.inf)
    top = jnp.maximum(jnp.max(cache_scores, axis=2), jnp.max(hand_scores, axis=2))[:, :, None]
    cache_expo = jnp.exp(cache_scores - top)
    hand_expo = jnp.exp(hand_scores - top)
    denom = (jnp.sum(cache_expo, axis=2) + jnp.sum(hand_expo, axis=2))[:, :, None]
    cache_prob = (cache_expo / denom).astype(jnp.bfloat16)
    hand_prob = (hand_expo / denom).astype(jnp.bfloat16)
    result = jnp.einsum(
        "qhc,qcv->qhv", cache_prob, cache_latents[:, :, :VDIM], preferred_element_type=jnp.float32
    )
    result = result + jnp.einsum(
        "qhr,rv->qhv", hand_prob, handed[:, :VDIM], preferred_element_type=jnp.float32
    )
    return result.astype(jnp.bfloat16)


def hand_over(prompt_latents, owners, requests):
    n_ep = lax.axis_size("ep")
    stretch, lat = prompt_latents.shape
    cap = 2 * stretch // n_ep
    places_at = jnp.arange(stretch, dtype=jnp.int32)
    earlier = (owners[:, None] == owners[None, :]) & (places_at[None, :] < places_at[:, None])
    target = owners * cap + jnp.sum(earlier.astype(jnp.int32), axis=1)
    slots = jnp.arange(n_ep * cap, dtype=jnp.int32)
    chosen = slots[:, None] == target[None, :]
    packed = jnp.dot(
        chosen.astype(jnp.bfloat16), prompt_latents, preferred_element_type=jnp.float32
    ).astype(jnp.bfloat16)
    mark = jnp.sum(jnp.where(chosen, requests[None, :] + 1, 0), axis=1).astype(jnp.bfloat16)
    fill = -(lat + 1) % 128
    outgoing = jnp.concatenate(
        [packed, mark[:, None], jnp.zeros((n_ep * cap, fill), jnp.bfloat16)], axis=1
    )
    return outgoing.reshape(n_ep, cap, lat + 1 + fill)


def on_device(
    moe_rows,
    routes,
    route_gates,
    gate_proj,
    up_proj,
    down_proj,
    queries,
    cache_latents,
    cache_lens,
    prompt_latents,
    kv_owner,
    kv_request,
):
    sections, count, width = moe_rows.shape
    top = routes.shape[2]
    expert_out, incoming, queries = expert_rows(
        moe_rows.reshape(sections * count, width),
        routes.reshape(sections * count, top),
        route_gates.reshape(sections * count, top),
        prompt_latents,
        kv_owner[:, 0],
        kv_request,
        queries,
        gate_proj,
        up_proj,
        down_proj,
    )
    expert_out = expert_out.reshape(moe_rows.shape)
    lat = prompt_latents.shape[1]
    handed = incoming[:, :, :lat].reshape(-1, lat)
    handed_mark = incoming[:, :, lat].reshape(-1).astype(jnp.float32)
    attended = attend(queries, cache_latents, cache_lens, handed, handed_mark)
    return (expert_out, attended)


def solution(mesh):
    placed = (
        P("section", ("groups", "ep"), None),
        P("section", ("groups", "ep"), None),
        P("section", ("groups", "ep"), None),
        P(None, "ep"),
        P(None, "ep"),
        P("ep", None),
        P(("groups", "ep"), None, None),
        P(("groups", "ep"), None, None),
        P(("groups", "ep")),
        P(("groups", "ep"), None),
        P(("groups", "ep"), None),
        P(("groups", "ep")),
    )
    return jax.shard_map(
        on_device,
        mesh=mesh,
        in_specs=placed,
        out_specs=(P("section", ("groups", "ep"), None), P(("groups", "ep"), None, None)),
        check_vma=False,
    )
```

```python
from functools import partial

import jax
import jax.numpy as jnp
from jax import lax
from jax.experimental import pallas as pl
from jax.experimental.pallas import tpu as pltpu
from jax.sharding import PartitionSpec as P

VDIM = 512
FF_WIN = 1024
SLOT_ROWS = 8
CORE, XBIT, YBIT = 1, 2, 4
VMEM_BYTES = 14 * 1024 * 1024


score_scale = 0.07216878364870323


def swap(value, bit):
    count = lax.axis_size("ep")
    return lax.ppermute(value, "ep", [(i, i ^ bit) for i in range(count)])


def shift(value, step):
    count = lax.axis_size("ep")
    return lax.ppermute(value, "ep", [(i, (i + step) % count) for i in range(count)])


def together(*values):
    return lax.optimization_barrier(values)


def pair_dot(rows, left, right):
    both = jnp.concatenate([left[...], right[...]], axis=1)
    return jnp.dot(rows, both, preferred_element_type=jnp.float32)


def gated(gate, up):
    return (gate / (1.0 + jnp.exp(-gate)) * up).astype(jnp.bfloat16)


def tag_kernel(experts, rows, picks, gates, out):
    width = rows.shape[1]
    count = rows.shape[0]
    lane = lax.broadcasted_iota(jnp.int32, (count, 128), 1)
    weight = jnp.zeros((count, 128), jnp.float32)
    for at in range(picks.shape[1]):
        hit = picks[:, at : at + 1] == lane % experts
        weight = weight + jnp.where(hit, gates[:, at : at + 1], 0.0)
    high = weight.astype(jnp.bfloat16).astype(jnp.float32)
    middle = (weight - high).astype(jnp.bfloat16).astype(jnp.float32)
    low = weight - high - middle
    part = lane // experts
    tag = jnp.where(part == 0, high, jnp.where(part == 1, middle, low))
    tag = jnp.where(part < 3, tag, 0.0)
    out[:, :width] = rows[...]
    out[:, width:] = tag.astype(jnp.bfloat16)


def tagged(rows, picks, gates, experts):
    count, width = rows.shape
    return pl.pallas_call(
        partial(tag_kernel, experts),
        out_shape=jax.ShapeDtypeStruct((count, width + 128), jnp.bfloat16),
        compiler_params=pltpu.CompilerParams(vmem_limit_bytes=VMEM_BYTES),
        cost_estimate=pl.CostEstimate(
            flops=0, bytes_accessed=4 * count * width, transcendentals=0
        ),
    )(rows, picks, gates)


def hidden_kernel(count, lead, *refs):
    units, weights = refs[:count], refs[count : count + 10]
    gate_o, gate_c, gate_x, gate_xc, up_o, up_c, up_xa, up_xca, up_xb, up_xcb = weights
    out, near_gate, far_gate, near_up, far_up = refs[count + 10 :]
    step = pl.program_id(0)

    @pl.when(step == 0)
    def _():
        for total in (near_gate, far_gate, near_up, far_up):
            total[...] = jnp.zeros_like(total)

    rows = jnp.concatenate([unit[...] for unit in units], axis=0)
    near_gate[...] += pair_dot(rows, gate_o, gate_c)
    near_up[...] += pair_dot(rows, up_o, up_c)
    far_gate[...] += pair_dot(rows, gate_x, gate_xc)

    @pl.when(step < lead)
    def _():
        far_up[...] += pair_dot(rows, up_xa, up_xca)

    @pl.when(step >= lead)
    def _():
        far_up[...] += pair_dot(rows, up_xb, up_xcb)

    @pl.when(step == pl.num_programs(0) - 1)
    def _():
        two = near_up.shape[1]
        out[:, :two] = gated(near_gate[...], near_up[...])
        out[:, two:] = gated(far_gate[...], far_up[...])


def hidden_units(units, weights, leads, rests, chunk):
    width, wide = weights[0].shape
    lead = leads[0].shape[0] // chunk
    count = sum(unit.shape[0] for unit in units)
    return pl.pallas_call(
        partial(hidden_kernel, len(units), lead),
        grid=(width // chunk,),
        in_specs=[pl.BlockSpec((unit.shape[0], chunk), lambda k: (0, k)) for unit in units]
        + [pl.BlockSpec((chunk, wide), lambda k: (k, 0)) for _ in weights]
        + [pl.BlockSpec((chunk, wide), lambda k: (jnp.minimum(k, lead - 1), 0)) for _ in leads]
        + [pl.BlockSpec((chunk, wide), lambda k: (jnp.maximum(k - lead, 0), 0)) for _ in rests],
        out_specs=pl.BlockSpec((count, 4 * wide), lambda k: (0, 0)),
        out_shape=jax.ShapeDtypeStruct((count, 4 * wide), jnp.bfloat16),
        scratch_shapes=[pltpu.VMEM((count, 2 * wide), jnp.float32)] * 4,
        compiler_params=pltpu.CompilerParams(vmem_limit_bytes=VMEM_BYTES),
        cost_estimate=pl.CostEstimate(
            flops=2 * count * width * wide * 8,
            bytes_accessed=2 * width * (count + wide * 8),
            transcendentals=0,
        ),
    )(*units, *weights, *leads, *rests)


def down_kernel(pairs, tags, *refs):
    chosen, metas, (own, own_c, side, side_c), outs = (
        refs[0],
        refs[1 : 1 + tags],
        refs[1 + tags + 2 * pairs : 5 + tags + 2 * pairs],
        refs[5 + tags + 2 * pairs :],
    )
    hiddens = refs[1 + tags : 1 + tags + 2 * pairs]
    deep = own.shape[0] // 2
    parts = (own, own_c, side, side_c)
    table = jnp.concatenate(
        [part[:deep, :] for part in parts] + [part[deep:, :] for part in parts], axis=0
    )
    meta = jnp.concatenate([part[...] for part in metas], axis=0).astype(jnp.float32)
    weight = jnp.sum(meta * chosen[...], axis=1, keepdims=True)
    rows = outs[0].shape[0] // 2
    first = 0
    for pair in range(pairs):
        mine, other = hiddens[2 * pair], hiddens[2 * pair + 1]
        half = mine.shape[0] // 2
        joined = jnp.concatenate(
            [
                jnp.concatenate([mine[:half, :], other[half:, :]], axis=1),
                jnp.concatenate([mine[half:, :], other[:half, :]], axis=1),
            ],
            axis=0,
        )
        value = jnp.dot(joined, table, preferred_element_type=jnp.float32)
        base = 2 * first * rows
        value = value * weight[base : base + 2 * half]
        units = half // rows
        for at in range(units):
            out = outs[first + at]
            out[:rows, :] = value[at * rows : (at + 1) * rows].astype(out.dtype)
            out[rows:, :] = value[half + at * rows : half + (at + 1) * rows].astype(out.dtype)
        first += units


def down_values(chosen, metas, hiddens, tables, kinds, chunk):
    rows = max(meta.shape[0] for meta in metas)
    width = tables[0].shape[1]
    at_tag = metas[0].shape[1] // 128 - 1
    count = rows * 2 * len(kinds)
    return pl.pallas_call(
        partial(down_kernel, len(hiddens) // 2, len(metas)),
        grid=(width // chunk,),
        in_specs=[pl.BlockSpec(chosen.shape, lambda k: (0, 0))]
        + [pl.BlockSpec((meta.shape[0], 128), lambda k: (0, at_tag)) for meta in metas]
        + [pl.BlockSpec(hidden.shape, lambda k: (0, 0)) for hidden in hiddens]
        + [pl.BlockSpec((table.shape[0], chunk), lambda k: (0, k)) for table in tables],
        out_specs=[pl.BlockSpec((2 * rows, chunk), lambda k: (0, k)) for _ in kinds],
        out_shape=[jax.ShapeDtypeStruct((2 * rows, width), kind) for kind in kinds],
        compiler_params=pltpu.CompilerParams(vmem_limit_bytes=VMEM_BYTES),
        cost_estimate=pl.CostEstimate(
            flops=2 * count * 4 * tables[0].shape[0] * width,
            bytes_accessed=8 * tables[0].shape[0] * width + 4 * count * width,
            transcendentals=0,
        ),
    )(chosen, *metas, *hiddens, *tables)


def expert_rows(
    rows, picks, gates, latents, owners, requests, queries, gate_proj, up_proj, down_proj
):
    n_ep = lax.axis_size("ep")
    split = FF_WIN // gate_proj.shape[1]
    planes = n_ep // split
    count, width = rows.shape
    here = lax.axis_index("ep")
    upper = here // YBIT % 2
    span = width // 4
    half = count // 2

    chunk = width // 7
    cut = 2 * chunk
    gate_x, up_xa = swap(gate_proj, XBIT), swap(up_proj[:cut], XBIT)
    rows = tagged(rows, picks, gates, planes)
    keep = lax.dynamic_slice_in_dim(down_proj, 2 * upper * span, 2 * span, 1)
    send = lax.dynamic_slice_in_dim(down_proj, (2 - 2 * upper) * span, 2 * span, 1)
    unit_1, peer_0 = shift(rows, split), swap(rows, YBIT)
    down_y0 = swap(send[:, :span], YBIT)
    outgoing = hand_over(latents, owners, requests)
    unit_1, peer_0, down_y0, gate_proj, outgoing = together(
        unit_1, peer_0, down_y0, gate_proj, outgoing
    )
    unit_2, peer_1 = shift(unit_1, split), swap(unit_1, YBIT)
    gate_c = swap(gate_proj, CORE)
    own_0 = jnp.concatenate([keep[:, :span], down_y0], axis=0)
    up_b = up_proj[cut:]
    unit_2, peer_1, gate_c, gate_x, up_xa, up_proj, up_b, own_0, send = together(
        unit_2, peer_1, gate_c, gate_x, up_xa, up_proj, up_b, own_0, send
    )
    unit_3, peer_2 = shift(unit_2, split), swap(unit_2, YBIT)
    up_xb, up_c, gate_xc = swap(up_b, XBIT), swap(up_proj, CORE), swap(gate_x, CORE)
    incoming = lax.all_to_all(outgoing, "ep", split_axis=0, concat_axis=0, tiled=True)
    unit_3, peer_2, up_xb, up_c, gate_xc, up_xa, own_0 = together(
        unit_3, peer_2, up_xb, up_c, gate_xc, up_xa, own_0
    )
    up_xca, up_xcb, side_0 = swap(up_xa, CORE), swap(up_xb, CORE), swap(own_0, XBIT)
    last = (shift(peer_2[:half], split), swap(unit_3[half:], YBIT))
    up_xca, up_xcb, *last = together(up_xca, up_xcb, *last)

    weights = (gate_proj, gate_c, gate_x, gate_xc, up_proj, up_c)
    parts = ((up_xa, up_xca), (up_xb, up_xcb))
    hidden_1 = hidden_units((unit_1, peer_1), weights, *parts, chunk)
    hidden_1, send = together(hidden_1, send)
    other_1, down_y1, side_0 = together(
        swap(hidden_1, YBIT), swap(send[:, span:], YBIT), side_0
    )
    own_0c = swap(own_0, CORE)
    hidden_2 = hidden_units(
        (unit_2, unit_3, rows, peer_2, *last, peer_0), weights, *parts, chunk
    )
    other_2 = swap(hidden_2, YBIT)
    own_1 = jnp.concatenate([keep[:, span:], down_y1], axis=0)

    lane = jnp.arange(128, dtype=jnp.int32)
    chosen = ((lane % planes == here // split) & (lane < 3 * planes)).astype(jnp.float32)[None, :]
    metas_1 = (unit_1, peer_1)
    metas_2 = (unit_2, unit_3, rows, peer_2, *last, peer_0)
    wide, thin = jnp.float32, jnp.bfloat16
    tables = (own_0, own_0c, side_0, swap(side_0, CORE))
    value_1 = down_values(chosen, metas_1, (hidden_1, other_1), tables, (thin,), span // 2)
    values_2 = down_values(
        chosen, metas_2, (hidden_2, other_2), tables, (wide,) * 3, span // 2
    )
    side_0, own_1 = together(side_0, own_1)
    side_1, own_1c = swap(own_1, XBIT), swap(own_1, CORE)
    tables = (own_1, own_1c, side_1, swap(side_1, CORE))
    values = down_values(
        chosen,
        metas_1 + metas_2,
        (hidden_1, other_1, hidden_2, other_2),
        tables,
        (thin, wide, wide, wide),
        span // 2,
    )
    outs, others = [], []
    for at, parts in enumerate(((*value_1, *values_2), values)):
        total = parts[0]
        for step in range(1, planes):
            total = (shift(total, split).astype(jnp.float32) + parts[step]).astype(jnp.bfloat16)
            if at == 0 and step == 1:
                total, incoming, queries = together(total, incoming, queries)
        outs.append(total[:count])
        others.append(swap(total[count:], YBIT))
    low_first = jnp.concatenate(outs + others, axis=1)
    high_first = jnp.concatenate(others + outs, axis=1)
    return jnp.where(upper == 0, low_first, high_first), incoming, queries


def attend(query_part, cache_latents, cache_lens, handed, handed_mark):
    requests = query_part.shape[0]
    cache_scores = (
        jnp.einsum("qhl,qcl->qhc", query_part, cache_latents, preferred_element_type=jnp.float32)
        * score_scale
    )
    hand_scores = (
        jnp.einsum("qhl,rl->qhr", query_part, handed, preferred_element_type=jnp.float32)
        * score_scale
    )
    cache_mask = (
        jnp.arange(cache_latents.shape[1], dtype=jnp.int32)[None, :] < cache_lens[:, None]
    )[:, None, :]
    marks = jnp.arange(1, requests + 1, dtype=jnp.int32).astype(jnp.float32)
    hand_mask = (handed_mark[None, :] == marks[:, None])[:, None, :]
    cache_scores = jnp.where(cache_mask, cache_scores, -jnp.inf)
    hand_scores = jnp.where(hand_mask, hand_scores, -jnp.inf)
    top = jnp.maximum(jnp.max(cache_scores, axis=2), jnp.max(hand_scores, axis=2))[:, :, None]
    cache_expo = jnp.exp(cache_scores - top)
    hand_expo = jnp.exp(hand_scores - top)
    denom = (jnp.sum(cache_expo, axis=2) + jnp.sum(hand_expo, axis=2))[:, :, None]
    cache_prob = (cache_expo / denom).astype(jnp.bfloat16)
    hand_prob = (hand_expo / denom).astype(jnp.bfloat16)
    result = jnp.einsum(
        "qhc,qcv->qhv", cache_prob, cache_latents[:, :, :VDIM], preferred_element_type=jnp.float32
    )
    result = result + jnp.einsum(
        "qhr,rv->qhv", hand_prob, handed[:, :VDIM], preferred_element_type=jnp.float32
    )
    return result.astype(jnp.bfloat16)


def hand_over(prompt_latents, owners, requests):
    n_ep = lax.axis_size("ep")
    stretch, lat = prompt_latents.shape
    cap = 2 * stretch // n_ep
    places_at = jnp.arange(stretch, dtype=jnp.int32)
    earlier = (owners[:, None] == owners[None, :]) & (places_at[None, :] < places_at[:, None])
    target = owners * cap + jnp.sum(earlier.astype(jnp.int32), axis=1)
    slots = jnp.arange(n_ep * cap, dtype=jnp.int32)
    chosen = slots[:, None] == target[None, :]
    packed = jnp.dot(
        chosen.astype(jnp.bfloat16), prompt_latents, preferred_element_type=jnp.float32
    ).astype(jnp.bfloat16)
    mark = jnp.sum(jnp.where(chosen, requests[None, :] + 1, 0), axis=1).astype(jnp.bfloat16)
    fill = -(lat + 1) % 128
    outgoing = jnp.concatenate(
        [packed, mark[:, None], jnp.zeros((n_ep * cap, fill), jnp.bfloat16)], axis=1
    )
    return outgoing.reshape(n_ep, cap, lat + 1 + fill)


def on_device(
    moe_rows,
    routes,
    route_gates,
    gate_proj,
    up_proj,
    down_proj,
    queries,
    cache_latents,
    cache_lens,
    prompt_latents,
    kv_owner,
    kv_request,
):
    sections, count, width = moe_rows.shape
    top = routes.shape[2]
    expert_out, incoming, queries = expert_rows(
        moe_rows.reshape(sections * count, width),
        routes.reshape(sections * count, top),
        route_gates.reshape(sections * count, top),
        prompt_latents,
        kv_owner[:, 0],
        kv_request,
        queries,
        gate_proj,
        up_proj,
        down_proj,
    )
    expert_out = expert_out.reshape(moe_rows.shape)
    lat = prompt_latents.shape[1]
    handed = incoming[:, :, :lat].reshape(-1, lat)
    handed_mark = incoming[:, :, lat].reshape(-1).astype(jnp.float32)
    attended = attend(queries, cache_latents, cache_lens, handed, handed_mark)
    return (expert_out, attended)


def solution(mesh):
    placed = (
        P("section", ("groups", "ep"), None),
        P("section", ("groups", "ep"), None),
        P("section", ("groups", "ep"), None),
        P(None, "ep"),
        P(None, "ep"),
        P("ep", None),
        P(("groups", "ep"), None, None),
        P(("groups", "ep"), None, None),
        P(("groups", "ep")),
        P(("groups", "ep"), None),
        P(("groups", "ep"), None),
        P(("groups", "ep")),
    )
    return jax.shard_map(
        on_device,
        mesh=mesh,
        in_specs=placed,
        out_specs=(P("section", ("groups", "ep"), None), P(("groups", "ep"), None, None)),
        check_vma=False,
    )
```

```python
from functools import partial

import jax
import jax.numpy as jnp
from jax import lax
from jax.experimental import pallas as pl
from jax.experimental.pallas import tpu as pltpu
from jax.sharding import PartitionSpec as P

VDIM = 512
FF_WIN = 1024
CORE, XBIT, YBIT = 1, 2, 4
VMEM_BYTES = 60 * 1024 * 1024


score_scale = 0.07216878364870323


def swap(value, bit):
    count = lax.axis_size("ep")
    return lax.ppermute(value, "ep", [(i, i ^ bit) for i in range(count)])


def shift(value, step):
    count = lax.axis_size("ep")
    return lax.ppermute(value, "ep", [(i, (i + step) % count) for i in range(count)])


def together(*values):
    return lax.optimization_barrier(values)


def pair_dot(rows, left, right):
    both = jnp.concatenate([left[...], right[...]], axis=1)
    return jnp.dot(rows, both, preferred_element_type=jnp.float32)


def gated(gate, up):
    return (gate / (1.0 + jnp.exp(-gate)) * up).astype(jnp.bfloat16)


def pack_kernel(chosen, rows, *outs):
    picked = jnp.dot(chosen[...], rows[...], preferred_element_type=jnp.float32)
    picked = picked.astype(jnp.bfloat16)
    slots = outs[0].shape[0]
    for at, out in enumerate(outs):
        out[...] = picked[at * slots : (at + 1) * slots]


def packs(chosen, rows, planes, chunk):
    count, width = rows.shape
    slots = chosen.shape[0] // planes
    return pl.pallas_call(
        pack_kernel,
        grid=(width // chunk,),
        in_specs=[
            pl.BlockSpec(chosen.shape, lambda k: (0, 0)),
            pl.BlockSpec((count, chunk), lambda k: (0, k)),
        ],
        out_specs=[pl.BlockSpec((slots, chunk), lambda k: (0, k))] * planes,
        out_shape=[jax.ShapeDtypeStruct((slots, width), jnp.bfloat16)] * planes,
        compiler_params=pltpu.CompilerParams(vmem_limit_bytes=VMEM_BYTES),
        cost_estimate=pl.CostEstimate(
            flops=2 * chosen.size * width,
            bytes_accessed=2 * width * (count + planes * slots),
            transcendentals=0,
        ),
    )(chosen, rows)


def hidden_kernel(count, *refs):
    units, weights = refs[:count], refs[count : count + 8]
    gate_o, gate_c, gate_x, gate_xc, up_o, up_c, up_x, up_xc = weights
    out, near_gate, far_gate, near_up, far_up = refs[count + 8 :]
    step = pl.program_id(0)

    @pl.when(step == 0)
    def _():
        for total in (near_gate, far_gate, near_up, far_up):
            total[...] = jnp.zeros_like(total)

    rows = jnp.concatenate([unit[...] for unit in units], axis=0)
    near_gate[...] += pair_dot(rows, gate_o, gate_c)
    near_up[...] += pair_dot(rows, up_o, up_c)
    far_gate[...] += pair_dot(rows, gate_x, gate_xc)
    far_up[...] += pair_dot(rows, up_x, up_xc)

    @pl.when(step == pl.num_programs(0) - 1)
    def _():
        two = near_up.shape[1]
        out[:, :two] = gated(near_gate[...], near_up[...])
        out[:, two:] = gated(far_gate[...], far_up[...])


def hidden_units(units, weights, chunk):
    width, wide = weights[0].shape
    count = sum(unit.shape[0] for unit in units)
    return pl.pallas_call(
        partial(hidden_kernel, len(units)),
        grid=(width // chunk,),
        in_specs=[pl.BlockSpec((unit.shape[0], chunk), lambda k: (0, k)) for unit in units]
        + [pl.BlockSpec((chunk, wide), lambda k: (k, 0)) for _ in weights],
        out_specs=pl.BlockSpec((count, 4 * wide), lambda k: (0, 0)),
        out_shape=jax.ShapeDtypeStruct((count, 4 * wide), jnp.bfloat16),
        scratch_shapes=[pltpu.VMEM((count, 2 * wide), jnp.float32)] * 4,
        compiler_params=pltpu.CompilerParams(vmem_limit_bytes=VMEM_BYTES),
        cost_estimate=pl.CostEstimate(
            flops=2 * count * width * wide * 8,
            bytes_accessed=2 * width * (count + wide * 8),
            transcendentals=0,
        ),
    )(*units, *weights)


def down_kernel(planes, mine, other, own, own_c, side, side_c, *outs):
    deep = own.shape[0] // 2
    parts = (own, own_c, side, side_c)
    table = jnp.concatenate(
        [part[:deep, :] for part in parts] + [part[deep:, :] for part in parts], axis=0
    )
    count = mine.shape[0] // 2
    rows = count // planes
    joined = jnp.concatenate(
        [
            jnp.concatenate([mine[:count, :], other[count:, :]], axis=1),
            jnp.concatenate([mine[count:, :], other[:count, :]], axis=1),
        ],
        axis=0,
    )
    value = jnp.dot(joined, table, preferred_element_type=jnp.float32).astype(jnp.bfloat16)

    def put(targets):
        for at, out in enumerate(targets):
            out[:rows, :] = value[at * rows : (at + 1) * rows]
            out[rows:, :] = value[count + at * rows : count + (at + 1) * rows]

    first = pl.program_id(0) < pl.num_programs(0) // 2

    @pl.when(first)
    def _():
        put(outs[:planes])

    @pl.when(jnp.logical_not(first))
    def _():
        put(outs[planes:])


def down_values(mine, other, tables, planes, chunk):
    count, inner = mine.shape
    deep, width = tables[0].shape
    rows = count // planes
    steps = width // chunk
    half = steps // 2
    return pl.pallas_call(
        partial(down_kernel, planes),
        grid=(steps,),
        in_specs=[pl.BlockSpec((count, inner), lambda k: (0, 0))] * 2
        + [pl.BlockSpec((deep, chunk), lambda k: (0, k)) for _ in tables],
        out_specs=[pl.BlockSpec((rows, chunk), lambda k: (0, jnp.minimum(k, half - 1)))] * planes
        + [pl.BlockSpec((rows, chunk), lambda k: (0, jnp.maximum(k - half, 0)))] * planes,
        out_shape=[jax.ShapeDtypeStruct((rows, width // 2), jnp.bfloat16)] * (2 * planes),
        compiler_params=pltpu.CompilerParams(vmem_limit_bytes=VMEM_BYTES),
        cost_estimate=pl.CostEstimate(
            flops=2 * count * 2 * inner * width,
            bytes_accessed=8 * deep * width + 2 * count * width,
            transcendentals=0,
        ),
    )(mine, other, *tables)


def combine_kernel(high, low, *refs):
    parts, (mine, theirs) = refs[:-2], refs[-2:]
    values = jnp.concatenate([part[...] for part in parts], axis=0)
    total = jnp.dot(high[...], values, preferred_element_type=jnp.float32)
    total = total + jnp.dot(low[...], values, preferred_element_type=jnp.float32)
    rows = mine.shape[0]
    mine[...] = total[:rows].astype(jnp.bfloat16)
    theirs[...] = total[rows:].astype(jnp.bfloat16)


def combine(high, low, parts, chunk):
    rows, width = parts[0].shape
    count = high.shape[0] // 2
    out = jax.ShapeDtypeStruct((count, width), jnp.bfloat16)
    return pl.pallas_call(
        combine_kernel,
        grid=(width // chunk,),
        in_specs=[pl.BlockSpec(high.shape, lambda k: (0, 0))] * 2
        + [pl.BlockSpec((rows, chunk), lambda k: (0, k)) for _ in parts],
        out_specs=[pl.BlockSpec((count, chunk), lambda k: (0, k))] * 2,
        out_shape=[out, out],
        compiler_params=pltpu.CompilerParams(vmem_limit_bytes=VMEM_BYTES),
        cost_estimate=pl.CostEstimate(
            flops=4 * high.size * width,
            bytes_accessed=2 * width * (len(parts) * rows + 2 * count),
            transcendentals=0,
        ),
    )(high, low, *parts)


def places(picks, planes, split):
    count = picks.shape[0]
    plane = lax.axis_index("ep") // split
    experts = (plane + jnp.arange(planes, dtype=jnp.int32)) % planes
    named = jnp.any(picks[None] == experts[:, None, None], axis=2)
    order = jnp.arange(count, dtype=jnp.int32)
    before = order[:, None] < order[None, :]
    rank = jnp.sum((named[:, :, None] & before[None]).astype(jnp.int32), axis=1)
    return experts, named, rank


def gate_table(picks, gates, planes, split, slots):
    experts, named, rank = places(picks, planes, split)
    weight = jnp.sum(
        jnp.where(picks[None] == experts[:, None, None], gates[None], jnp.zeros_like(gates)[None]),
        axis=2,
    )
    at = jnp.arange(slots, dtype=jnp.int32)
    found = (rank.T[:, :, None] == at[None, None, :]) & named.T[:, :, None]
    return jnp.where(found, weight.T[:, :, None], 0.0)


def expert_rows(
    rows, picks, gates, latents, owners, requests, queries, gate_proj, up_proj, down_proj
):
    n_ep = lax.axis_size("ep")
    split = FF_WIN // gate_proj.shape[1]
    planes = n_ep // split
    count, width = rows.shape
    slots = -(-3 * count * picks.shape[1] // (2 * planes * 16)) * 16
    chunk = width // 4
    upper = lax.axis_index("ep") // YBIT % 2
    span = width // 4

    gate_x = swap(gate_proj, XBIT)
    _, named, rank = places(picks, planes, split)
    at = jnp.arange(slots, dtype=jnp.int32)
    chosen = (rank[:, None, :] == at[None, :, None]) & named[:, None, :]
    chosen = chosen.astype(jnp.bfloat16)

    own_0, out_1, out_2, out_3 = packs(chosen.reshape(planes * slots, count), rows, planes, span)
    own_0, out_1, out_3, latents, owners, requests, down_proj = together(
        own_0, out_1, out_3, latents, owners, requests, down_proj
    )
    own_1, own_3, peer_0 = shift(out_1, split), shift(out_3, 3 * split), swap(own_0, YBIT)
    send = lax.dynamic_slice_in_dim(down_proj, (2 - 2 * upper) * span, 2 * span, 1)
    down_y = swap(send, YBIT)
    outgoing = hand_over(latents, owners, requests)

    own_1, own_3, peer_0, down_y, gate_x, out_2, outgoing, down_proj, gate_proj = together(
        own_1, own_3, peer_0, down_y, gate_x, out_2, outgoing, down_proj, gate_proj
    )
    own_2, peer_1, peer_3 = shift(out_2, 2 * split), swap(own_1, YBIT), swap(own_3, YBIT)
    up_x, gate_c = swap(up_proj, XBIT), swap(gate_proj, CORE)
    incoming = lax.all_to_all(outgoing, "ep", split_axis=0, concat_axis=0, tiled=True)
    keep = lax.dynamic_slice_in_dim(down_proj, 2 * upper * span, 2 * span, 1)
    own = jnp.concatenate([keep, down_y], axis=0)

    own_2, peer_1, peer_3, up_x, gate_x, gate_c, up_proj, own, incoming = together(
        own_2, peer_1, peer_3, up_x, gate_x, gate_c, up_proj, own, incoming
    )
    peer_2, side = swap(own_2, YBIT), swap(own, XBIT)
    up_c, gate_xc, up_xc = swap(up_proj, CORE), swap(gate_x, CORE), swap(up_x, CORE)

    peer_2, up_c, gate_xc, up_xc = together(peer_2, up_c, gate_xc, up_xc)
    units = (own_0, own_1, own_2, own_3, peer_0, peer_1, peer_2, peer_3)
    weights = (gate_proj, gate_c, gate_x, gate_xc, up_proj, up_c, up_x, up_xc)
    hidden = hidden_units(units, weights, chunk)
    hidden, own, picks, gates = together(hidden, own, picks, gates)
    other, own_c = swap(hidden, YBIT), swap(own, CORE)
    other, own_c, side = together(other, own_c, side)
    side_c = swap(side, CORE)
    info = swap(jnp.concatenate([picks.astype(jnp.float32), gates], axis=1), YBIT)
    values = down_values(hidden, other, (own, own_c, side, side_c), planes, span // 2)

    def returned(part):
        return [part[0]] + [shift(part[k], n_ep - k * split) for k in range(1, planes)]

    first = returned(values[:planes])
    first[1], info, picks, gates, *values = together(
        first[1], info, picks, gates, *values[planes:]
    )
    second = returned(values)
    backs = (together(*first), together(*second))

    top = picks.shape[1]
    tables = [
        gate_table(picks, gates, planes, split, slots),
        gate_table(info[:, :top].astype(jnp.int32), info[:, top:], planes, split, slots),
    ]
    tables = [
        jnp.pad(tables[0], ((0, 0), (0, 0), (0, slots))),
        jnp.pad(tables[1], ((0, 0), (0, 0), (slots, 0))),
    ]
    table = jnp.concatenate(tables, axis=0).reshape(2 * count, planes * 2 * slots)
    high = lax.reduce_precision(table, 8, 7)
    high, low = high.astype(jnp.bfloat16), (table - high).astype(jnp.bfloat16)

    outs, others = [], []
    for back in backs:
        mine, theirs = combine(high, low, back, span // 2)
        if not outs:
            mine, theirs, incoming, queries = together(mine, theirs, incoming, queries)
        outs.append(mine)
        others.append(swap(theirs, YBIT))
    low_first = jnp.concatenate(outs + others, axis=1)
    high_first = jnp.concatenate(others + outs, axis=1)
    return jnp.where(upper == 0, low_first, high_first), incoming, queries


def attend(query_part, cache_latents, cache_lens, handed, handed_mark):
    requests = query_part.shape[0]
    cache_scores = (
        jnp.einsum("qhl,qcl->qhc", query_part, cache_latents, preferred_element_type=jnp.float32)
        * score_scale
    )
    hand_scores = (
        jnp.einsum("qhl,rl->qhr", query_part, handed, preferred_element_type=jnp.float32)
        * score_scale
    )
    cache_mask = (
        jnp.arange(cache_latents.shape[1], dtype=jnp.int32)[None, :] < cache_lens[:, None]
    )[:, None, :]
    marks = jnp.arange(1, requests + 1, dtype=jnp.int32).astype(jnp.float32)
    hand_mask = (handed_mark[None, :] == marks[:, None])[:, None, :]
    cache_scores = jnp.where(cache_mask, cache_scores, -jnp.inf)
    hand_scores = jnp.where(hand_mask, hand_scores, -jnp.inf)
    top = jnp.maximum(jnp.max(cache_scores, axis=2), jnp.max(hand_scores, axis=2))[:, :, None]
    cache_expo = jnp.exp(cache_scores - top)
    hand_expo = jnp.exp(hand_scores - top)
    denom = (jnp.sum(cache_expo, axis=2) + jnp.sum(hand_expo, axis=2))[:, :, None]
    cache_prob = (cache_expo / denom).astype(jnp.bfloat16)
    hand_prob = (hand_expo / denom).astype(jnp.bfloat16)
    result = jnp.einsum(
        "qhc,qcv->qhv", cache_prob, cache_latents[:, :, :VDIM], preferred_element_type=jnp.float32
    )
    result = result + jnp.einsum(
        "qhr,rv->qhv", hand_prob, handed[:, :VDIM], preferred_element_type=jnp.float32
    )
    return result.astype(jnp.bfloat16)


def hand_over(prompt_latents, owners, requests):
    n_ep = lax.axis_size("ep")
    stretch, lat = prompt_latents.shape
    cap = 2 * stretch // n_ep
    places_at = jnp.arange(stretch, dtype=jnp.int32)
    earlier = (owners[:, None] == owners[None, :]) & (places_at[None, :] < places_at[:, None])
    target = owners * cap + jnp.sum(earlier.astype(jnp.int32), axis=1)
    slots = jnp.arange(n_ep * cap, dtype=jnp.int32)
    chosen = slots[:, None] == target[None, :]
    packed = jnp.dot(
        chosen.astype(jnp.bfloat16), prompt_latents, preferred_element_type=jnp.float32
    ).astype(jnp.bfloat16)
    mark = jnp.sum(jnp.where(chosen, requests[None, :] + 1, 0), axis=1).astype(jnp.bfloat16)
    fill = -(lat + 1) % 128
    outgoing = jnp.concatenate(
        [packed, mark[:, None], jnp.zeros((n_ep * cap, fill), jnp.bfloat16)], axis=1
    )
    return outgoing.reshape(n_ep, cap, lat + 1 + fill)


def on_device(
    moe_rows,
    routes,
    route_gates,
    gate_proj,
    up_proj,
    down_proj,
    queries,
    cache_latents,
    cache_lens,
    prompt_latents,
    kv_owner,
    kv_request,
):
    sections, count, width = moe_rows.shape
    top = routes.shape[2]
    expert_out, incoming, queries = expert_rows(
        moe_rows.reshape(sections * count, width),
        routes.reshape(sections * count, top),
        route_gates.reshape(sections * count, top),
        prompt_latents,
        kv_owner[:, 0],
        kv_request,
        queries,
        gate_proj,
        up_proj,
        down_proj,
    )
    expert_out = expert_out.reshape(moe_rows.shape)
    lat = prompt_latents.shape[1]
    handed = incoming[:, :, :lat].reshape(-1, lat)
    handed_mark = incoming[:, :, lat].reshape(-1).astype(jnp.float32)
    attended = attend(queries, cache_latents, cache_lens, handed, handed_mark)
    return (expert_out, attended)


def solution(mesh):
    placed = (
        P("section", ("groups", "ep"), None),
        P("section", ("groups", "ep"), None),
        P("section", ("groups", "ep"), None),
        P(None, "ep"),
        P(None, "ep"),
        P("ep", None),
        P(("groups", "ep"), None, None),
        P(("groups", "ep"), None, None),
        P(("groups", "ep")),
        P(("groups", "ep"), None),
        P(("groups", "ep"), None),
        P(("groups", "ep")),
    )
    return jax.shard_map(
        on_device,
        mesh=mesh,
        in_specs=placed,
        out_specs=(P("section", ("groups", "ep"), None), P(("groups", "ep"), None, None)),
        check_vma=False,
    )
```

```python
from functools import partial

import jax
import jax.numpy as jnp
from jax import lax
from jax.experimental import pallas as pl
from jax.experimental.pallas import tpu as pltpu
from jax.sharding import PartitionSpec as P

VDIM = 512
FF_WIN = 1024
SLOT_ROWS = 8
CORE, XBIT, YBIT = 1, 2, 4
VMEM_BYTES = 60 * 1024 * 1024


score_scale = 0.07216878364870323


def swap(value, bit):
    count = lax.axis_size("ep")
    return lax.ppermute(value, "ep", [(i, i ^ bit) for i in range(count)])


def shift(value, step):
    count = lax.axis_size("ep")
    return lax.ppermute(value, "ep", [(i, (i + step) % count) for i in range(count)])


def together(*values):
    return lax.optimization_barrier(values)


def pair_dot(rows, left, right):
    both = jnp.concatenate([left[...], right[...]], axis=1)
    return jnp.dot(rows, both, preferred_element_type=jnp.float32)


def gated(gate, up):
    return (gate / (1.0 + jnp.exp(-gate)) * up).astype(jnp.bfloat16)


def hidden_kernel(count, lead, *refs):
    units, weights = refs[:count], refs[count : count + 10]
    gate_o, gate_c, gate_x, gate_xc, up_o, up_c, up_xa, up_xca, up_xb, up_xcb = weights
    out, near_gate, far_gate, near_up, far_up = refs[count + 10 :]
    step = pl.program_id(0)

    @pl.when(step == 0)
    def _():
        for total in (near_gate, far_gate, near_up, far_up):
            total[...] = jnp.zeros_like(total)

    rows = jnp.concatenate([unit[...] for unit in units], axis=0)
    near_gate[...] += pair_dot(rows, gate_o, gate_c)
    near_up[...] += pair_dot(rows, up_o, up_c)
    far_gate[...] += pair_dot(rows, gate_x, gate_xc)

    @pl.when(step < lead)
    def _():
        far_up[...] += pair_dot(rows, up_xa, up_xca)

    @pl.when(step >= lead)
    def _():
        far_up[...] += pair_dot(rows, up_xb, up_xcb)

    @pl.when(step == pl.num_programs(0) - 1)
    def _():
        two = near_up.shape[1]
        out[:, :two] = gated(near_gate[...], near_up[...])
        out[:, two:] = gated(far_gate[...], far_up[...])


def hidden_units(units, weights, leads, rests, chunk):
    width, wide = weights[0].shape
    lead = leads[0].shape[0] // chunk
    count = sum(unit.shape[0] for unit in units)
    return pl.pallas_call(
        partial(hidden_kernel, len(units), lead),
        grid=(width // chunk,),
        in_specs=[pl.BlockSpec((unit.shape[0], chunk), lambda k: (0, k)) for unit in units]
        + [pl.BlockSpec((chunk, wide), lambda k: (k, 0)) for _ in weights]
        + [pl.BlockSpec((chunk, wide), lambda k: (jnp.minimum(k, lead - 1), 0)) for _ in leads]
        + [pl.BlockSpec((chunk, wide), lambda k: (jnp.maximum(k - lead, 0), 0)) for _ in rests],
        out_specs=pl.BlockSpec((count, 4 * wide), lambda k: (0, 0)),
        out_shape=jax.ShapeDtypeStruct((count, 4 * wide), jnp.bfloat16),
        scratch_shapes=[pltpu.VMEM((count, 2 * wide), jnp.float32)] * 4,
        compiler_params=pltpu.CompilerParams(vmem_limit_bytes=VMEM_BYTES),
        cost_estimate=pl.CostEstimate(
            flops=2 * count * width * wide * 8,
            bytes_accessed=2 * width * (count + wide * 8),
            transcendentals=0,
        ),
    )(*units, *weights, *leads, *rests)


def down_kernel(planes, mine, other, weight, *refs):
    blocks, outs = refs[:-planes], refs[-planes:]
    table = jnp.concatenate([block[...] for block in blocks], axis=0)
    count = mine.shape[0] // 2
    rows = count // planes
    joined = jnp.concatenate(
        [
            jnp.concatenate([mine[:count, :], other[count:, :]], axis=1),
            jnp.concatenate([mine[count:, :], other[:count, :]], axis=1),
        ],
        axis=0,
    )
    value = jnp.dot(joined, table, preferred_element_type=jnp.float32) * weight[...]
    for at, out in enumerate(outs):
        out[:rows, :] = value[at * rows : (at + 1) * rows].astype(out.dtype)
        out[rows:, :] = value[count + at * rows : count + (at + 1) * rows].astype(out.dtype)


def down_values(mine, other, weight, blocks, planes, chunk, offset):
    count, inner = mine.shape
    width = min(block.shape[1] for block in blocks)
    depth = blocks[0].shape[0]
    rows = count // planes
    kinds = [jnp.float32] * (planes - 1) + [jnp.bfloat16]
    return pl.pallas_call(
        partial(down_kernel, planes),
        grid=(width // chunk,),
        in_specs=[pl.BlockSpec((count, inner), lambda k: (0, 0))] * 2
        + [pl.BlockSpec((count, 1), lambda k: (0, 0))]
        + [
            pl.BlockSpec((depth, chunk), lambda k: (0, k))
            if block.shape[1] == width
            else pl.BlockSpec((depth, chunk), lambda k: (0, k + offset))
            for block in blocks
        ],
        out_specs=[pl.BlockSpec((rows, chunk), lambda k: (0, k)) for _ in kinds],
        out_shape=[jax.ShapeDtypeStruct((rows, width), kind) for kind in kinds],
        compiler_params=pltpu.CompilerParams(vmem_limit_bytes=VMEM_BYTES),
        cost_estimate=pl.CostEstimate(
            flops=2 * count * 2 * inner * width,
            bytes_accessed=2 * 2 * inner * width + 4 * count * width,
            transcendentals=0,
        ),
    )(mine, other, weight, *blocks)


def expert_rows(rows, outgoing, queries, gate_proj, up_proj, down_proj):
    n_ep = lax.axis_size("ep")
    split = FF_WIN // gate_proj.shape[1]
    planes = n_ep // split
    count, width = rows.shape
    chunk = width // 7

    cut = 2 * chunk
    upper = lax.axis_index("ep") // YBIT % 2
    span = width // 4
    half = count // 2

    gate_x, up_xa = swap(gate_proj, XBIT), swap(up_proj[:cut], XBIT)
    unit_1, peer_0, gate_c = shift(rows, split), swap(rows, YBIT), swap(gate_proj, CORE)
    unit_1, peer_0, gate_c, outgoing, up_proj, down_proj = together(
        unit_1, peer_0, gate_c, outgoing, up_proj, down_proj
    )
    up_b = up_proj[cut:]
    unit_2, peer_1, up_c = shift(unit_1, split), swap(unit_1, YBIT), swap(up_proj, CORE)
    keep = lax.dynamic_slice_in_dim(down_proj, 2 * upper * span, 2 * span, 1)
    unit_2, peer_1, gate_x, up_xa, up_c, up_b, keep, down_proj = together(
        unit_2, peer_1, gate_x, up_xa, up_c, up_b, keep, down_proj
    )
    unit_3, peer_2 = shift(unit_2, split), swap(unit_2, YBIT)
    up_xb, gate_xc = swap(up_b, XBIT), swap(gate_x, CORE)
    send = lax.dynamic_slice_in_dim(down_proj, (2 - 2 * upper) * span, 2 * span, 1)
    send_0, send_1 = send[:, :span], send[:, span:]
    unit_3, peer_2, up_xb, gate_xc, up_xa, keep, send_0, send_1 = together(
        unit_3, peer_2, up_xb, gate_xc, up_xa, keep, send_0, send_1
    )
    up_xca, up_xcb, keep_x = swap(up_xa, CORE), swap(up_xb, CORE), swap(keep, XBIT)
    last = (shift(peer_2[:half], split), swap(unit_3[half:], YBIT))
    up_xca, up_xcb, send_0, send_1, keep, *last = together(
        up_xca, up_xcb, send_0, send_1, keep, *last
    )
    down_y0, down_y1, keep_c = swap(send_0, YBIT), swap(send_1, YBIT), swap(keep, CORE)
    incoming = lax.all_to_all(outgoing, "ep", split_axis=0, concat_axis=0, tiled=True)

    units = (rows, unit_1, unit_2, unit_3, peer_0, peer_1, peer_2, *last)
    weights = (gate_proj, gate_c, gate_x, gate_xc, up_proj, up_c)
    hidden = hidden_units(units, weights, (up_xa, up_xca), (up_xb, up_xcb), chunk)
    hidden, keep_x, keep_c, down_y0, down_y1, incoming = together(
        hidden, keep_x, keep_c, down_y0, down_y1, incoming
    )
    other, down_yx0 = swap(hidden, YBIT), swap(down_y0, XBIT)
    keep_xc, down_yc0 = swap(keep_x, CORE), swap(down_y0, CORE)
    weight = row_weights(incoming, count, planes, split)
    down_yx0, down_y1 = together(down_yx0, down_y1)
    down_yx1, down_yc1 = swap(down_y1, XBIT), swap(down_y1, CORE)
    whole = (keep, keep_c, keep_x, keep_xc)
    parts = (
        (down_y0, down_yc0, down_yx0, swap(down_yx0, CORE)),
        (down_y1, down_yc1, down_yx1, swap(down_yx1, CORE)),
    )

    outs, others = [], []
    for at, part in enumerate(parts):
        values = down_values(hidden, other, weight, whole + part, planes, span // 2, 2 * at)
        total = values[-1]
        for step in range(planes - 2, -1, -1):
            total = shift(total, n_ep - split).astype(jnp.float32) + values[step]
            total = total.astype(jnp.bfloat16)
            if at == 0 and step == planes - 2:
                total, incoming, queries = together(total, incoming, queries)
        outs.append(total[:count])
        others.append(swap(total[count:], YBIT))
    low = jnp.concatenate(outs + others, axis=1)
    high = jnp.concatenate(others + outs, axis=1)
    return jnp.where(upper == 0, low, high), incoming, queries


def attend(query_part, cache_latents, cache_lens, handed, handed_mark):
    requests = query_part.shape[0]
    cache_scores = (
        jnp.einsum("qhl,qcl->qhc", query_part, cache_latents, preferred_element_type=jnp.float32)
        * score_scale
    )
    hand_scores = (
        jnp.einsum("qhl,rl->qhr", query_part, handed, preferred_element_type=jnp.float32)
        * score_scale
    )
    cache_mask = (
        jnp.arange(cache_latents.shape[1], dtype=jnp.int32)[None, :] < cache_lens[:, None]
    )[:, None, :]
    marks = jnp.arange(1, requests + 1, dtype=jnp.int32).astype(jnp.float32)
    hand_mask = (handed_mark[None, :] == marks[:, None])[:, None, :]
    cache_scores = jnp.where(cache_mask, cache_scores, -jnp.inf)
    hand_scores = jnp.where(hand_mask, hand_scores, -jnp.inf)
    top = jnp.maximum(jnp.max(cache_scores, axis=2), jnp.max(hand_scores, axis=2))[:, :, None]
    cache_expo = jnp.exp(cache_scores - top)
    hand_expo = jnp.exp(hand_scores - top)
    denom = (jnp.sum(cache_expo, axis=2) + jnp.sum(hand_expo, axis=2))[:, :, None]
    cache_prob = (cache_expo / denom).astype(jnp.bfloat16)
    hand_prob = (hand_expo / denom).astype(jnp.bfloat16)
    result = jnp.einsum(
        "qhc,qcv->qhv", cache_prob, cache_latents[:, :, :VDIM], preferred_element_type=jnp.float32
    )
    result = result + jnp.einsum(
        "qhr,rv->qhv", hand_prob, handed[:, :VDIM], preferred_element_type=jnp.float32
    )
    return result.astype(jnp.bfloat16)


def pieces(value):
    parts = []
    for _ in range(3):
        part = lax.reduce_precision(value, 8, 7)
        parts.append(part.astype(jnp.bfloat16))
        value = value - part
    return parts


def hand_over(prompt_latents, owners, requests, picks, gates, split):
    n_ep = lax.axis_size("ep")
    stretch, lat = prompt_latents.shape
    cap = 2 * stretch // n_ep
    places = jnp.arange(stretch, dtype=jnp.int32)
    earlier = (owners[:, None] == owners[None, :]) & (places[None, :] < places[:, None])
    target = owners * cap + jnp.sum(earlier.astype(jnp.int32), axis=1)
    slots = jnp.arange(n_ep * cap, dtype=jnp.int32)
    chosen = slots[:, None] == target[None, :]
    packed = jnp.dot(
        chosen.astype(jnp.bfloat16), prompt_latents, preferred_element_type=jnp.float32
    ).astype(jnp.bfloat16)
    mark = jnp.sum(jnp.where(chosen, requests[None, :] + 1, 0), axis=1).astype(jnp.bfloat16)
    planes = n_ep // split
    experts = jnp.arange(planes, dtype=jnp.int32)
    weights = jnp.sum(
        jnp.where(picks[None] == experts[:, None, None], gates[None], jnp.zeros_like(gates)[None]),
        axis=2,
    )
    lanes = weights.shape[1] // cap
    table = jnp.concatenate(
        [part.reshape(planes, 1, cap, lanes) for part in pieces(weights)], axis=3
    )
    table = jnp.broadcast_to(table, (planes, split, cap, 3 * lanes)).reshape(n_ep, cap, 3 * lanes)
    fill = -(lat + 1 + 3 * lanes) % 128
    outgoing = jnp.concatenate(
        [
            packed.reshape(n_ep, cap, lat),
            mark.reshape(n_ep, cap, 1),
            jnp.zeros((n_ep, cap, fill), jnp.bfloat16),
            table,
        ],
        axis=2,
    )
    return outgoing


def row_weights(incoming, count, planes, split):
    n_ep, cap, width = incoming.shape
    lanes = count // cap
    start = width - 3 * lanes
    here = lax.axis_index("ep")
    found = []
    for place in (here, here ^ YBIT):
        for step in range(planes):
            source = (place - step * split + n_ep) % n_ep
            tile = lax.dynamic_slice(incoming, (source, 0, start), (1, cap, 3 * lanes))
            tile = tile.astype(jnp.float32).reshape(cap, 3, lanes)
            found.append((tile[:, 0] + tile[:, 1] + tile[:, 2]).reshape(count, 1))
    return jnp.concatenate(found, axis=0)


def on_device(
    moe_rows,
    routes,
    route_gates,
    gate_proj,
    up_proj,
    down_proj,
    queries,
    cache_latents,
    cache_lens,
    prompt_latents,
    kv_owner,
    kv_request,
):
    sections, count, width = moe_rows.shape
    top = routes.shape[2]
    split = FF_WIN // gate_proj.shape[1]
    outgoing = hand_over(
        prompt_latents,
        kv_owner[:, 0],
        kv_request,
        routes.reshape(sections * count, top),
        route_gates.reshape(sections * count, top),
        split,
    )
    expert_out, incoming, queries = expert_rows(
        moe_rows.reshape(sections * count, width),
        outgoing,
        queries,
        gate_proj,
        up_proj,
        down_proj,
    )
    expert_out = expert_out.reshape(moe_rows.shape)
    lat = prompt_latents.shape[1]
    handed = incoming[:, :, :lat].reshape(-1, lat)
    handed_mark = incoming[:, :, lat].reshape(-1).astype(jnp.float32)
    attended = attend(queries, cache_latents, cache_lens, handed, handed_mark)
    return (expert_out, attended)


def solution(mesh):
    placed = (
        P("section", ("groups", "ep"), None),
        P("section", ("groups", "ep"), None),
        P("section", ("groups", "ep"), None),
        P(None, "ep"),
        P(None, "ep"),
        P("ep", None),
        P(("groups", "ep"), None, None),
        P(("groups", "ep"), None, None),
        P(("groups", "ep")),
        P(("groups", "ep"), None),
        P(("groups", "ep"), None),
        P(("groups", "ep")),
    )
    return jax.shard_map(
        on_device,
        mesh=mesh,
        in_specs=placed,
        out_specs=(P("section", ("groups", "ep"), None), P(("groups", "ep"), None, None)),
        check_vma=False,
    )
```

```python
from functools import partial

import jax
import jax.numpy as jnp
from jax import lax
from jax.experimental import pallas as pl
from jax.experimental.pallas import tpu as pltpu
from jax.sharding import PartitionSpec as P

VDIM = 512
FF_WIN = 1024
CORE, XBIT, YBIT = 1, 2, 4
VMEM_BYTES = 60 * 1024 * 1024


score_scale = 0.07216878364870323


def swap(value, bit):
    count = lax.axis_size("ep")
    return lax.ppermute(value, "ep", [(i, i ^ bit) for i in range(count)])


def shift(value, step):
    count = lax.axis_size("ep")
    return lax.ppermute(value, "ep", [(i, (i + step) % count) for i in range(count)])


def together(*values):
    return lax.optimization_barrier(values)


def pair_dot(rows, left, right):
    both = jnp.concatenate([left[...], right[...]], axis=1)
    return jnp.dot(rows, both, preferred_element_type=jnp.float32)


def gated(gate, up):
    return (gate / (1.0 + jnp.exp(-gate)) * up).astype(jnp.bfloat16)


def pack_kernel(chosen, rows, *outs):
    picked = jnp.dot(chosen[...], rows[...], preferred_element_type=jnp.float32)
    picked = picked.astype(jnp.bfloat16)
    slots = outs[0].shape[0]
    for at, out in enumerate(outs):
        out[...] = picked[at * slots : (at + 1) * slots]


def packs(chosen, rows, planes, chunk):
    count, width = rows.shape
    slots = chosen.shape[0] // planes
    return pl.pallas_call(
        pack_kernel,
        grid=(width // chunk,),
        in_specs=[
            pl.BlockSpec(chosen.shape, lambda k: (0, 0)),
            pl.BlockSpec((count, chunk), lambda k: (0, k)),
        ],
        out_specs=[pl.BlockSpec((slots, chunk), lambda k: (0, k))] * planes,
        out_shape=[jax.ShapeDtypeStruct((slots, width), jnp.bfloat16)] * planes,
        compiler_params=pltpu.CompilerParams(vmem_limit_bytes=VMEM_BYTES),
        cost_estimate=pl.CostEstimate(
            flops=2 * chosen.size * width,
            bytes_accessed=2 * width * (count + planes * slots),
            transcendentals=0,
        ),
    )(chosen, rows)


def hidden_kernel(count, *refs):
    units, weights = refs[:count], refs[count : count + 8]
    gate_o, gate_c, gate_x, gate_xc, up_o, up_c, up_x, up_xc = weights
    out, near_gate, far_gate, near_up, far_up = refs[count + 8 :]
    step = pl.program_id(0)

    @pl.when(step == 0)
    def _():
        for total in (near_gate, far_gate, near_up, far_up):
            total[...] = jnp.zeros_like(total)

    rows = jnp.concatenate([unit[...] for unit in units], axis=0)
    near_gate[...] += pair_dot(rows, gate_o, gate_c)
    near_up[...] += pair_dot(rows, up_o, up_c)
    far_gate[...] += pair_dot(rows, gate_x, gate_xc)
    far_up[...] += pair_dot(rows, up_x, up_xc)

    @pl.when(step == pl.num_programs(0) - 1)
    def _():
        two = near_up.shape[1]
        out[:, :two] = gated(near_gate[...], near_up[...])
        out[:, two:] = gated(far_gate[...], far_up[...])


def hidden_units(units, weights, chunk):
    width, wide = weights[0].shape
    count = sum(unit.shape[0] for unit in units)
    return pl.pallas_call(
        partial(hidden_kernel, len(units)),
        grid=(width // chunk,),
        in_specs=[pl.BlockSpec((unit.shape[0], chunk), lambda k: (0, k)) for unit in units]
        + [pl.BlockSpec((chunk, wide), lambda k: (k, 0)) for _ in weights],
        out_specs=pl.BlockSpec((count, 4 * wide), lambda k: (0, 0)),
        out_shape=jax.ShapeDtypeStruct((count, 4 * wide), jnp.bfloat16),
        scratch_shapes=[pltpu.VMEM((count, 2 * wide), jnp.float32)] * 4,
        compiler_params=pltpu.CompilerParams(vmem_limit_bytes=VMEM_BYTES),
        cost_estimate=pl.CostEstimate(
            flops=2 * count * width * wide * 8,
            bytes_accessed=2 * width * (count + wide * 8),
            transcendentals=0,
        ),
    )(*units, *weights)


def down_kernel(mine, other, own, own_c, side, side_c, *outs):
    deep = own.shape[0] // 2
    parts = (own, own_c, side, side_c)
    table = jnp.concatenate(
        [part[:deep, :] for part in parts] + [part[deep:, :] for part in parts], axis=0
    )
    count = mine.shape[0] // 2
    rows = count // len(outs)
    joined = jnp.concatenate(
        [
            jnp.concatenate([mine[:count, :], other[count:, :]], axis=1),
            jnp.concatenate([mine[count:, :], other[:count, :]], axis=1),
        ],
        axis=0,
    )
    value = jnp.dot(joined, table, preferred_element_type=jnp.float32).astype(jnp.bfloat16)
    for at, out in enumerate(outs):
        out[:rows, :] = value[at * rows : (at + 1) * rows]
        out[rows:, :] = value[count + at * rows : count + (at + 1) * rows]


def down_values(mine, other, own, side, planes, chunk, offset):
    count, inner = mine.shape
    deep, width = side[0].shape
    rows = count // planes
    return pl.pallas_call(
        down_kernel,
        grid=(width // chunk,),
        in_specs=[pl.BlockSpec((count, inner), lambda k: (0, 0))] * 2
        + [pl.BlockSpec((deep, chunk), lambda k: (0, k + offset)) for _ in own]
        + [pl.BlockSpec((deep, chunk), lambda k: (0, k)) for _ in side],
        out_specs=[pl.BlockSpec((rows, chunk), lambda k: (0, k))] * planes,
        out_shape=[jax.ShapeDtypeStruct((rows, width), jnp.bfloat16)] * planes,
        compiler_params=pltpu.CompilerParams(vmem_limit_bytes=VMEM_BYTES),
        cost_estimate=pl.CostEstimate(
            flops=2 * count * 2 * inner * width,
            bytes_accessed=8 * deep * width + 2 * count * width,
            transcendentals=0,
        ),
    )(mine, other, *own, *side)


def combine_kernel(high, low, *refs):
    parts, (mine, theirs) = refs[:-2], refs[-2:]
    values = jnp.concatenate([part[...] for part in parts], axis=0)
    total = jnp.dot(high[...], values, preferred_element_type=jnp.float32)
    total = total + jnp.dot(low[...], values, preferred_element_type=jnp.float32)
    rows = mine.shape[0]
    mine[...] = total[:rows].astype(jnp.bfloat16)
    theirs[...] = total[rows:].astype(jnp.bfloat16)


def combine(high, low, parts, chunk):
    rows, width = parts[0].shape
    count = high.shape[0] // 2
    out = jax.ShapeDtypeStruct((count, width), jnp.bfloat16)
    return pl.pallas_call(
        combine_kernel,
        grid=(width // chunk,),
        in_specs=[pl.BlockSpec(high.shape, lambda k: (0, 0))] * 2
        + [pl.BlockSpec((rows, chunk), lambda k: (0, k)) for _ in parts],
        out_specs=[pl.BlockSpec((count, chunk), lambda k: (0, k))] * 2,
        out_shape=[out, out],
        compiler_params=pltpu.CompilerParams(vmem_limit_bytes=VMEM_BYTES),
        cost_estimate=pl.CostEstimate(
            flops=4 * high.size * width,
            bytes_accessed=2 * width * (len(parts) * rows + 2 * count),
            transcendentals=0,
        ),
    )(high, low, *parts)


def places(picks, planes, split):
    count = picks.shape[0]
    plane = lax.axis_index("ep") // split
    experts = (plane + jnp.arange(planes, dtype=jnp.int32)) % planes
    named = jnp.any(picks[None] == experts[:, None, None], axis=2)
    order = jnp.arange(count, dtype=jnp.int32)
    before = order[:, None] < order[None, :]
    rank = jnp.sum((named[:, :, None] & before[None]).astype(jnp.int32), axis=1)
    return experts, named, rank


def gate_table(picks, gates, planes, split, slots):
    experts, named, rank = places(picks, planes, split)
    weight = jnp.sum(
        jnp.where(picks[None] == experts[:, None, None], gates[None], jnp.zeros_like(gates)[None]),
        axis=2,
    )
    at = jnp.arange(slots, dtype=jnp.int32)
    found = (rank.T[:, :, None] == at[None, None, :]) & named.T[:, :, None]
    return jnp.where(found, weight.T[:, :, None], 0.0)


def expert_rows(
    rows, picks, gates, latents, owners, requests, queries, gate_proj, up_proj, down_proj
):
    n_ep = lax.axis_size("ep")
    split = FF_WIN // gate_proj.shape[1]
    planes = n_ep // split
    count, width = rows.shape
    slots = -(-3 * count * picks.shape[1] // (2 * planes * 16)) * 16
    chunk = width // 4
    upper = lax.axis_index("ep") // YBIT % 2
    span = width // 4

    gate_x = swap(gate_proj, XBIT)
    _, named, rank = places(picks, planes, split)
    at = jnp.arange(slots, dtype=jnp.int32)
    chosen = (rank[:, None, :] == at[None, :, None]) & named[:, None, :]
    chosen = chosen.astype(jnp.bfloat16)

    pack_0, out_1, out_2, out_3 = packs(chosen.reshape(planes * slots, count), rows, planes, span)
    pack_0, out_1, out_3, latents, owners, requests, down_proj = together(
        pack_0, out_1, out_3, latents, owners, requests, down_proj
    )
    own_1, own_3, peer_0 = shift(out_1, split), shift(out_3, 3 * split), swap(pack_0, YBIT)
    send = lax.dynamic_slice_in_dim(down_proj, (2 - 2 * upper) * span, 2 * span, 1)
    down_y = swap(send, YBIT)
    outgoing = hand_over(latents, owners, requests)

    own_1, own_3, peer_0, down_y, gate_x, out_2, outgoing, down_proj, gate_proj = together(
        own_1, own_3, peer_0, down_y, gate_x, out_2, outgoing, down_proj, gate_proj
    )
    own_2, peer_1, peer_3 = shift(out_2, 2 * split), swap(own_1, YBIT), swap(own_3, YBIT)
    up_x, gate_c = swap(up_proj, XBIT), swap(gate_proj, CORE)
    keep = lax.dynamic_slice_in_dim(down_proj, 2 * upper * span, 2 * span, 1)
    own = jnp.concatenate([keep, down_y], axis=0)
    own_0, rest = own[:, :span], own[:, span:]

    own_2, peer_1, peer_3, up_x, gate_x, gate_c, up_proj, own, own_0, rest = together(
        own_2, peer_1, peer_3, up_x, gate_x, gate_c, up_proj, own, own_0, rest
    )
    peer_2, side_0 = swap(own_2, YBIT), swap(own_0, XBIT)
    up_c, gate_xc, up_xc = swap(up_proj, CORE), swap(gate_x, CORE), swap(up_x, CORE)
    incoming = lax.all_to_all(outgoing, "ep", split_axis=0, concat_axis=0, tiled=True)

    peer_2, up_c, gate_xc, up_xc = together(peer_2, up_c, gate_xc, up_xc)
    own_c = swap(own, CORE)
    units = (pack_0, own_1, own_2, own_3, peer_0, peer_1, peer_2, peer_3)
    weights = (gate_proj, gate_c, gate_x, gate_xc, up_proj, up_c, up_x, up_xc)
    hidden = hidden_units(units, weights, chunk)
    hidden, own_c, side_0, rest, picks, gates, incoming = together(
        hidden, own_c, side_0, rest, picks, gates, incoming
    )
    other, side_0c, side_1 = swap(hidden, YBIT), swap(side_0, CORE), swap(rest, XBIT)
    info = swap(jnp.concatenate([picks.astype(jnp.float32), gates], axis=1), YBIT)
    other, side_0c, info, picks, gates = together(other, side_0c, info, picks, gates)
    halves = (
        down_values(hidden, other, (own, own_c), (side_0, side_0c), planes, span // 2, 0),
        down_values(hidden, other, (own, own_c), (side_1, swap(side_1, CORE)), planes, span // 2, 2),
    )

    top = picks.shape[1]
    tables = [
        gate_table(picks, gates, planes, split, slots),
        gate_table(info[:, :top].astype(jnp.int32), info[:, top:], planes, split, slots),
    ]
    tables = [
        jnp.pad(tables[0], ((0, 0), (0, 0), (0, slots))),
        jnp.pad(tables[1], ((0, 0), (0, 0), (slots, 0))),
    ]
    table = jnp.concatenate(tables, axis=0).reshape(2 * count, planes * 2 * slots)
    high = lax.reduce_precision(table, 8, 7)
    high, low = high.astype(jnp.bfloat16), (table - high).astype(jnp.bfloat16)

    backs = [
        [values[0]] + [shift(values[k], n_ep - k * split) for k in range(1, planes)]
        for values in halves
    ]
    backs[1][0], incoming, queries, *backs[0] = together(
        backs[1][0], incoming, queries, *backs[0]
    )
    outs, others = [], []
    for back in backs:
        mine, theirs = combine(high, low, back, span // 2)
        outs.append(mine)
        others.append(swap(theirs, YBIT))
    low_first = jnp.concatenate(outs + others, axis=1)
    high_first = jnp.concatenate(others + outs, axis=1)
    return jnp.where(upper == 0, low_first, high_first), incoming, queries


def attend(query_part, cache_latents, cache_lens, handed, handed_mark):
    requests = query_part.shape[0]
    cache_scores = (
        jnp.einsum("qhl,qcl->qhc", query_part, cache_latents, preferred_element_type=jnp.float32)
        * score_scale
    )
    hand_scores = (
        jnp.einsum("qhl,rl->qhr", query_part, handed, preferred_element_type=jnp.float32)
        * score_scale
    )
    cache_mask = (
        jnp.arange(cache_latents.shape[1], dtype=jnp.int32)[None, :] < cache_lens[:, None]
    )[:, None, :]
    marks = jnp.arange(1, requests + 1, dtype=jnp.int32).astype(jnp.float32)
    hand_mask = (handed_mark[None, :] == marks[:, None])[:, None, :]
    cache_scores = jnp.where(cache_mask, cache_scores, -jnp.inf)
    hand_scores = jnp.where(hand_mask, hand_scores, -jnp.inf)
    top = jnp.maximum(jnp.max(cache_scores, axis=2), jnp.max(hand_scores, axis=2))[:, :, None]
    cache_expo = jnp.exp(cache_scores - top)
    hand_expo = jnp.exp(hand_scores - top)
    denom = (jnp.sum(cache_expo, axis=2) + jnp.sum(hand_expo, axis=2))[:, :, None]
    cache_prob = (cache_expo / denom).astype(jnp.bfloat16)
    hand_prob = (hand_expo / denom).astype(jnp.bfloat16)
    result = jnp.einsum(
        "qhc,qcv->qhv", cache_prob, cache_latents[:, :, :VDIM], preferred_element_type=jnp.float32
    )
    result = result + jnp.einsum(
        "qhr,rv->qhv", hand_prob, handed[:, :VDIM], preferred_element_type=jnp.float32
    )
    return result.astype(jnp.bfloat16)


def hand_over(prompt_latents, owners, requests):
    n_ep = lax.axis_size("ep")
    stretch, lat = prompt_latents.shape
    cap = 2 * stretch // n_ep
    places_at = jnp.arange(stretch, dtype=jnp.int32)
    earlier = (owners[:, None] == owners[None, :]) & (places_at[None, :] < places_at[:, None])
    target = owners * cap + jnp.sum(earlier.astype(jnp.int32), axis=1)
    slots = jnp.arange(n_ep * cap, dtype=jnp.int32)
    chosen = slots[:, None] == target[None, :]
    packed = jnp.dot(
        chosen.astype(jnp.bfloat16), prompt_latents, preferred_element_type=jnp.float32
    ).astype(jnp.bfloat16)
    mark = jnp.sum(jnp.where(chosen, requests[None, :] + 1, 0), axis=1).astype(jnp.bfloat16)
    fill = -(lat + 1) % 128
    outgoing = jnp.concatenate(
        [packed, mark[:, None], jnp.zeros((n_ep * cap, fill), jnp.bfloat16)], axis=1
    )
    return outgoing.reshape(n_ep, cap, lat + 1 + fill)


def on_device(
    moe_rows,
    routes,
    route_gates,
    gate_proj,
    up_proj,
    down_proj,
    queries,
    cache_latents,
    cache_lens,
    prompt_latents,
    kv_owner,
    kv_request,
):
    sections, count, width = moe_rows.shape
    top = routes.shape[2]
    expert_out, incoming, queries = expert_rows(
        moe_rows.reshape(sections * count, width),
        routes.reshape(sections * count, top),
        route_gates.reshape(sections * count, top),
        prompt_latents,
        kv_owner[:, 0],
        kv_request,
        queries,
        gate_proj,
        up_proj,
        down_proj,
    )
    expert_out = expert_out.reshape(moe_rows.shape)
    lat = prompt_latents.shape[1]
    handed = incoming[:, :, :lat].reshape(-1, lat)
    handed_mark = incoming[:, :, lat].reshape(-1).astype(jnp.float32)
    attended = attend(queries, cache_latents, cache_lens, handed, handed_mark)
    return (expert_out, attended)


def solution(mesh):
    placed = (
        P("section", ("groups", "ep"), None),
        P("section", ("groups", "ep"), None),
        P("section", ("groups", "ep"), None),
        P(None, "ep"),
        P(None, "ep"),
        P("ep", None),
        P(("groups", "ep"), None, None),
        P(("groups", "ep"), None, None),
        P(("groups", "ep")),
        P(("groups", "ep"), None),
        P(("groups", "ep"), None),
        P(("groups", "ep")),
    )
    return jax.shard_map(
        on_device,
        mesh=mesh,
        in_specs=placed,
        out_specs=(P("section", ("groups", "ep"), None), P(("groups", "ep"), None, None)),
        check_vma=False,
    )
```

```python
from functools import partial

import jax
import jax.numpy as jnp
from jax import lax
from jax.experimental import pallas as pl
from jax.experimental.pallas import tpu as pltpu
from jax.sharding import PartitionSpec as P

VDIM = 512
FF_WIN = 1024
CORE, XBIT, YBIT = 1, 2, 4
VMEM_BYTES = 60 * 1024 * 1024


score_scale = 0.07216878364870323


def swap(value, bit):
    count = lax.axis_size("ep")
    return lax.ppermute(value, "ep", [(i, i ^ bit) for i in range(count)])


def shift(value, step):
    count = lax.axis_size("ep")
    return lax.ppermute(value, "ep", [(i, (i + step) % count) for i in range(count)])


def together(*values):
    return lax.optimization_barrier(values)


def pair_dot(rows, left, right):
    both = jnp.concatenate([left[...], right[...]], axis=1)
    return jnp.dot(rows, both, preferred_element_type=jnp.float32)


def gated(gate, up):
    return (gate / (1.0 + jnp.exp(-gate)) * up).astype(jnp.bfloat16)


def pack_kernel(chosen, rows, *outs):
    picked = jnp.dot(chosen[...], rows[...], preferred_element_type=jnp.float32)
    picked = picked.astype(jnp.bfloat16)
    slots = outs[0].shape[0]
    for at, out in enumerate(outs):
        out[...] = picked[at * slots : (at + 1) * slots]


def packs(chosen, rows, planes, chunk):
    count, width = rows.shape
    slots = chosen.shape[0] // planes
    return pl.pallas_call(
        pack_kernel,
        grid=(width // chunk,),
        in_specs=[
            pl.BlockSpec(chosen.shape, lambda k: (0, 0)),
            pl.BlockSpec((count, chunk), lambda k: (0, k)),
        ],
        out_specs=[pl.BlockSpec((slots, chunk), lambda k: (0, k))] * planes,
        out_shape=[jax.ShapeDtypeStruct((slots, width), jnp.bfloat16)] * planes,
        compiler_params=pltpu.CompilerParams(vmem_limit_bytes=VMEM_BYTES),
        cost_estimate=pl.CostEstimate(
            flops=2 * chosen.size * width,
            bytes_accessed=2 * width * (count + planes * slots),
            transcendentals=0,
        ),
    )(chosen, rows)


def hidden_kernel(count, *refs):
    units, weights = refs[:count], refs[count : count + 8]
    gate_o, gate_c, gate_x, gate_xc, up_o, up_c, up_x, up_xc = weights
    out, near_gate, far_gate, near_up, far_up = refs[count + 8 :]
    step = pl.program_id(0)

    @pl.when(step == 0)
    def _():
        for total in (near_gate, far_gate, near_up, far_up):
            total[...] = jnp.zeros_like(total)

    rows = jnp.concatenate([unit[...] for unit in units], axis=0)
    near_gate[...] += pair_dot(rows, gate_o, gate_c)
    near_up[...] += pair_dot(rows, up_o, up_c)
    far_gate[...] += pair_dot(rows, gate_x, gate_xc)
    far_up[...] += pair_dot(rows, up_x, up_xc)

    @pl.when(step == pl.num_programs(0) - 1)
    def _():
        two = near_up.shape[1]
        out[:, :two] = gated(near_gate[...], near_up[...])
        out[:, two:] = gated(far_gate[...], far_up[...])


def hidden_units(units, weights, chunk):
    width, wide = weights[0].shape
    count = sum(unit.shape[0] for unit in units)
    return pl.pallas_call(
        partial(hidden_kernel, len(units)),
        grid=(width // chunk,),
        in_specs=[pl.BlockSpec((unit.shape[0], chunk), lambda k: (0, k)) for unit in units]
        + [pl.BlockSpec((chunk, wide), lambda k: (k, 0)) for _ in weights],
        out_specs=pl.BlockSpec((count, 4 * wide), lambda k: (0, 0)),
        out_shape=jax.ShapeDtypeStruct((count, 4 * wide), jnp.bfloat16),
        scratch_shapes=[pltpu.VMEM((count, 2 * wide), jnp.float32)] * 4,
        compiler_params=pltpu.CompilerParams(vmem_limit_bytes=VMEM_BYTES),
        cost_estimate=pl.CostEstimate(
            flops=2 * count * width * wide * 8,
            bytes_accessed=2 * width * (count + wide * 8),
            transcendentals=0,
        ),
    )(*units, *weights)


def down_kernel(mine, other, own, own_c, side, side_c, *outs):
    deep = own.shape[0] // 2
    parts = (own, own_c, side, side_c)
    table = jnp.concatenate(
        [part[:deep, :] for part in parts] + [part[deep:, :] for part in parts], axis=0
    )
    count = mine.shape[0] // 2
    rows = count // len(outs)
    joined = jnp.concatenate(
        [
            jnp.concatenate([mine[:count, :], other[count:, :]], axis=1),
            jnp.concatenate([mine[count:, :], other[:count, :]], axis=1),
        ],
        axis=0,
    )
    value = jnp.dot(joined, table, preferred_element_type=jnp.float32).astype(jnp.bfloat16)
    for at, out in enumerate(outs):
        out[:rows, :] = value[at * rows : (at + 1) * rows]
        out[rows:, :] = value[count + at * rows : count + (at + 1) * rows]


def down_values(mine, other, own, side, planes, chunk, offset):
    count, inner = mine.shape
    deep, width = side[0].shape
    rows = count // planes
    return pl.pallas_call(
        down_kernel,
        grid=(width // chunk,),
        in_specs=[pl.BlockSpec((count, inner), lambda k: (0, 0))] * 2
        + [pl.BlockSpec((deep, chunk), lambda k: (0, k + offset)) for _ in own]
        + [pl.BlockSpec((deep, chunk), lambda k: (0, k)) for _ in side],
        out_specs=[pl.BlockSpec((rows, chunk), lambda k: (0, k))] * planes,
        out_shape=[jax.ShapeDtypeStruct((rows, width), jnp.bfloat16)] * planes,
        compiler_params=pltpu.CompilerParams(vmem_limit_bytes=VMEM_BYTES),
        cost_estimate=pl.CostEstimate(
            flops=2 * count * 2 * inner * width,
            bytes_accessed=8 * deep * width + 2 * count * width,
            transcendentals=0,
        ),
    )(mine, other, *own, *side)


def combine_kernel(high, low, *refs):
    parts, (mine, theirs) = refs[:-2], refs[-2:]
    values = jnp.concatenate([part[...] for part in parts], axis=0)
    total = jnp.dot(high[...], values, preferred_element_type=jnp.float32)
    total = total + jnp.dot(low[...], values, preferred_element_type=jnp.float32)
    rows = mine.shape[0]
    mine[...] = total[:rows].astype(jnp.bfloat16)
    theirs[...] = total[rows:].astype(jnp.bfloat16)


def combine(high, low, parts, chunk):
    rows, width = parts[0].shape
    count = high.shape[0] // 2
    out = jax.ShapeDtypeStruct((count, width), jnp.bfloat16)
    return pl.pallas_call(
        combine_kernel,
        grid=(width // chunk,),
        in_specs=[pl.BlockSpec(high.shape, lambda k: (0, 0))] * 2
        + [pl.BlockSpec((rows, chunk), lambda k: (0, k)) for _ in parts],
        out_specs=[pl.BlockSpec((count, chunk), lambda k: (0, k))] * 2,
        out_shape=[out, out],
        compiler_params=pltpu.CompilerParams(vmem_limit_bytes=VMEM_BYTES),
        cost_estimate=pl.CostEstimate(
            flops=4 * high.size * width,
            bytes_accessed=2 * width * (len(parts) * rows + 2 * count),
            transcendentals=0,
        ),
    )(high, low, *parts)


def places(picks, planes, split):
    count = picks.shape[0]
    plane = lax.axis_index("ep") // split
    experts = (plane + jnp.arange(planes, dtype=jnp.int32)) % planes
    named = jnp.any(picks[None] == experts[:, None, None], axis=2)
    order = jnp.arange(count, dtype=jnp.int32)
    before = order[:, None] < order[None, :]
    rank = jnp.sum((named[:, :, None] & before[None]).astype(jnp.int32), axis=1)
    return experts, named, rank


def gate_table(picks, gates, planes, split, slots):
    experts, named, rank = places(picks, planes, split)
    weight = jnp.sum(
        jnp.where(picks[None] == experts[:, None, None], gates[None], jnp.zeros_like(gates)[None]),
        axis=2,
    )
    at = jnp.arange(slots, dtype=jnp.int32)
    found = (rank.T[:, :, None] == at[None, None, :]) & named.T[:, :, None]
    return jnp.where(found, weight.T[:, :, None], 0.0)


def layer(
    rows,
    picks,
    gates,
    latents,
    owners,
    requests,
    queries,
    cache_latents,
    cache_lens,
    gate_proj,
    up_proj,
    down_proj,
):
    n_ep = lax.axis_size("ep")
    split = FF_WIN // gate_proj.shape[1]
    planes = n_ep // split
    count, width = rows.shape
    slots = -(-3 * count * picks.shape[1] // (2 * planes * 16)) * 16
    chunk = width // 4
    upper = lax.axis_index("ep") // YBIT % 2
    span = width // 4

    gate_x = swap(gate_proj, XBIT)
    _, named, rank = places(picks, planes, split)
    at = jnp.arange(slots, dtype=jnp.int32)
    chosen = (rank[:, None, :] == at[None, :, None]) & named[:, None, :]
    chosen = chosen.astype(jnp.bfloat16)

    pack_0, out_1, out_2, out_3 = packs(
        chosen.reshape(planes * slots, count), rows, planes, 2 * span
    )
    pack_0, out_1, out_3, latents, owners, requests, down_proj = together(
        pack_0, out_1, out_3, latents, owners, requests, down_proj
    )
    own_1, own_3, peer_0 = shift(out_1, split), shift(out_3, 3 * split), swap(pack_0, YBIT)
    send = lax.dynamic_slice_in_dim(down_proj, (2 - 2 * upper) * span, 2 * span, 1)
    down_y = swap(send, YBIT)
    outgoing = hand_over(latents, owners, requests)

    incoming = lax.all_to_all(outgoing, "ep", split_axis=0, concat_axis=0, tiled=True)
    own_1, own_3, peer_0, down_y, gate_x, out_2, incoming, down_proj, gate_proj = together(
        own_1, own_3, peer_0, down_y, gate_x, out_2, incoming, down_proj, gate_proj
    )
    handed = incoming.reshape(-1, incoming.shape[2])
    marks = handed[:, latents.shape[1]].astype(jnp.float32)[None, :]
    attended = attend(queries, cache_latents, cache_lens, handed, marks)
    own_2, peer_1, peer_3 = shift(out_2, 2 * split), swap(own_1, YBIT), swap(own_3, YBIT)
    up_x, gate_c = swap(up_proj, XBIT), swap(gate_proj, CORE)
    keep = lax.dynamic_slice_in_dim(down_proj, 2 * upper * span, 2 * span, 1)
    own = jnp.concatenate([keep, down_y], axis=0)
    own_0, rest = own[:, :span], own[:, span:]

    own_2, peer_1, peer_3, up_x, gate_x, gate_c, up_proj, own, own_0, rest, attended = together(
        own_2, peer_1, peer_3, up_x, gate_x, gate_c, up_proj, own, own_0, rest, attended
    )
    peer_2, side_0 = swap(own_2, YBIT), swap(own_0, XBIT)
    up_c, gate_xc, up_xc = swap(up_proj, CORE), swap(gate_x, CORE), swap(up_x, CORE)

    peer_2, up_c, gate_xc, up_xc, own = together(peer_2, up_c, gate_xc, up_xc, own)
    own_c = swap(own, CORE)
    units = (pack_0, own_1, own_2, own_3, peer_0, peer_1, peer_2, peer_3)
    weights = (gate_proj, gate_c, gate_x, gate_xc, up_proj, up_c, up_x, up_xc)
    hidden = hidden_units(units, weights, chunk)
    hidden, own_c, side_0, rest, picks, gates = together(
        hidden, own_c, side_0, rest, picks, gates
    )
    other, side_0c, side_1 = swap(hidden, YBIT), swap(side_0, CORE), swap(rest, XBIT)
    info = swap(jnp.concatenate([picks.astype(jnp.float32), gates], axis=1), YBIT)
    other, side_0c, info, picks, gates = together(other, side_0c, info, picks, gates)
    halves = (
        down_values(hidden, other, (own, own_c), (side_0, side_0c), planes, span // 2, 0),
        down_values(hidden, other, (own, own_c), (side_1, swap(side_1, CORE)), planes, span // 2, 2),
    )

    top = picks.shape[1]
    tables = [
        gate_table(picks, gates, planes, split, slots),
        gate_table(info[:, :top].astype(jnp.int32), info[:, top:], planes, split, slots),
    ]
    tables = [
        jnp.pad(tables[0], ((0, 0), (0, 0), (0, slots))),
        jnp.pad(tables[1], ((0, 0), (0, 0), (slots, 0))),
    ]
    table = jnp.concatenate(tables, axis=0).reshape(2 * count, planes * 2 * slots)
    high = lax.reduce_precision(table, 8, 7)
    high, low = high.astype(jnp.bfloat16), (table - high).astype(jnp.bfloat16)

    backs = [
        [values[0]] + [shift(values[k], n_ep - k * split) for k in range(1, planes)]
        for values in halves
    ]
    flat = together(*backs[0], *backs[1])
    outs, others = [], []
    for back in (flat[:planes], flat[planes:]):
        mine, theirs = combine(high, low, back, span // 2)
        outs.append(mine)
        others.append(swap(theirs, YBIT))
    low_first = jnp.concatenate(outs + others, axis=1)
    high_first = jnp.concatenate(others + outs, axis=1)
    return jnp.where(upper == 0, low_first, high_first), attended


def attend_kernel(lens, query, cache, handed, marks, out):
    request = pl.program_id(0)
    heads = query.shape[2]
    wide = out.shape[2]
    lat = query.shape[1]
    asked = query[0].astype(jnp.float32).T.astype(jnp.bfloat16)
    given = handed[:, :lat]
    near = jnp.dot(asked, cache[0], preferred_element_type=jnp.float32) * score_scale
    over_last = (((1,), (1,)), ((), ()))
    far = lax.dot_general(asked, given, over_last, preferred_element_type=jnp.float32)
    far = far * score_scale
    place = lax.broadcasted_iota(jnp.int32, (heads, near.shape[1]), 1)
    near = jnp.where(place < lens[request], near, -jnp.inf)
    mark = (request + 1).astype(jnp.float32)
    far = jnp.where(jnp.broadcast_to(marks[...], far.shape) == mark, far, -jnp.inf)
    top = jnp.maximum(
        jnp.max(near, axis=1, keepdims=True), jnp.max(far, axis=1, keepdims=True)
    )
    near, far = jnp.exp(near - top), jnp.exp(far - top)
    total = jnp.sum(near, axis=1, keepdims=True) + jnp.sum(far, axis=1, keepdims=True)
    near, far = (near / total).astype(jnp.bfloat16), (far / total).astype(jnp.bfloat16)
    result = lax.dot_general(near, cache[0, :wide], over_last, preferred_element_type=jnp.float32)
    result = result + jnp.dot(far, given[:, :wide], preferred_element_type=jnp.float32)
    out[0] = result.astype(jnp.bfloat16)


def attend(queries, cache_latents, cache_lens, handed, marks):
    requests, heads, lat = queries.shape
    cached = cache_latents.shape[1]
    return pl.pallas_call(
        attend_kernel,
        grid=(requests,),
        in_specs=[
            pl.BlockSpec(memory_space=pltpu.SMEM),
            pl.BlockSpec((1, lat, heads), lambda k: (k, 0, 0)),
            pl.BlockSpec((1, lat, cached), lambda k: (k, 0, 0)),
            pl.BlockSpec(handed.shape, lambda k: (0, 0)),
            pl.BlockSpec(marks.shape, lambda k: (0, 0)),
        ],
        out_specs=pl.BlockSpec((1, heads, VDIM), lambda k: (k, 0, 0)),
        out_shape=jax.ShapeDtypeStruct((requests, heads, VDIM), jnp.bfloat16),
        compiler_params=pltpu.CompilerParams(vmem_limit_bytes=VMEM_BYTES),
        cost_estimate=pl.CostEstimate(
            flops=2 * requests * heads * (cached + handed.shape[0]) * (lat + VDIM),
            bytes_accessed=2 * requests * (heads * (lat + VDIM) + cached * lat),
            transcendentals=requests * heads * (cached + handed.shape[0]),
        ),
    )(
        cache_lens,
        jnp.swapaxes(queries, 1, 2),
        jnp.swapaxes(cache_latents, 1, 2),
        handed,
        marks,
    )


def hand_over(prompt_latents, owners, requests):
    n_ep = lax.axis_size("ep")
    stretch, lat = prompt_latents.shape
    cap = 2 * stretch // n_ep
    places_at = jnp.arange(stretch, dtype=jnp.int32)
    earlier = (owners[:, None] == owners[None, :]) & (places_at[None, :] < places_at[:, None])
    target = owners * cap + jnp.sum(earlier.astype(jnp.int32), axis=1)
    slots = jnp.arange(n_ep * cap, dtype=jnp.int32)
    chosen = slots[:, None] == target[None, :]
    packed = jnp.dot(
        chosen.astype(jnp.bfloat16), prompt_latents, preferred_element_type=jnp.float32
    ).astype(jnp.bfloat16)
    mark = jnp.sum(jnp.where(chosen, requests[None, :] + 1, 0), axis=1).astype(jnp.bfloat16)
    fill = -(lat + 1) % 128
    outgoing = jnp.concatenate(
        [packed, mark[:, None], jnp.zeros((n_ep * cap, fill), jnp.bfloat16)], axis=1
    )
    return outgoing.reshape(n_ep, cap, lat + 1 + fill)


def on_device(
    moe_rows,
    routes,
    route_gates,
    gate_proj,
    up_proj,
    down_proj,
    queries,
    cache_latents,
    cache_lens,
    prompt_latents,
    kv_owner,
    kv_request,
):
    sections, count, width = moe_rows.shape
    top = routes.shape[2]
    expert_out, attended = layer(
        moe_rows.reshape(sections * count, width),
        routes.reshape(sections * count, top),
        route_gates.reshape(sections * count, top),
        prompt_latents,
        kv_owner[:, 0],
        kv_request,
        queries,
        cache_latents,
        cache_lens,
        gate_proj,
        up_proj,
        down_proj,
    )
    expert_out = expert_out.reshape(moe_rows.shape)
    return (expert_out, attended)


def solution(mesh):
    placed = (
        P("section", ("groups", "ep"), None),
        P("section", ("groups", "ep"), None),
        P("section", ("groups", "ep"), None),
        P(None, "ep"),
        P(None, "ep"),
        P("ep", None),
        P(("groups", "ep"), None, None),
        P(("groups", "ep"), None, None),
        P(("groups", "ep")),
        P(("groups", "ep"), None),
        P(("groups", "ep"), None),
        P(("groups", "ep")),
    )
    return jax.shard_map(
        on_device,
        mesh=mesh,
        in_specs=placed,
        out_specs=(P("section", ("groups", "ep"), None), P(("groups", "ep"), None, None)),
        check_vma=False,
    )
```

```python
from functools import partial

import jax
import jax.numpy as jnp
from jax import lax
from jax.experimental import pallas as pl
from jax.experimental.pallas import tpu as pltpu
from jax.sharding import PartitionSpec as P

VDIM = 512
FF_WIN = 1024
CORE, XBIT, YBIT = 1, 2, 4
VMEM_BYTES = 60 * 1024 * 1024
SMALL_BYTES = 14 * 1024 * 1024


score_scale = 0.07216878364870323


def swap(value, bit):
    count = lax.axis_size("ep")
    return lax.ppermute(value, "ep", [(i, i ^ bit) for i in range(count)])


def shift(value, step):
    count = lax.axis_size("ep")
    return lax.ppermute(value, "ep", [(i, (i + step) % count) for i in range(count)])


def together(*values):
    return lax.optimization_barrier(values)


def pair_dot(rows, left, right):
    both = jnp.concatenate([left[...], right[...]], axis=1)
    return jnp.dot(rows, both, preferred_element_type=jnp.float32)


def gated(gate, up):
    return (gate / (1.0 + jnp.exp(-gate)) * up).astype(jnp.bfloat16)


def pack_kernel(chosen, rows, *outs):
    picked = jnp.dot(chosen[...], rows[...], preferred_element_type=jnp.float32)
    picked = picked.astype(jnp.bfloat16)
    slots = outs[0].shape[0]
    for at, out in enumerate(outs):
        out[...] = picked[at * slots : (at + 1) * slots]


def packs(chosen, rows, planes, chunk):
    count, width = rows.shape
    slots = chosen.shape[0] // planes
    return pl.pallas_call(
        pack_kernel,
        grid=(width // chunk,),
        in_specs=[
            pl.BlockSpec(chosen.shape, lambda k: (0, 0)),
            pl.BlockSpec((count, chunk), lambda k: (0, k)),
        ],
        out_specs=[pl.BlockSpec((slots, chunk), lambda k: (0, k))] * planes,
        out_shape=[jax.ShapeDtypeStruct((slots, width), jnp.bfloat16)] * planes,
        compiler_params=pltpu.CompilerParams(vmem_limit_bytes=SMALL_BYTES),
        cost_estimate=pl.CostEstimate(
            flops=2 * chosen.size * width,
            bytes_accessed=2 * width * (count + planes * slots),
            transcendentals=0,
        ),
    )(chosen, rows)


def hidden_kernel(count, *refs):
    units, weights = refs[:count], refs[count : count + 8]
    gate_o, gate_c, gate_x, gate_xc, up_o, up_c, up_x, up_xc = weights
    out, near_gate, far_gate, near_up, far_up = refs[count + 8 :]
    step = pl.program_id(0)

    @pl.when(step == 0)
    def _():
        for total in (near_gate, far_gate, near_up, far_up):
            total[...] = jnp.zeros_like(total)

    rows = jnp.concatenate([unit[...] for unit in units], axis=0)
    near_gate[...] += pair_dot(rows, gate_o, gate_c)
    near_up[...] += pair_dot(rows, up_o, up_c)
    far_gate[...] += pair_dot(rows, gate_x, gate_xc)
    far_up[...] += pair_dot(rows, up_x, up_xc)

    @pl.when(step == pl.num_programs(0) - 1)
    def _():
        two = near_up.shape[1]
        out[:, :two] = gated(near_gate[...], near_up[...])
        out[:, two:] = gated(far_gate[...], far_up[...])


def hidden_units(units, weights, chunk):
    width, wide = weights[0].shape
    count = sum(unit.shape[0] for unit in units)
    return pl.pallas_call(
        partial(hidden_kernel, len(units)),
        grid=(width // chunk,),
        in_specs=[pl.BlockSpec((unit.shape[0], chunk), lambda k: (0, k)) for unit in units]
        + [pl.BlockSpec((chunk, wide), lambda k: (k, 0)) for _ in weights],
        out_specs=pl.BlockSpec((count, 4 * wide), lambda k: (0, 0)),
        out_shape=jax.ShapeDtypeStruct((count, 4 * wide), jnp.bfloat16),
        scratch_shapes=[pltpu.VMEM((count, 2 * wide), jnp.float32)] * 4,
        compiler_params=pltpu.CompilerParams(vmem_limit_bytes=VMEM_BYTES),
        cost_estimate=pl.CostEstimate(
            flops=2 * count * width * wide * 8,
            bytes_accessed=2 * width * (count + wide * 8),
            transcendentals=0,
        ),
    )(*units, *weights)


def down_kernel(mine, other, own, own_c, side, side_c, *outs):
    deep = own.shape[0] // 2
    parts = (own, own_c, side, side_c)
    table = jnp.concatenate(
        [part[:deep, :] for part in parts] + [part[deep:, :] for part in parts], axis=0
    )
    count = mine.shape[0] // 2
    rows = count // len(outs)
    joined = jnp.concatenate(
        [
            jnp.concatenate([mine[:count, :], other[count:, :]], axis=1),
            jnp.concatenate([mine[count:, :], other[:count, :]], axis=1),
        ],
        axis=0,
    )
    value = jnp.dot(joined, table, preferred_element_type=jnp.float32).astype(jnp.bfloat16)
    for at, out in enumerate(outs):
        out[:rows, :] = value[at * rows : (at + 1) * rows]
        out[rows:, :] = value[count + at * rows : count + (at + 1) * rows]


def down_values(mine, other, own, side, planes, chunk, offset):
    count, inner = mine.shape
    deep, width = side[0].shape
    rows = count // planes
    return pl.pallas_call(
        down_kernel,
        grid=(width // chunk,),
        in_specs=[pl.BlockSpec((count, inner), lambda k: (0, 0))] * 2
        + [pl.BlockSpec((deep, chunk), lambda k: (0, k + offset)) for _ in own]
        + [pl.BlockSpec((deep, chunk), lambda k: (0, k)) for _ in side],
        out_specs=[pl.BlockSpec((rows, chunk), lambda k: (0, k))] * planes,
        out_shape=[jax.ShapeDtypeStruct((rows, width), jnp.bfloat16)] * planes,
        compiler_params=pltpu.CompilerParams(vmem_limit_bytes=SMALL_BYTES),
        cost_estimate=pl.CostEstimate(
            flops=2 * count * 2 * inner * width,
            bytes_accessed=8 * deep * width + 2 * count * width,
            transcendentals=0,
        ),
    )(mine, other, *own, *side)


def combine_kernel(high, low, *refs):
    parts, (mine, theirs) = refs[:-2], refs[-2:]
    values = jnp.concatenate([part[...] for part in parts], axis=0)
    total = jnp.dot(high[...], values, preferred_element_type=jnp.float32)
    total = total + jnp.dot(low[...], values, preferred_element_type=jnp.float32)
    rows = mine.shape[0]
    mine[...] = total[:rows].astype(jnp.bfloat16)
    theirs[...] = total[rows:].astype(jnp.bfloat16)


def combine(high, low, parts, chunk):
    rows, width = parts[0].shape
    count = high.shape[0] // 2
    out = jax.ShapeDtypeStruct((count, width), jnp.bfloat16)
    return pl.pallas_call(
        combine_kernel,
        grid=(width // chunk,),
        in_specs=[pl.BlockSpec(high.shape, lambda k: (0, 0))] * 2
        + [pl.BlockSpec((rows, chunk), lambda k: (0, k)) for _ in parts],
        out_specs=[pl.BlockSpec((count, chunk), lambda k: (0, k))] * 2,
        out_shape=[out, out],
        compiler_params=pltpu.CompilerParams(vmem_limit_bytes=SMALL_BYTES),
        cost_estimate=pl.CostEstimate(
            flops=4 * high.size * width,
            bytes_accessed=2 * width * (len(parts) * rows + 2 * count),
            transcendentals=0,
        ),
    )(high, low, *parts)


def places(picks, planes, split):
    count = picks.shape[0]
    plane = lax.axis_index("ep") // split
    experts = (plane + jnp.arange(planes, dtype=jnp.int32)) % planes
    named = jnp.any(picks[None] == experts[:, None, None], axis=2)
    order = jnp.arange(count, dtype=jnp.int32)
    before = order[:, None] < order[None, :]
    rank = jnp.sum((named[:, :, None] & before[None]).astype(jnp.int32), axis=1)
    return experts, named, rank


def gate_table(picks, gates, planes, split, slots):
    experts, named, rank = places(picks, planes, split)
    weight = jnp.sum(
        jnp.where(picks[None] == experts[:, None, None], gates[None], jnp.zeros_like(gates)[None]),
        axis=2,
    )
    at = jnp.arange(slots, dtype=jnp.int32)
    found = (rank.T[:, :, None] == at[None, None, :]) & named.T[:, :, None]
    return jnp.where(found, weight.T[:, :, None], 0.0)


def layer(
    rows,
    picks,
    gates,
    latents,
    owners,
    requests,
    queries,
    cache_latents,
    cache_lens,
    gate_proj,
    up_proj,
    down_proj,
):
    n_ep = lax.axis_size("ep")
    split = FF_WIN // gate_proj.shape[1]
    planes = n_ep // split
    count, width = rows.shape
    slots = -(-3 * count * picks.shape[1] // (2 * planes * 16)) * 16
    chunk = width // 4
    upper = lax.axis_index("ep") // YBIT % 2
    span = width // 4

    gate_x = swap(gate_proj, XBIT)
    _, named, rank = places(picks, planes, split)
    at = jnp.arange(slots, dtype=jnp.int32)
    chosen = (rank[:, None, :] == at[None, :, None]) & named[:, None, :]
    chosen = chosen.astype(jnp.bfloat16)

    pack_0, out_1, out_2, out_3 = packs(
        chosen.reshape(planes * slots, count), rows, planes, span
    )
    pack_0, out_1, out_3, latents, owners, requests, down_proj = together(
        pack_0, out_1, out_3, latents, owners, requests, down_proj
    )
    own_1, own_3, peer_0 = shift(out_1, split), shift(out_3, 3 * split), swap(pack_0, YBIT)
    send = lax.dynamic_slice_in_dim(down_proj, (2 - 2 * upper) * span, 2 * span, 1)
    down_y = swap(send, YBIT)
    outgoing = hand_over(latents, owners, requests)

    own_1, own_3, peer_0, down_y, gate_x, out_2, outgoing, down_proj, gate_proj = together(
        own_1, own_3, peer_0, down_y, gate_x, out_2, outgoing, down_proj, gate_proj
    )
    own_2, peer_1, peer_3 = shift(out_2, 2 * split), swap(own_1, YBIT), swap(own_3, YBIT)
    up_x, gate_c = swap(up_proj, XBIT), swap(gate_proj, CORE)
    keep = lax.dynamic_slice_in_dim(down_proj, 2 * upper * span, 2 * span, 1)
    own = jnp.concatenate([keep, down_y], axis=0)
    own_0, rest = own[:, :span], own[:, span:]

    own_2, peer_1, peer_3, up_x, gate_x, gate_c, up_proj, own, own_0, rest = together(
        own_2, peer_1, peer_3, up_x, gate_x, gate_c, up_proj, own, own_0, rest
    )
    peer_2, side_0 = swap(own_2, YBIT), swap(own_0, XBIT)
    up_c, gate_xc, up_xc = swap(up_proj, CORE), swap(gate_x, CORE), swap(up_x, CORE)

    peer_2, up_c, gate_xc, up_xc, side_0, own = together(
        peer_2, up_c, gate_xc, up_xc, side_0, own
    )
    own_c, side_0c = swap(own, CORE), swap(side_0, CORE)
    units = (pack_0, own_1, own_2, own_3, peer_0, peer_1, peer_2, peer_3)
    weights = (gate_proj, gate_c, gate_x, gate_xc, up_proj, up_c, up_x, up_xc)
    hidden = hidden_units(units, weights, chunk)
    hidden, own_c, side_0c, rest, picks, gates = together(
        hidden, own_c, side_0c, rest, picks, gates
    )
    other, side_1 = swap(hidden, YBIT), swap(rest, XBIT)
    info = swap(jnp.concatenate([picks.astype(jnp.float32), gates], axis=1), YBIT)
    first = down_values(
        hidden, other, (own, own_c), (side_0, side_0c), planes, span // 2, 0
    )
    first = list(first)
    side_1, info, picks, gates, first[0] = together(side_1, info, picks, gates, first[0])
    second = down_values(
        hidden, other, (own, own_c), (side_1, swap(side_1, CORE)), planes, span // 2, 2
    )
    second = list(second)
    outgoing, second[0] = together(outgoing, second[0])
    incoming = lax.all_to_all(outgoing, "ep", split_axis=0, concat_axis=0, tiled=True)
    handed = incoming.reshape(-1, incoming.shape[2])
    marks = handed[:, latents.shape[1]].astype(jnp.float32)[None, :]
    attended = attend(queries, cache_latents, cache_lens, handed, marks)

    top = picks.shape[1]
    tables = [
        gate_table(picks, gates, planes, split, slots),
        gate_table(info[:, :top].astype(jnp.int32), info[:, top:], planes, split, slots),
    ]
    tables = [
        jnp.pad(tables[0], ((0, 0), (0, 0), (0, slots))),
        jnp.pad(tables[1], ((0, 0), (0, 0), (slots, 0))),
    ]
    table = jnp.concatenate(tables, axis=0).reshape(2 * count, planes * 2 * slots)
    high = lax.reduce_precision(table, 8, 7)
    high, low = high.astype(jnp.bfloat16), (table - high).astype(jnp.bfloat16)

    backs = [
        [values[0]] + [shift(values[k], n_ep - k * split) for k in range(1, planes)]
        for values in (first, second)
    ]
    *flat, attended = together(*backs[0], *backs[1], attended)
    outs, others = [], []
    for back in (flat[:planes], flat[planes:]):
        mine, theirs = combine(high, low, back, span // 2)
        outs.append(mine)
        others.append(swap(theirs, YBIT))
    low_first = jnp.concatenate(outs + others, axis=1)
    high_first = jnp.concatenate(others + outs, axis=1)
    return jnp.where(upper == 0, low_first, high_first), attended


def attend_kernel(lens, query, cache, handed, marks, out):
    request = pl.program_id(0)
    heads = query.shape[2]
    wide = out.shape[2]
    lat = query.shape[1]
    asked = query[0].astype(jnp.float32).T.astype(jnp.bfloat16)
    given = handed[:, :lat]
    near = jnp.dot(asked, cache[0], preferred_element_type=jnp.float32) * score_scale
    over_last = (((1,), (1,)), ((), ()))
    far = lax.dot_general(asked, given, over_last, preferred_element_type=jnp.float32)
    far = far * score_scale
    place = lax.broadcasted_iota(jnp.int32, (heads, near.shape[1]), 1)
    near = jnp.where(place < lens[request], near, -jnp.inf)
    mark = (request + 1).astype(jnp.float32)
    far = jnp.where(jnp.broadcast_to(marks[...], far.shape) == mark, far, -jnp.inf)
    top = jnp.maximum(
        jnp.max(near, axis=1, keepdims=True), jnp.max(far, axis=1, keepdims=True)
    )
    near, far = jnp.exp(near - top), jnp.exp(far - top)
    total = jnp.sum(near, axis=1, keepdims=True) + jnp.sum(far, axis=1, keepdims=True)
    near, far = (near / total).astype(jnp.bfloat16), (far / total).astype(jnp.bfloat16)
    result = lax.dot_general(near, cache[0, :wide], over_last, preferred_element_type=jnp.float32)
    result = result + jnp.dot(far, given[:, :wide], preferred_element_type=jnp.float32)
    out[0] = result.astype(jnp.bfloat16)


def attend(queries, cache_latents, cache_lens, handed, marks):
    requests, heads, lat = queries.shape
    cached = cache_latents.shape[1]
    return pl.pallas_call(
        attend_kernel,
        grid=(requests,),
        in_specs=[
            pl.BlockSpec(memory_space=pltpu.SMEM),
            pl.BlockSpec((1, lat, heads), lambda k: (k, 0, 0)),
            pl.BlockSpec((1, lat, cached), lambda k: (k, 0, 0)),
            pl.BlockSpec(handed.shape, lambda k: (0, 0)),
            pl.BlockSpec(marks.shape, lambda k: (0, 0)),
        ],
        out_specs=pl.BlockSpec((1, heads, VDIM), lambda k: (k, 0, 0)),
        out_shape=jax.ShapeDtypeStruct((requests, heads, VDIM), jnp.bfloat16),
        compiler_params=pltpu.CompilerParams(vmem_limit_bytes=VMEM_BYTES),
        cost_estimate=pl.CostEstimate(
            flops=2 * requests * heads * (cached + handed.shape[0]) * (lat + VDIM),
            bytes_accessed=2 * requests * (heads * (lat + VDIM) + cached * lat),
            transcendentals=requests * heads * (cached + handed.shape[0]),
        ),
    )(
        cache_lens,
        jnp.swapaxes(queries, 1, 2),
        jnp.swapaxes(cache_latents, 1, 2),
        handed,
        marks,
    )


def hand_over(prompt_latents, owners, requests):
    n_ep = lax.axis_size("ep")
    stretch, lat = prompt_latents.shape
    cap = 2 * stretch // n_ep
    places_at = jnp.arange(stretch, dtype=jnp.int32)
    earlier = (owners[:, None] == owners[None, :]) & (places_at[None, :] < places_at[:, None])
    target = owners * cap + jnp.sum(earlier.astype(jnp.int32), axis=1)
    slots = jnp.arange(n_ep * cap, dtype=jnp.int32)
    chosen = slots[:, None] == target[None, :]
    packed = jnp.dot(
        chosen.astype(jnp.bfloat16), prompt_latents, preferred_element_type=jnp.float32
    ).astype(jnp.bfloat16)
    mark = jnp.sum(jnp.where(chosen, requests[None, :] + 1, 0), axis=1).astype(jnp.bfloat16)
    fill = -(lat + 1) % 128
    outgoing = jnp.concatenate(
        [packed, mark[:, None], jnp.zeros((n_ep * cap, fill), jnp.bfloat16)], axis=1
    )
    return outgoing.reshape(n_ep, cap, lat + 1 + fill)


def on_device(
    moe_rows,
    routes,
    route_gates,
    gate_proj,
    up_proj,
    down_proj,
    queries,
    cache_latents,
    cache_lens,
    prompt_latents,
    kv_owner,
    kv_request,
):
    sections, count, width = moe_rows.shape
    top = routes.shape[2]
    expert_out, attended = layer(
        moe_rows.reshape(sections * count, width),
        routes.reshape(sections * count, top),
        route_gates.reshape(sections * count, top),
        prompt_latents,
        kv_owner[:, 0],
        kv_request,
        queries,
        cache_latents,
        cache_lens,
        gate_proj,
        up_proj,
        down_proj,
    )
    expert_out = expert_out.reshape(moe_rows.shape)
    return (expert_out, attended)


def solution(mesh):
    placed = (
        P("section", ("groups", "ep"), None),
        P("section", ("groups", "ep"), None),
        P("section", ("groups", "ep"), None),
        P(None, "ep"),
        P(None, "ep"),
        P("ep", None),
        P(("groups", "ep"), None, None),
        P(("groups", "ep"), None, None),
        P(("groups", "ep")),
        P(("groups", "ep"), None),
        P(("groups", "ep"), None),
        P(("groups", "ep")),
    )
    return jax.shard_map(
        on_device,
        mesh=mesh,
        in_specs=placed,
        out_specs=(P("section", ("groups", "ep"), None), P(("groups", "ep"), None, None)),
        check_vma=False,
    )
```

```python
from functools import partial

import jax
import jax.numpy as jnp
from jax import lax
from jax.experimental import pallas as pl
from jax.experimental.pallas import tpu as pltpu
from jax.sharding import PartitionSpec as P

VDIM = 512
FF_WIN = 1024
CORE, XBIT, YBIT = 1, 2, 4
VMEM_BYTES = 60 * 1024 * 1024
SMALL_BYTES = 14 * 1024 * 1024


score_scale = 0.07216878364870323


def swap(value, bit):
    count = lax.axis_size("ep")
    return lax.ppermute(value, "ep", [(i, i ^ bit) for i in range(count)])


def shift(value, step):
    count = lax.axis_size("ep")
    return lax.ppermute(value, "ep", [(i, (i + step) % count) for i in range(count)])


def cross(value, step):
    count = lax.axis_size("ep")
    pairs = [(i, (i + step) % count ^ YBIT) for i in range(count)]
    return lax.ppermute(value, "ep", pairs)


def together(*values):
    return lax.optimization_barrier(values)


def pair_dot(rows, left, right):
    both = jnp.concatenate([left[...], right[...]], axis=1)
    return jnp.dot(rows, both, preferred_element_type=jnp.float32)


def gated(gate, up):
    return (gate / (1.0 + jnp.exp(-gate)) * up).astype(jnp.bfloat16)


def pack_kernel(chosen, rows, *outs):
    picked = jnp.dot(chosen[...], rows[...], preferred_element_type=jnp.float32)
    picked = picked.astype(jnp.bfloat16)
    slots = outs[0].shape[0]
    for at, out in enumerate(outs):
        out[...] = picked[at * slots : (at + 1) * slots]


def packs(chosen, rows, planes, chunk):
    count, width = rows.shape
    slots = chosen.shape[0] // planes
    return pl.pallas_call(
        pack_kernel,
        grid=(width // chunk,),
        in_specs=[
            pl.BlockSpec(chosen.shape, lambda k: (0, 0)),
            pl.BlockSpec((count, chunk), lambda k: (0, k)),
        ],
        out_specs=[pl.BlockSpec((slots, chunk), lambda k: (0, k))] * planes,
        out_shape=[jax.ShapeDtypeStruct((slots, width), jnp.bfloat16)] * planes,
        compiler_params=pltpu.CompilerParams(vmem_limit_bytes=SMALL_BYTES),
        cost_estimate=pl.CostEstimate(
            flops=2 * chosen.size * width,
            bytes_accessed=2 * width * (count + planes * slots),
            transcendentals=0,
        ),
    )(chosen, rows)


def hidden_kernel(count, *refs):
    units, weights = refs[:count], refs[count : count + 8]
    gate_o, gate_c, gate_x, gate_xc, up_o, up_c, up_x, up_xc = weights
    out, near_gate, far_gate, near_up, far_up = refs[count + 8 :]
    step = pl.program_id(0)

    @pl.when(step == 0)
    def _():
        for total in (near_gate, far_gate, near_up, far_up):
            total[...] = jnp.zeros_like(total)

    rows = jnp.concatenate([unit[...] for unit in units], axis=0)
    near_gate[...] += pair_dot(rows, gate_o, gate_c)
    near_up[...] += pair_dot(rows, up_o, up_c)
    far_gate[...] += pair_dot(rows, gate_x, gate_xc)
    far_up[...] += pair_dot(rows, up_x, up_xc)

    @pl.when(step == pl.num_programs(0) - 1)
    def _():
        two = near_up.shape[1]
        out[:, :two] = gated(near_gate[...], near_up[...])
        out[:, two:] = gated(far_gate[...], far_up[...])


def hidden_units(units, weights, chunk):
    width, wide = weights[0].shape
    count = sum(unit.shape[0] for unit in units)
    return pl.pallas_call(
        partial(hidden_kernel, len(units)),
        grid=(width // chunk,),
        in_specs=[pl.BlockSpec((unit.shape[0], chunk), lambda k: (0, k)) for unit in units]
        + [pl.BlockSpec((chunk, wide), lambda k: (k, 0)) for _ in weights],
        out_specs=pl.BlockSpec((count, 4 * wide), lambda k: (0, 0)),
        out_shape=jax.ShapeDtypeStruct((count, 4 * wide), jnp.bfloat16),
        scratch_shapes=[pltpu.VMEM((count, 2 * wide), jnp.float32)] * 4,
        compiler_params=pltpu.CompilerParams(vmem_limit_bytes=VMEM_BYTES),
        cost_estimate=pl.CostEstimate(
            flops=2 * count * width * wide * 8,
            bytes_accessed=2 * width * (count + wide * 8),
            transcendentals=0,
        ),
    )(*units, *weights)


def down_kernel(mine, other, own, own_c, side_0, side_0c, side_1, side_1c, *outs):
    deep = own.shape[0] // 2
    count = mine.shape[0] // 2
    rows = 2 * count // len(outs)

    def fill(side, side_c):
        parts = (own, own_c, side, side_c)
        table = jnp.concatenate(
            [part[:deep, :] for part in parts] + [part[deep:, :] for part in parts], axis=0
        )
        joined = jnp.concatenate(
            [
                jnp.concatenate([mine[:count, :], other[count:, :]], axis=1),
                jnp.concatenate([mine[count:, :], other[:count, :]], axis=1),
            ],
            axis=0,
        )
        value = jnp.dot(joined, table, preferred_element_type=jnp.float32).astype(jnp.bfloat16)
        for at, out in enumerate(outs):
            out[...] = value[at * rows : (at + 1) * rows]

    first = pl.program_id(0) < pl.num_programs(0) // 2

    @pl.when(first)
    def _():
        fill(side_0, side_0c)

    @pl.when(jnp.logical_not(first))
    def _():
        fill(side_1, side_1c)


def down_values(mine, other, own, firsts, seconds, planes, chunk):
    count, inner = mine.shape
    deep, width = own[0].shape
    rows = count // (2 * planes)
    steps = width // chunk
    half = steps // 2
    return pl.pallas_call(
        down_kernel,
        grid=(steps,),
        in_specs=[pl.BlockSpec((count, inner), lambda k: (0, 0))] * 2
        + [pl.BlockSpec((deep, chunk), lambda k: (0, k)) for _ in own]
        + [pl.BlockSpec((deep, chunk), lambda k: (0, jnp.minimum(k, half - 1))) for _ in firsts]
        + [pl.BlockSpec((deep, chunk), lambda k: (0, jnp.maximum(k - half, 0))) for _ in seconds],
        out_specs=[pl.BlockSpec((rows, chunk), lambda k: (0, k))] * (2 * planes),
        out_shape=[jax.ShapeDtypeStruct((rows, width), jnp.bfloat16)] * (2 * planes),
        compiler_params=pltpu.CompilerParams(vmem_limit_bytes=SMALL_BYTES),
        cost_estimate=pl.CostEstimate(
            flops=2 * count * 2 * inner * width,
            bytes_accessed=8 * deep * width + 2 * count * width,
            transcendentals=0,
        ),
    )(mine, other, *own, *firsts, *seconds)


def combine_kernel(upper, high, low, *refs):
    parts, out = refs[:-1], refs[-1]
    planes = len(parts) // 2

    def mix(chosen):
        values = jnp.concatenate([part[...] for part in chosen], axis=0)
        total = jnp.dot(high[...], values, preferred_element_type=jnp.float32)
        total = total + jnp.dot(low[...], values, preferred_element_type=jnp.float32)
        out[...] = total.astype(jnp.bfloat16)

    side = pl.program_id(0)

    @pl.when(side == 0)
    def _():
        mix(parts[:planes])

    @pl.when(side == 1)
    def _():
        mix(parts[planes:])


def combine(upper, high, low, mine, theirs, chunk):
    rows, width = mine[0].shape
    count = high.shape[0]
    steps = width // chunk

    def own_block(g, k, upper):
        return 0, jnp.where(g == 0, k, steps - 1)

    def other_block(g, k, upper):
        return 0, jnp.where(g == 0, 0, k)

    def out_block(g, k, upper):
        return 0, (upper[0] + g) % 2 * steps + k

    return pl.pallas_call(
        combine_kernel,
        grid_spec=pltpu.PrefetchScalarGridSpec(
            num_scalar_prefetch=1,
            grid=(2, steps),
            in_specs=[pl.BlockSpec(high.shape, lambda g, k, upper: (0, 0))] * 2
            + [pl.BlockSpec((rows, chunk), own_block) for _ in mine]
            + [pl.BlockSpec((rows, chunk), other_block) for _ in theirs],
            out_specs=pl.BlockSpec((count, chunk), out_block),
        ),
        out_shape=jax.ShapeDtypeStruct((count, 2 * width), jnp.bfloat16),
        compiler_params=pltpu.CompilerParams(vmem_limit_bytes=SMALL_BYTES),
        cost_estimate=pl.CostEstimate(
            flops=8 * high.size * width,
            bytes_accessed=4 * width * (len(mine) * rows + count),
            transcendentals=0,
        ),
    )(upper.reshape(1), high, low, *mine, *theirs)


def places(picks, planes, split):
    count = picks.shape[0]
    plane = lax.axis_index("ep") // split
    experts = (plane + jnp.arange(planes, dtype=jnp.int32)) % planes
    named = jnp.any(picks[None] == experts[:, None, None], axis=2)
    order = jnp.arange(count, dtype=jnp.int32)
    before = order[:, None] < order[None, :]
    rank = jnp.sum((named[:, :, None] & before[None]).astype(jnp.int32), axis=1)
    return experts, named, rank


def gate_table(picks, gates, planes, split, slots):
    experts, named, rank = places(picks, planes, split)
    weight = jnp.sum(
        jnp.where(picks[None] == experts[:, None, None], gates[None], jnp.zeros_like(gates)[None]),
        axis=2,
    )
    at = jnp.arange(slots, dtype=jnp.int32)
    found = (rank.T[:, :, None] == at[None, None, :]) & named.T[:, :, None]
    return jnp.where(found, weight.T[:, :, None], 0.0)


def layer(
    rows,
    picks,
    gates,
    latents,
    owners,
    requests,
    queries,
    cache_latents,
    cache_lens,
    gate_proj,
    up_proj,
    down_proj,
):
    n_ep = lax.axis_size("ep")
    split = FF_WIN // gate_proj.shape[1]
    planes = n_ep // split
    count, width = rows.shape
    slots = -(-3 * count * picks.shape[1] // (2 * planes * 16)) * 16
    chunk = width // 4
    upper = lax.axis_index("ep") // YBIT % 2
    span = width // 4

    gate_x = swap(gate_proj, XBIT)
    _, named, rank = places(picks, planes, split)
    at = jnp.arange(slots, dtype=jnp.int32)
    chosen = (rank[:, None, :] == at[None, :, None]) & named[:, None, :]
    chosen = chosen.astype(jnp.bfloat16)

    pack_0, out_1, out_2, out_3 = packs(
        chosen.reshape(planes * slots, count), rows, planes, span
    )
    pack_0, out_1, out_3, latents, owners, requests, down_proj = together(
        pack_0, out_1, out_3, latents, owners, requests, down_proj
    )
    own_1, own_3, peer_0 = shift(out_1, split), shift(out_3, 3 * split), swap(pack_0, YBIT)
    send = lax.dynamic_slice_in_dim(down_proj, (2 - 2 * upper) * span, 2 * span, 1)
    down_y = swap(send, YBIT)
    outgoing = hand_over(latents, owners, requests)

    own_1, own_3, peer_0, down_y, gate_x, out_2, outgoing, down_proj, gate_proj = together(
        own_1, own_3, peer_0, down_y, gate_x, out_2, outgoing, down_proj, gate_proj
    )
    own_2, peer_1, peer_3 = shift(out_2, 2 * split), swap(own_1, YBIT), swap(own_3, YBIT)
    up_x, gate_c = swap(up_proj, XBIT), swap(gate_proj, CORE)
    incoming = lax.all_to_all(outgoing, "ep", split_axis=0, concat_axis=0, tiled=True)
    keep = lax.dynamic_slice_in_dim(down_proj, 2 * upper * span, 2 * span, 1)
    own = jnp.concatenate([keep, down_y], axis=0)
    begin, rest = own[:, :span], own[:, span:]

    own_2, peer_1, peer_3, up_x, gate_x, gate_c, up_proj, own, begin, rest, incoming = together(
        own_2, peer_1, peer_3, up_x, gate_x, gate_c, up_proj, own, begin, rest, incoming
    )
    peer_2, side_0 = swap(own_2, YBIT), swap(begin, XBIT)
    up_c, gate_xc, up_xc = swap(up_proj, CORE), swap(gate_x, CORE), swap(up_x, CORE)
    handed = incoming.reshape(-1, incoming.shape[2])
    marks = handed[:, latents.shape[1]].astype(jnp.float32)[None, :]
    attended = attend(queries, cache_latents, cache_lens, handed, marks)
    peer_2, up_c, gate_xc, up_xc, side_0, rest, own, attended, picks, gates = together(
        peer_2, up_c, gate_xc, up_xc, side_0, rest, own, attended, picks, gates
    )
    own_c, side_0c, side_1 = swap(own, CORE), swap(side_0, CORE), swap(rest, XBIT)
    units = (pack_0, own_1, own_2, own_3, peer_0, peer_1, peer_2, peer_3)
    weights = (gate_proj, gate_c, gate_x, gate_xc, up_proj, up_c, up_x, up_xc)
    hidden = hidden_units(units, weights, chunk)
    hidden, own_c, side_0c, picks, gates = together(hidden, own_c, side_0c, picks, gates)
    table = gate_table(picks, gates, planes, split, slots).reshape(count, planes * slots)
    high = lax.reduce_precision(table, 8, 7)
    high, low = high.astype(jnp.bfloat16), (table - high).astype(jnp.bfloat16)
    other, side_1, high, low = together(swap(hidden, YBIT), side_1, high, low)
    firsts, seconds = (side_0, side_0c), (side_1, swap(side_1, CORE))
    values = down_values(hidden, other, (own, own_c), firsts, seconds, planes, span // 2)
    mine = [values[0]] + [shift(values[k], n_ep - k * split) for k in range(1, planes)]
    theirs = [swap(values[planes], YBIT)] + [
        cross(values[planes + k], n_ep - k * split) for k in range(1, planes)
    ]
    return combine(upper, high, low, mine, theirs, span), attended


def attend_kernel(lens, query, cache, handed, marks, out):
    request = pl.program_id(0)
    heads = query.shape[2]
    wide = out.shape[2]
    lat = query.shape[1]
    asked = query[0].astype(jnp.float32).T.astype(jnp.bfloat16)
    given = handed[:, :lat]
    near = jnp.dot(asked, cache[0], preferred_element_type=jnp.float32) * score_scale
    over_last = (((1,), (1,)), ((), ()))
    far = lax.dot_general(asked, given, over_last, preferred_element_type=jnp.float32)
    far = far * score_scale
    place = lax.broadcasted_iota(jnp.int32, (heads, near.shape[1]), 1)
    near = jnp.where(place < lens[request], near, -jnp.inf)
    mark = (request + 1).astype(jnp.float32)
    far = jnp.where(jnp.broadcast_to(marks[...], far.shape) == mark, far, -jnp.inf)
    top = jnp.maximum(
        jnp.max(near, axis=1, keepdims=True), jnp.max(far, axis=1, keepdims=True)
    )
    near, far = jnp.exp(near - top), jnp.exp(far - top)
    total = jnp.sum(near, axis=1, keepdims=True) + jnp.sum(far, axis=1, keepdims=True)
    near, far = (near / total).astype(jnp.bfloat16), (far / total).astype(jnp.bfloat16)
    result = lax.dot_general(near, cache[0, :wide], over_last, preferred_element_type=jnp.float32)
    result = result + jnp.dot(far, given[:, :wide], preferred_element_type=jnp.float32)
    out[0] = result.astype(jnp.bfloat16)


def attend(queries, cache_latents, cache_lens, handed, marks):
    requests, heads, lat = queries.shape
    cached = cache_latents.shape[1]
    return pl.pallas_call(
        attend_kernel,
        grid=(requests,),
        in_specs=[
            pl.BlockSpec(memory_space=pltpu.SMEM),
            pl.BlockSpec((1, lat, heads), lambda k: (k, 0, 0)),
            pl.BlockSpec((1, lat, cached), lambda k: (k, 0, 0)),
            pl.BlockSpec(handed.shape, lambda k: (0, 0)),
            pl.BlockSpec(marks.shape, lambda k: (0, 0)),
        ],
        out_specs=pl.BlockSpec((1, heads, VDIM), lambda k: (k, 0, 0)),
        out_shape=jax.ShapeDtypeStruct((requests, heads, VDIM), jnp.bfloat16),
        compiler_params=pltpu.CompilerParams(vmem_limit_bytes=VMEM_BYTES),
        cost_estimate=pl.CostEstimate(
            flops=2 * requests * heads * (cached + handed.shape[0]) * (lat + VDIM),
            bytes_accessed=2 * requests * (heads * (lat + VDIM) + cached * lat),
            transcendentals=requests * heads * (cached + handed.shape[0]),
        ),
    )(
        cache_lens,
        jnp.swapaxes(queries, 1, 2),
        jnp.swapaxes(cache_latents, 1, 2),
        handed,
        marks,
    )


def hand_over(prompt_latents, owners, requests):
    n_ep = lax.axis_size("ep")
    stretch, lat = prompt_latents.shape
    cap = 2 * stretch // n_ep
    places_at = jnp.arange(stretch, dtype=jnp.int32)
    earlier = (owners[:, None] == owners[None, :]) & (places_at[None, :] < places_at[:, None])
    target = owners * cap + jnp.sum(earlier.astype(jnp.int32), axis=1)
    slots = jnp.arange(n_ep * cap, dtype=jnp.int32)
    chosen = slots[:, None] == target[None, :]
    packed = jnp.dot(
        chosen.astype(jnp.bfloat16), prompt_latents, preferred_element_type=jnp.float32
    ).astype(jnp.bfloat16)
    mark = jnp.sum(jnp.where(chosen, requests[None, :] + 1, 0), axis=1).astype(jnp.bfloat16)
    fill = -(lat + 1) % 128
    outgoing = jnp.concatenate(
        [packed, mark[:, None], jnp.zeros((n_ep * cap, fill), jnp.bfloat16)], axis=1
    )
    return outgoing.reshape(n_ep, cap, lat + 1 + fill)


def on_device(
    moe_rows,
    routes,
    route_gates,
    gate_proj,
    up_proj,
    down_proj,
    queries,
    cache_latents,
    cache_lens,
    prompt_latents,
    kv_owner,
    kv_request,
):
    sections, count, width = moe_rows.shape
    top = routes.shape[2]
    expert_out, attended = layer(
        moe_rows.reshape(sections * count, width),
        routes.reshape(sections * count, top),
        route_gates.reshape(sections * count, top),
        prompt_latents,
        kv_owner[:, 0],
        kv_request,
        queries,
        cache_latents,
        cache_lens,
        gate_proj,
        up_proj,
        down_proj,
    )
    expert_out = expert_out.reshape(moe_rows.shape)
    return (expert_out, attended)


def solution(mesh):
    placed = (
        P("section", ("groups", "ep"), None),
        P("section", ("groups", "ep"), None),
        P("section", ("groups", "ep"), None),
        P(None, "ep"),
        P(None, "ep"),
        P("ep", None),
        P(("groups", "ep"), None, None),
        P(("groups", "ep"), None, None),
        P(("groups", "ep")),
        P(("groups", "ep"), None),
        P(("groups", "ep"), None),
        P(("groups", "ep")),
    )
    return jax.shard_map(
        on_device,
        mesh=mesh,
        in_specs=placed,
        out_specs=(P("section", ("groups", "ep"), None), P(("groups", "ep"), None, None)),
        check_vma=False,
    )
```

```python
from functools import partial

import jax
import jax.numpy as jnp
from jax import lax
from jax.experimental import pallas as pl
from jax.experimental.pallas import tpu as pltpu
from jax.sharding import PartitionSpec as P

VDIM = 512
FF_WIN = 1024
CORE, XBIT, YBIT = 1, 2, 4
VMEM_BYTES = 60 * 1024 * 1024
SMALL_BYTES = 14 * 1024 * 1024


score_scale = 0.07216878364870323


def swap(value, bit):
    count = lax.axis_size("ep")
    return lax.ppermute(value, "ep", [(i, i ^ bit) for i in range(count)])


def shift(value, step):
    count = lax.axis_size("ep")
    return lax.ppermute(value, "ep", [(i, (i + step) % count) for i in range(count)])


def cross(value, step):
    count = lax.axis_size("ep")
    pairs = [(i, (i + step) % count ^ YBIT) for i in range(count)]
    return lax.ppermute(value, "ep", pairs)


def together(*values):
    return lax.optimization_barrier(values)


def pair_dot(rows, left, right):
    both = jnp.concatenate([left[...], right[...]], axis=1)
    return jnp.dot(rows, both, preferred_element_type=jnp.float32)


def gated(gate, up):
    return (gate / (1.0 + jnp.exp(-gate)) * up).astype(jnp.bfloat16)


def pack_kernel(chosen, rows, *outs):
    picked = jnp.dot(chosen[...], rows[...], preferred_element_type=jnp.float32)
    picked = picked.astype(jnp.bfloat16)
    slots = outs[0].shape[0]
    for at, out in enumerate(outs):
        out[...] = picked[at * slots : (at + 1) * slots]


def packs(chosen, rows, planes, chunk):
    count, width = rows.shape
    slots = chosen.shape[0] // planes
    return pl.pallas_call(
        pack_kernel,
        grid=(width // chunk,),
        in_specs=[
            pl.BlockSpec(chosen.shape, lambda k: (0, 0)),
            pl.BlockSpec((count, chunk), lambda k: (0, k)),
        ],
        out_specs=[pl.BlockSpec((slots, chunk), lambda k: (0, k))] * planes,
        out_shape=[jax.ShapeDtypeStruct((slots, width), jnp.bfloat16)] * planes,
        compiler_params=pltpu.CompilerParams(vmem_limit_bytes=SMALL_BYTES),
        cost_estimate=pl.CostEstimate(
            flops=2 * chosen.size * width,
            bytes_accessed=2 * width * (count + planes * slots),
            transcendentals=0,
        ),
    )(chosen, rows)


def hidden_kernel(count, *refs):
    units, weights = refs[:count], refs[count : count + 8]
    gate_o, gate_c, gate_x, gate_xc, up_o, up_c, up_x, up_xc = weights
    out, near_gate, far_gate, near_up, far_up = refs[count + 8 :]
    step = pl.program_id(0)

    @pl.when(step == 0)
    def _():
        for total in (near_gate, far_gate, near_up, far_up):
            total[...] = jnp.zeros_like(total)

    rows = jnp.concatenate([unit[...] for unit in units], axis=0)
    near_gate[...] += pair_dot(rows, gate_o, gate_c)
    near_up[...] += pair_dot(rows, up_o, up_c)
    far_gate[...] += pair_dot(rows, gate_x, gate_xc)
    far_up[...] += pair_dot(rows, up_x, up_xc)

    @pl.when(step == pl.num_programs(0) - 1)
    def _():
        two = near_up.shape[1]
        out[:, :two] = gated(near_gate[...], near_up[...])
        out[:, two:] = gated(far_gate[...], far_up[...])


def hidden_units(units, weights, chunk):
    width, wide = weights[0].shape
    count = sum(unit.shape[0] for unit in units)
    return pl.pallas_call(
        partial(hidden_kernel, len(units)),
        grid=(width // chunk,),
        in_specs=[pl.BlockSpec((unit.shape[0], chunk), lambda k: (0, k)) for unit in units]
        + [pl.BlockSpec((chunk, wide), lambda k: (k, 0)) for _ in weights],
        out_specs=pl.BlockSpec((count, 4 * wide), lambda k: (0, 0)),
        out_shape=jax.ShapeDtypeStruct((count, 4 * wide), jnp.bfloat16),
        scratch_shapes=[pltpu.VMEM((count, 2 * wide), jnp.float32)] * 4,
        compiler_params=pltpu.CompilerParams(vmem_limit_bytes=VMEM_BYTES),
        cost_estimate=pl.CostEstimate(
            flops=2 * count * width * wide * 8,
            bytes_accessed=2 * width * (count + wide * 8),
            transcendentals=0,
        ),
    )(*units, *weights)


def down_kernel(mine, other, own, own_c, side_0, side_0c, side_1, side_1c, *outs):
    deep = own.shape[0] // 2
    count = mine.shape[0] // 2
    rows = 2 * count // len(outs)

    def fill(side, side_c):
        parts = (own, own_c, side, side_c)
        table = jnp.concatenate(
            [part[:deep, :] for part in parts] + [part[deep:, :] for part in parts], axis=0
        )
        joined = jnp.concatenate(
            [
                jnp.concatenate([mine[:count, :], other[count:, :]], axis=1),
                jnp.concatenate([mine[count:, :], other[:count, :]], axis=1),
            ],
            axis=0,
        )
        value = jnp.dot(joined, table, preferred_element_type=jnp.float32).astype(jnp.bfloat16)
        for at, out in enumerate(outs):
            out[...] = value[at * rows : (at + 1) * rows]

    first = pl.program_id(0) < pl.num_programs(0) // 2

    @pl.when(first)
    def _():
        fill(side_0, side_0c)

    @pl.when(jnp.logical_not(first))
    def _():
        fill(side_1, side_1c)


def down_values(mine, other, own, firsts, seconds, planes, chunk):
    count, inner = mine.shape
    deep, width = own[0].shape
    rows = count // (2 * planes)
    steps = width // chunk
    half = steps // 2
    return pl.pallas_call(
        down_kernel,
        grid=(steps,),
        in_specs=[pl.BlockSpec((count, inner), lambda k: (0, 0))] * 2
        + [pl.BlockSpec((deep, chunk), lambda k: (0, k)) for _ in own]
        + [pl.BlockSpec((deep, chunk), lambda k: (0, jnp.minimum(k, half - 1))) for _ in firsts]
        + [pl.BlockSpec((deep, chunk), lambda k: (0, jnp.maximum(k - half, 0))) for _ in seconds],
        out_specs=[pl.BlockSpec((rows, chunk), lambda k: (0, k))] * (2 * planes),
        out_shape=[jax.ShapeDtypeStruct((rows, width), jnp.bfloat16)] * (2 * planes),
        compiler_params=pltpu.CompilerParams(vmem_limit_bytes=SMALL_BYTES),
        cost_estimate=pl.CostEstimate(
            flops=2 * count * 2 * inner * width,
            bytes_accessed=8 * deep * width + 2 * count * width,
            transcendentals=0,
        ),
    )(mine, other, *own, *firsts, *seconds)


def combine_kernel(upper, high, low, *refs):
    parts, out = refs[:-1], refs[-1]
    planes = len(parts) // 2

    def mix(chosen):
        values = jnp.concatenate([part[...] for part in chosen], axis=0)
        total = jnp.dot(high[...], values, preferred_element_type=jnp.float32)
        total = total + jnp.dot(low[...], values, preferred_element_type=jnp.float32)
        out[...] = total.astype(jnp.bfloat16)

    side = pl.program_id(0)

    @pl.when(side == 0)
    def _():
        mix(parts[:planes])

    @pl.when(side == 1)
    def _():
        mix(parts[planes:])


def combine(upper, high, low, mine, theirs, chunk):
    rows, width = mine[0].shape
    count = high.shape[0]
    steps = width // chunk

    def own_block(g, k, upper):
        return 0, jnp.where(g == 0, k, steps - 1)

    def other_block(g, k, upper):
        return 0, jnp.where(g == 0, 0, k)

    def out_block(g, k, upper):
        return 0, (upper[0] + g) % 2 * steps + k

    return pl.pallas_call(
        combine_kernel,
        grid_spec=pltpu.PrefetchScalarGridSpec(
            num_scalar_prefetch=1,
            grid=(2, steps),
            in_specs=[pl.BlockSpec(high.shape, lambda g, k, upper: (0, 0))] * 2
            + [pl.BlockSpec((rows, chunk), own_block) for _ in mine]
            + [pl.BlockSpec((rows, chunk), other_block) for _ in theirs],
            out_specs=pl.BlockSpec((count, chunk), out_block),
        ),
        out_shape=jax.ShapeDtypeStruct((count, 2 * width), jnp.bfloat16),
        compiler_params=pltpu.CompilerParams(vmem_limit_bytes=SMALL_BYTES),
        cost_estimate=pl.CostEstimate(
            flops=8 * high.size * width,
            bytes_accessed=4 * width * (len(mine) * rows + count),
            transcendentals=0,
        ),
    )(upper.reshape(1), high, low, *mine, *theirs)


def places(picks, planes, split):
    count = picks.shape[0]
    plane = lax.axis_index("ep") // split
    experts = (plane + jnp.arange(planes, dtype=jnp.int32)) % planes
    named = jnp.any(picks[None] == experts[:, None, None], axis=2)
    order = jnp.arange(count, dtype=jnp.int32)
    before = order[:, None] < order[None, :]
    rank = jnp.sum((named[:, :, None] & before[None]).astype(jnp.int32), axis=1)
    return experts, named, rank


def gate_table(picks, gates, planes, split, slots):
    experts, named, rank = places(picks, planes, split)
    weight = jnp.sum(
        jnp.where(picks[None] == experts[:, None, None], gates[None], jnp.zeros_like(gates)[None]),
        axis=2,
    )
    at = jnp.arange(slots, dtype=jnp.int32)
    found = (rank.T[:, :, None] == at[None, None, :]) & named.T[:, :, None]
    return jnp.where(found, weight.T[:, :, None], 0.0)


def layer(
    rows,
    picks,
    gates,
    latents,
    owners,
    requests,
    queries,
    cache_latents,
    cache_lens,
    gate_proj,
    up_proj,
    down_proj,
):
    n_ep = lax.axis_size("ep")
    split = FF_WIN // gate_proj.shape[1]
    planes = n_ep // split
    count, width = rows.shape
    slots = -(-3 * count * picks.shape[1] // (2 * planes * 16)) * 16
    chunk = width // 4
    upper = lax.axis_index("ep") // YBIT % 2
    span = width // 4

    gate_x = swap(gate_proj, XBIT)
    _, named, rank = places(picks, planes, split)
    at = jnp.arange(slots, dtype=jnp.int32)
    chosen = (rank[:, None, :] == at[None, :, None]) & named[:, None, :]
    chosen = chosen.astype(jnp.bfloat16)

    pack_0, out_1, out_2, out_3 = packs(
        chosen.reshape(planes * slots, count), rows, planes, span
    )
    pack_0, out_1, out_3, latents, owners, requests, down_proj = together(
        pack_0, out_1, out_3, latents, owners, requests, down_proj
    )
    own_1, own_3, peer_0 = shift(out_1, split), shift(out_3, 3 * split), swap(pack_0, YBIT)
    send = lax.dynamic_slice_in_dim(down_proj, (2 - 2 * upper) * span, 2 * span, 1)
    down_y = swap(send, YBIT)
    outgoing = hand_over(latents, owners, requests)

    own_1, own_3, peer_0, down_y, gate_x, out_2, outgoing, down_proj, gate_proj = together(
        own_1, own_3, peer_0, down_y, gate_x, out_2, outgoing, down_proj, gate_proj
    )
    own_2, peer_1, peer_3 = shift(out_2, 2 * split), swap(own_1, YBIT), swap(own_3, YBIT)
    up_x, gate_c = swap(up_proj, XBIT), swap(gate_proj, CORE)
    keep = lax.dynamic_slice_in_dim(down_proj, 2 * upper * span, 2 * span, 1)
    own = jnp.concatenate([keep, down_y], axis=0)
    begin, rest = own[:, :span], own[:, span:]

    own_2, peer_1, peer_3, up_x, gate_x, gate_c, up_proj, own, begin, rest = together(
        own_2, peer_1, peer_3, up_x, gate_x, gate_c, up_proj, own, begin, rest
    )
    peer_2, side_0 = swap(own_2, YBIT), swap(begin, XBIT)
    up_c, gate_xc, up_xc = swap(up_proj, CORE), swap(gate_x, CORE), swap(up_x, CORE)
    peer_2, up_c, gate_xc, up_xc, side_0, rest, own, picks, gates = together(
        peer_2, up_c, gate_xc, up_xc, side_0, rest, own, picks, gates
    )
    own_c, side_0c, side_1 = swap(own, CORE), swap(side_0, CORE), swap(rest, XBIT)
    units = (pack_0, own_1, own_2, own_3, peer_0, peer_1, peer_2, peer_3)
    weights = (gate_proj, gate_c, gate_x, gate_xc, up_proj, up_c, up_x, up_xc)
    hidden = hidden_units(units, weights, chunk)
    hidden, own_c, side_0c, picks, gates = together(hidden, own_c, side_0c, picks, gates)
    table = gate_table(picks, gates, planes, split, slots).reshape(count, planes * slots)
    high = lax.reduce_precision(table, 8, 7)
    high, low = high.astype(jnp.bfloat16), (table - high).astype(jnp.bfloat16)
    other, side_1, high, low, outgoing = together(
        swap(hidden, YBIT), side_1, high, low, outgoing
    )
    firsts, seconds = (side_0, side_0c), (side_1, swap(side_1, CORE))
    values = down_values(hidden, other, (own, own_c), firsts, seconds, planes, span // 2)
    mine, theirs = list(values[:planes]), list(values[planes:])
    theirs[0] = swap(theirs[0], YBIT)
    mine[1] = shift(mine[1], n_ep - split)
    mine[2], theirs[2] = shift(mine[2], n_ep - 2 * split), cross(theirs[2], n_ep - 2 * split)
    theirs[3] = cross(theirs[3], n_ep - 3 * split)
    theirs[1] = cross(theirs[1], n_ep - split)
    mine[3] = shift(mine[3], n_ep - 3 * split)
    incoming = lax.all_to_all(outgoing, "ep", split_axis=0, concat_axis=0, tiled=True)
    theirs[0], incoming = together(theirs[0], incoming)
    handed = incoming.reshape(-1, incoming.shape[2])
    marks = handed[:, latents.shape[1]].astype(jnp.float32)[None, :]
    attended = attend(queries, cache_latents, cache_lens, handed, marks)
    mine[1], mine[2], theirs[2], theirs[3], theirs[1], mine[3], attended = together(
        mine[1], mine[2], theirs[2], theirs[3], theirs[1], mine[3], attended
    )
    return combine(upper, high, low, mine, theirs, span), attended


def attend_kernel(lens, query, cache, handed, marks, out):
    request = pl.program_id(0)
    heads = query.shape[2]
    wide = out.shape[2]
    lat = query.shape[1]
    asked = query[0].astype(jnp.float32).T.astype(jnp.bfloat16)
    given = handed[:, :lat]
    near = jnp.dot(asked, cache[0], preferred_element_type=jnp.float32) * score_scale
    over_last = (((1,), (1,)), ((), ()))
    far = lax.dot_general(asked, given, over_last, preferred_element_type=jnp.float32)
    far = far * score_scale
    place = lax.broadcasted_iota(jnp.int32, (heads, near.shape[1]), 1)
    near = jnp.where(place < lens[request], near, -jnp.inf)
    mark = (request + 1).astype(jnp.float32)
    far = jnp.where(jnp.broadcast_to(marks[...], far.shape) == mark, far, -jnp.inf)
    top = jnp.maximum(
        jnp.max(near, axis=1, keepdims=True), jnp.max(far, axis=1, keepdims=True)
    )
    near, far = jnp.exp(near - top), jnp.exp(far - top)
    total = jnp.sum(near, axis=1, keepdims=True) + jnp.sum(far, axis=1, keepdims=True)
    near, far = (near / total).astype(jnp.bfloat16), (far / total).astype(jnp.bfloat16)
    result = lax.dot_general(near, cache[0, :wide], over_last, preferred_element_type=jnp.float32)
    result = result + jnp.dot(far, given[:, :wide], preferred_element_type=jnp.float32)
    out[0] = result.astype(jnp.bfloat16)


def attend(queries, cache_latents, cache_lens, handed, marks):
    requests, heads, lat = queries.shape
    cached = cache_latents.shape[1]
    return pl.pallas_call(
        attend_kernel,
        grid=(requests,),
        in_specs=[
            pl.BlockSpec(memory_space=pltpu.SMEM),
            pl.BlockSpec((1, lat, heads), lambda k: (k, 0, 0)),
            pl.BlockSpec((1, lat, cached), lambda k: (k, 0, 0)),
            pl.BlockSpec(handed.shape, lambda k: (0, 0)),
            pl.BlockSpec(marks.shape, lambda k: (0, 0)),
        ],
        out_specs=pl.BlockSpec((1, heads, VDIM), lambda k: (k, 0, 0)),
        out_shape=jax.ShapeDtypeStruct((requests, heads, VDIM), jnp.bfloat16),
        compiler_params=pltpu.CompilerParams(vmem_limit_bytes=VMEM_BYTES),
        cost_estimate=pl.CostEstimate(
            flops=2 * requests * heads * (cached + handed.shape[0]) * (lat + VDIM),
            bytes_accessed=2 * requests * (heads * (lat + VDIM) + cached * lat),
            transcendentals=requests * heads * (cached + handed.shape[0]),
        ),
    )(
        cache_lens,
        jnp.swapaxes(queries, 1, 2),
        jnp.swapaxes(cache_latents, 1, 2),
        handed,
        marks,
    )


def hand_over(prompt_latents, owners, requests):
    n_ep = lax.axis_size("ep")
    stretch, lat = prompt_latents.shape
    cap = 2 * stretch // n_ep
    places_at = jnp.arange(stretch, dtype=jnp.int32)
    earlier = (owners[:, None] == owners[None, :]) & (places_at[None, :] < places_at[:, None])
    target = owners * cap + jnp.sum(earlier.astype(jnp.int32), axis=1)
    slots = jnp.arange(n_ep * cap, dtype=jnp.int32)
    chosen = slots[:, None] == target[None, :]
    packed = jnp.dot(
        chosen.astype(jnp.bfloat16), prompt_latents, preferred_element_type=jnp.float32
    ).astype(jnp.bfloat16)
    mark = jnp.sum(jnp.where(chosen, requests[None, :] + 1, 0), axis=1).astype(jnp.bfloat16)
    fill = -(lat + 1) % 128
    outgoing = jnp.concatenate(
        [packed, mark[:, None], jnp.zeros((n_ep * cap, fill), jnp.bfloat16)], axis=1
    )
    return outgoing.reshape(n_ep, cap, lat + 1 + fill)


def on_device(
    moe_rows,
    routes,
    route_gates,
    gate_proj,
    up_proj,
    down_proj,
    queries,
    cache_latents,
    cache_lens,
    prompt_latents,
    kv_owner,
    kv_request,
):
    sections, count, width = moe_rows.shape
    top = routes.shape[2]
    expert_out, attended = layer(
        moe_rows.reshape(sections * count, width),
        routes.reshape(sections * count, top),
        route_gates.reshape(sections * count, top),
        prompt_latents,
        kv_owner[:, 0],
        kv_request,
        queries,
        cache_latents,
        cache_lens,
        gate_proj,
        up_proj,
        down_proj,
    )
    expert_out = expert_out.reshape(moe_rows.shape)
    return (expert_out, attended)


def solution(mesh):
    placed = (
        P("section", ("groups", "ep"), None),
        P("section", ("groups", "ep"), None),
        P("section", ("groups", "ep"), None),
        P(None, "ep"),
        P(None, "ep"),
        P("ep", None),
        P(("groups", "ep"), None, None),
        P(("groups", "ep"), None, None),
        P(("groups", "ep")),
        P(("groups", "ep"), None),
        P(("groups", "ep"), None),
        P(("groups", "ep")),
    )
    return jax.shard_map(
        on_device,
        mesh=mesh,
        in_specs=placed,
        out_specs=(P("section", ("groups", "ep"), None), P(("groups", "ep"), None, None)),
        check_vma=False,
    )
```

```python
from functools import partial

import jax
import jax.numpy as jnp
from jax import lax
from jax.experimental import pallas as pl
from jax.experimental.pallas import tpu as pltpu
from jax.sharding import PartitionSpec as P

VDIM = 512
FF_WIN = 1024
CORE, XBIT, YBIT = 1, 2, 4
VMEM_BYTES = 60 * 1024 * 1024
SMALL_BYTES = 14 * 1024 * 1024


score_scale = 0.07216878364870323


def swap(value, bit):
    count = lax.axis_size("ep")
    return lax.ppermute(value, "ep", [(i, i ^ bit) for i in range(count)])


def shift(value, step):
    count = lax.axis_size("ep")
    return lax.ppermute(value, "ep", [(i, (i + step) % count) for i in range(count)])


def cross(value, step):
    count = lax.axis_size("ep")
    pairs = [(i, (i + step) % count ^ YBIT) for i in range(count)]
    return lax.ppermute(value, "ep", pairs)


def together(*values):
    return lax.optimization_barrier(values)


def pair_dot(rows, left, right):
    both = jnp.concatenate([left[...], right[...]], axis=1)
    return jnp.dot(rows, both, preferred_element_type=jnp.float32)


def gated(gate, up):
    return (gate / (1.0 + jnp.exp(-gate)) * up).astype(jnp.bfloat16)


def pack_kernel(chosen, rows, *outs):
    picked = jnp.dot(chosen[...], rows[...], preferred_element_type=jnp.float32)
    picked = picked.astype(jnp.bfloat16)
    slots = outs[0].shape[0]
    for at, out in enumerate(outs):
        out[...] = picked[at * slots : (at + 1) * slots]


def packs(chosen, rows, planes, chunk):
    count, width = rows.shape
    slots = chosen.shape[0] // planes
    return pl.pallas_call(
        pack_kernel,
        grid=(width // chunk,),
        in_specs=[
            pl.BlockSpec(chosen.shape, lambda k: (0, 0)),
            pl.BlockSpec((count, chunk), lambda k: (0, k)),
        ],
        out_specs=[pl.BlockSpec((slots, chunk), lambda k: (0, k))] * planes,
        out_shape=[jax.ShapeDtypeStruct((slots, width), jnp.bfloat16)] * planes,
        compiler_params=pltpu.CompilerParams(vmem_limit_bytes=SMALL_BYTES),
        cost_estimate=pl.CostEstimate(
            flops=2 * chosen.size * width,
            bytes_accessed=2 * width * (count + planes * slots),
            transcendentals=0,
        ),
    )(chosen, rows)


def hidden_kernel(count, *refs):
    units, weights = refs[:count], refs[count : count + 8]
    gate_o, gate_c, gate_x, gate_xc, up_o, up_c, up_x, up_xc = weights
    out, near_gate, far_gate, near_up, far_up = refs[count + 8 :]
    step = pl.program_id(0)

    @pl.when(step == 0)
    def _():
        for total in (near_gate, far_gate, near_up, far_up):
            total[...] = jnp.zeros_like(total)

    rows = jnp.concatenate([unit[...] for unit in units], axis=0)
    near_gate[...] += pair_dot(rows, gate_o, gate_c)
    near_up[...] += pair_dot(rows, up_o, up_c)
    far_gate[...] += pair_dot(rows, gate_x, gate_xc)
    far_up[...] += pair_dot(rows, up_x, up_xc)

    @pl.when(step == pl.num_programs(0) - 1)
    def _():
        two = near_up.shape[1]
        out[:, :two] = gated(near_gate[...], near_up[...])
        out[:, two:] = gated(far_gate[...], far_up[...])


def hidden_units(units, weights, chunk):
    width, wide = weights[0].shape
    count = sum(unit.shape[0] for unit in units)
    return pl.pallas_call(
        partial(hidden_kernel, len(units)),
        grid=(width // chunk,),
        in_specs=[pl.BlockSpec((unit.shape[0], chunk), lambda k: (0, k)) for unit in units]
        + [pl.BlockSpec((chunk, wide), lambda k: (k, 0)) for _ in weights],
        out_specs=pl.BlockSpec((count, 4 * wide), lambda k: (0, 0)),
        out_shape=jax.ShapeDtypeStruct((count, 4 * wide), jnp.bfloat16),
        scratch_shapes=[pltpu.VMEM((count, 2 * wide), jnp.float32)] * 4,
        compiler_params=pltpu.CompilerParams(vmem_limit_bytes=VMEM_BYTES),
        cost_estimate=pl.CostEstimate(
            flops=2 * count * width * wide * 8,
            bytes_accessed=2 * width * (count + wide * 8),
            transcendentals=0,
        ),
    )(*units, *weights)


def down_kernel(mine, other, own, own_c, side_0, side_0c, side_1, side_1c, *outs):
    deep = own.shape[0] // 2
    count = mine.shape[0] // 2
    rows = 2 * count // len(outs)

    def fill(side, side_c):
        parts = (own, own_c, side, side_c)
        table = jnp.concatenate(
            [part[:deep, :] for part in parts] + [part[deep:, :] for part in parts], axis=0
        )
        joined = jnp.concatenate(
            [
                jnp.concatenate([mine[:count, :], other[count:, :]], axis=1),
                jnp.concatenate([mine[count:, :], other[:count, :]], axis=1),
            ],
            axis=0,
        )
        value = jnp.dot(joined, table, preferred_element_type=jnp.float32).astype(jnp.bfloat16)
        for at, out in enumerate(outs):
            out[...] = value[at * rows : (at + 1) * rows]

    first = pl.program_id(0) < pl.num_programs(0) // 2

    @pl.when(first)
    def _():
        fill(side_0, side_0c)

    @pl.when(jnp.logical_not(first))
    def _():
        fill(side_1, side_1c)


def down_values(mine, other, own, firsts, seconds, planes, chunk):
    count, inner = mine.shape
    deep, width = own[0].shape
    rows = count // (2 * planes)
    steps = width // chunk
    half = steps // 2
    return pl.pallas_call(
        down_kernel,
        grid=(steps,),
        in_specs=[pl.BlockSpec((count, inner), lambda k: (0, 0))] * 2
        + [pl.BlockSpec((deep, chunk), lambda k: (0, k)) for _ in own]
        + [pl.BlockSpec((deep, chunk), lambda k: (0, jnp.minimum(k, half - 1))) for _ in firsts]
        + [pl.BlockSpec((deep, chunk), lambda k: (0, jnp.maximum(k - half, 0))) for _ in seconds],
        out_specs=[pl.BlockSpec((rows, chunk), lambda k: (0, k))] * (2 * planes),
        out_shape=[jax.ShapeDtypeStruct((rows, width), jnp.bfloat16)] * (2 * planes),
        compiler_params=pltpu.CompilerParams(vmem_limit_bytes=VMEM_BYTES),
        cost_estimate=pl.CostEstimate(
            flops=2 * count * 2 * inner * width,
            bytes_accessed=8 * deep * width + 2 * count * width,
            transcendentals=0,
        ),
    )(mine, other, *own, *firsts, *seconds)


def combine_kernel(upper, high, low, *refs):
    parts, out = refs[:-1], refs[-1]
    planes = len(parts) // 2

    def mix(chosen):
        values = jnp.concatenate([part[...] for part in chosen], axis=0)
        total = jnp.dot(high[...], values, preferred_element_type=jnp.float32)
        total = total + jnp.dot(low[...], values, preferred_element_type=jnp.float32)
        out[...] = total.astype(jnp.bfloat16)

    side = pl.program_id(0)

    @pl.when(side == 0)
    def _():
        mix(parts[:planes])

    @pl.when(side == 1)
    def _():
        mix(parts[planes:])


def combine(upper, high, low, mine, theirs, chunk):
    rows, width = mine[0].shape
    count = high.shape[0]
    steps = width // chunk

    def own_block(g, k, upper):
        return 0, jnp.where(g == 0, k, steps - 1)

    def other_block(g, k, upper):
        return 0, jnp.where(g == 0, 0, k)

    def out_block(g, k, upper):
        return 0, (upper[0] + g) % 2 * steps + k

    return pl.pallas_call(
        combine_kernel,
        grid_spec=pltpu.PrefetchScalarGridSpec(
            num_scalar_prefetch=1,
            grid=(2, steps),
            in_specs=[pl.BlockSpec(high.shape, lambda g, k, upper: (0, 0))] * 2
            + [pl.BlockSpec((rows, chunk), own_block) for _ in mine]
            + [pl.BlockSpec((rows, chunk), other_block) for _ in theirs],
            out_specs=pl.BlockSpec((count, chunk), out_block),
        ),
        out_shape=jax.ShapeDtypeStruct((count, 2 * width), jnp.bfloat16),
        compiler_params=pltpu.CompilerParams(vmem_limit_bytes=SMALL_BYTES),
        cost_estimate=pl.CostEstimate(
            flops=8 * high.size * width,
            bytes_accessed=4 * width * (len(mine) * rows + count),
            transcendentals=0,
        ),
    )(upper.reshape(1), high, low, *mine, *theirs)


def places(picks, planes, split):
    count = picks.shape[0]
    plane = lax.axis_index("ep") // split
    experts = (plane + jnp.arange(planes, dtype=jnp.int32)) % planes
    named = jnp.any(picks[None] == experts[:, None, None], axis=2)
    order = jnp.arange(count, dtype=jnp.int32)
    before = order[:, None] < order[None, :]
    rank = jnp.sum((named[:, :, None] & before[None]).astype(jnp.int32), axis=1)
    return experts, named, rank


def gate_table(picks, gates, planes, split, slots):
    experts, named, rank = places(picks, planes, split)
    weight = jnp.sum(
        jnp.where(picks[None] == experts[:, None, None], gates[None], jnp.zeros_like(gates)[None]),
        axis=2,
    )
    at = jnp.arange(slots, dtype=jnp.int32)
    found = (rank.T[:, :, None] == at[None, None, :]) & named.T[:, :, None]
    return jnp.where(found, weight.T[:, :, None], 0.0)


def layer(
    rows,
    picks,
    gates,
    latents,
    owners,
    requests,
    queries,
    cache_latents,
    cache_lens,
    gate_proj,
    up_proj,
    down_proj,
):
    n_ep = lax.axis_size("ep")
    split = FF_WIN // gate_proj.shape[1]
    planes = n_ep // split
    count, width = rows.shape
    slots = -(-3 * count * picks.shape[1] // (2 * planes * 16)) * 16
    chunk = width // 4
    upper = lax.axis_index("ep") // YBIT % 2
    span = width // 4

    gate_x = swap(gate_proj, XBIT)
    _, named, rank = places(picks, planes, split)
    at = jnp.arange(slots, dtype=jnp.int32)
    chosen = (rank[:, None, :] == at[None, :, None]) & named[:, None, :]
    chosen = chosen.astype(jnp.bfloat16)

    pack_0, out_1, out_2, out_3 = packs(
        chosen.reshape(planes * slots, count), rows, planes, span
    )
    pack_0, out_1, out_3, latents, owners, requests, down_proj = together(
        pack_0, out_1, out_3, latents, owners, requests, down_proj
    )
    own_1, own_3, peer_0 = shift(out_1, split), shift(out_3, 3 * split), swap(pack_0, YBIT)
    send = lax.dynamic_slice_in_dim(down_proj, (2 - 2 * upper) * span, 2 * span, 1)
    down_y = swap(send, YBIT)
    outgoing = hand_over(latents, owners, requests)

    own_1, own_3, peer_0, down_y, gate_x, out_2, outgoing, down_proj, gate_proj = together(
        own_1, own_3, peer_0, down_y, gate_x, out_2, outgoing, down_proj, gate_proj
    )
    own_2, peer_1, peer_3 = shift(out_2, 2 * split), swap(own_1, YBIT), swap(own_3, YBIT)
    up_x, gate_c = swap(up_proj, XBIT), swap(gate_proj, CORE)
    keep = lax.dynamic_slice_in_dim(down_proj, 2 * upper * span, 2 * span, 1)
    own = jnp.concatenate([keep, down_y], axis=0)
    begin, rest = own[:, :span], own[:, span:]

    own_2, peer_1, peer_3, up_x, gate_x, gate_c, up_proj, own, begin, rest = together(
        own_2, peer_1, peer_3, up_x, gate_x, gate_c, up_proj, own, begin, rest
    )
    peer_2, side_0 = swap(own_2, YBIT), swap(begin, XBIT)
    up_c, gate_xc, up_xc = swap(up_proj, CORE), swap(gate_x, CORE), swap(up_x, CORE)
    peer_2, up_c, gate_xc, up_xc, side_0, rest, own, picks, gates = together(
        peer_2, up_c, gate_xc, up_xc, side_0, rest, own, picks, gates
    )
    own_c, side_0c, side_1 = swap(own, CORE), swap(side_0, CORE), swap(rest, XBIT)
    units = (pack_0, own_1, own_2, own_3, peer_0, peer_1, peer_2, peer_3)
    weights = (gate_proj, gate_c, gate_x, gate_xc, up_proj, up_c, up_x, up_xc)
    hidden = hidden_units(units, weights, chunk)
    hidden, own_c, side_0c, picks, gates, outgoing = together(
        hidden, own_c, side_0c, picks, gates, outgoing
    )
    table = gate_table(picks, gates, planes, split, slots).reshape(count, planes * slots)
    high = lax.reduce_precision(table, 8, 7)
    high, low = high.astype(jnp.bfloat16), (table - high).astype(jnp.bfloat16)
    other, side_1, high, low = together(swap(hidden, YBIT), side_1, high, low)
    firsts, seconds = (side_0, side_0c), (side_1, swap(side_1, CORE))
    values = down_values(hidden, other, (own, own_c), firsts, seconds, planes, span // 2)
    mine, theirs = list(values[:planes]), list(values[planes:])
    theirs[0] = swap(theirs[0], YBIT)
    mine[1] = shift(mine[1], n_ep - split)
    mine[2], theirs[2] = shift(mine[2], n_ep - 2 * split), cross(theirs[2], n_ep - 2 * split)
    theirs[3] = cross(theirs[3], n_ep - 3 * split)
    theirs[1] = cross(theirs[1], n_ep - split)
    mine[3] = shift(mine[3], n_ep - 3 * split)
    incoming = lax.all_to_all(outgoing, "ep", split_axis=0, concat_axis=0, tiled=True)
    theirs[0], incoming = together(theirs[0], incoming)
    handed = incoming.reshape(-1, incoming.shape[2])
    marks = handed[:, latents.shape[1]].astype(jnp.float32)[None, :]
    attended = attend(queries, cache_latents, cache_lens, handed, marks)
    mine[3], attended = together(mine[3], attended)
    return combine(upper, high, low, mine, theirs, span), attended


def attend_kernel(lens, query, cache, handed, marks, out):
    request = pl.program_id(0)
    heads = query.shape[2]
    wide = out.shape[2]
    lat = query.shape[1]
    asked = query[0].astype(jnp.float32).T.astype(jnp.bfloat16)
    given = handed[:, :lat]
    near = jnp.dot(asked, cache[0], preferred_element_type=jnp.float32) * score_scale
    over_last = (((1,), (1,)), ((), ()))
    far = lax.dot_general(asked, given, over_last, preferred_element_type=jnp.float32)
    far = far * score_scale
    place = lax.broadcasted_iota(jnp.int32, (heads, near.shape[1]), 1)
    near = jnp.where(place < lens[request], near, -jnp.inf)
    mark = (request + 1).astype(jnp.float32)
    far = jnp.where(jnp.broadcast_to(marks[...], far.shape) == mark, far, -jnp.inf)
    top = jnp.maximum(
        jnp.max(near, axis=1, keepdims=True), jnp.max(far, axis=1, keepdims=True)
    )
    near, far = jnp.exp(near - top), jnp.exp(far - top)
    total = jnp.sum(near, axis=1, keepdims=True) + jnp.sum(far, axis=1, keepdims=True)
    near, far = (near / total).astype(jnp.bfloat16), (far / total).astype(jnp.bfloat16)
    result = lax.dot_general(near, cache[0, :wide], over_last, preferred_element_type=jnp.float32)
    result = result + jnp.dot(far, given[:, :wide], preferred_element_type=jnp.float32)
    out[0] = result.astype(jnp.bfloat16)


def attend(queries, cache_latents, cache_lens, handed, marks):
    requests, heads, lat = queries.shape
    cached = cache_latents.shape[1]
    return pl.pallas_call(
        attend_kernel,
        grid=(requests,),
        in_specs=[
            pl.BlockSpec(memory_space=pltpu.SMEM),
            pl.BlockSpec((1, lat, heads), lambda k: (k, 0, 0)),
            pl.BlockSpec((1, lat, cached), lambda k: (k, 0, 0)),
            pl.BlockSpec(handed.shape, lambda k: (0, 0)),
            pl.BlockSpec(marks.shape, lambda k: (0, 0)),
        ],
        out_specs=pl.BlockSpec((1, heads, VDIM), lambda k: (k, 0, 0)),
        out_shape=jax.ShapeDtypeStruct((requests, heads, VDIM), jnp.bfloat16),
        compiler_params=pltpu.CompilerParams(vmem_limit_bytes=VMEM_BYTES),
        cost_estimate=pl.CostEstimate(
            flops=2 * requests * heads * (cached + handed.shape[0]) * (lat + VDIM),
            bytes_accessed=2 * requests * (heads * (lat + VDIM) + cached * lat),
            transcendentals=requests * heads * (cached + handed.shape[0]),
        ),
    )(
        cache_lens,
        jnp.swapaxes(queries, 1, 2),
        jnp.swapaxes(cache_latents, 1, 2),
        handed,
        marks,
    )


def hand_over(prompt_latents, owners, requests):
    n_ep = lax.axis_size("ep")
    stretch, lat = prompt_latents.shape
    cap = 2 * stretch // n_ep
    places_at = jnp.arange(stretch, dtype=jnp.int32)
    earlier = (owners[:, None] == owners[None, :]) & (places_at[None, :] < places_at[:, None])
    target = owners * cap + jnp.sum(earlier.astype(jnp.int32), axis=1)
    slots = jnp.arange(n_ep * cap, dtype=jnp.int32)
    chosen = slots[:, None] == target[None, :]
    packed = jnp.dot(
        chosen.astype(jnp.bfloat16), prompt_latents, preferred_element_type=jnp.float32
    ).astype(jnp.bfloat16)
    mark = jnp.sum(jnp.where(chosen, requests[None, :] + 1, 0), axis=1).astype(jnp.bfloat16)
    fill = -(lat + 1) % 128
    outgoing = jnp.concatenate(
        [packed, mark[:, None], jnp.zeros((n_ep * cap, fill), jnp.bfloat16)], axis=1
    )
    return outgoing.reshape(n_ep, cap, lat + 1 + fill)


def on_device(
    moe_rows,
    routes,
    route_gates,
    gate_proj,
    up_proj,
    down_proj,
    queries,
    cache_latents,
    cache_lens,
    prompt_latents,
    kv_owner,
    kv_request,
):
    sections, count, width = moe_rows.shape
    top = routes.shape[2]
    expert_out, attended = layer(
        moe_rows.reshape(sections * count, width),
        routes.reshape(sections * count, top),
        route_gates.reshape(sections * count, top),
        prompt_latents,
        kv_owner[:, 0],
        kv_request,
        queries,
        cache_latents,
        cache_lens,
        gate_proj,
        up_proj,
        down_proj,
    )
    expert_out = expert_out.reshape(moe_rows.shape)
    return (expert_out, attended)


def solution(mesh):
    placed = (
        P("section", ("groups", "ep"), None),
        P("section", ("groups", "ep"), None),
        P("section", ("groups", "ep"), None),
        P(None, "ep"),
        P(None, "ep"),
        P("ep", None),
        P(("groups", "ep"), None, None),
        P(("groups", "ep"), None, None),
        P(("groups", "ep")),
        P(("groups", "ep"), None),
        P(("groups", "ep"), None),
        P(("groups", "ep")),
    )
    return jax.shard_map(
        on_device,
        mesh=mesh,
        in_specs=placed,
        out_specs=(P("section", ("groups", "ep"), None), P(("groups", "ep"), None, None)),
        check_vma=False,
    )
```

```python
from functools import partial

import jax
import jax.numpy as jnp
from jax import lax
from jax.experimental import pallas as pl
from jax.experimental.pallas import tpu as pltpu
from jax.sharding import PartitionSpec as P

VDIM = 512
FF_WIN = 1024
CORE, XBIT, YBIT = 1, 2, 4
VMEM_BYTES = 60 * 1024 * 1024
SMALL_BYTES = 14 * 1024 * 1024


score_scale = 0.07216878364870323


def swap(value, bit):
    count = lax.axis_size("ep")
    return lax.ppermute(value, "ep", [(i, i ^ bit) for i in range(count)])


def shift(value, step):
    count = lax.axis_size("ep")
    return lax.ppermute(value, "ep", [(i, (i + step) % count) for i in range(count)])


def cross(value, step):
    count = lax.axis_size("ep")
    pairs = [(i, (i + step) % count ^ YBIT) for i in range(count)]
    return lax.ppermute(value, "ep", pairs)


def together(*values):
    return lax.optimization_barrier(values)


def pair_dot(rows, left, right):
    both = jnp.concatenate([left[...], right[...]], axis=1)
    return jnp.dot(rows, both, preferred_element_type=jnp.float32)


def gated(gate, up):
    return (gate / (1.0 + jnp.exp(-gate)) * up).astype(jnp.bfloat16)


def pack_kernel(chosen, rows, *outs):
    picked = jnp.dot(chosen[...], rows[...], preferred_element_type=jnp.float32)
    picked = picked.astype(jnp.bfloat16)
    slots = outs[0].shape[0]
    for at, out in enumerate(outs):
        out[...] = picked[at * slots : (at + 1) * slots]


def packs(chosen, rows, planes, chunk):
    count, width = rows.shape
    slots = chosen.shape[0] // planes
    return pl.pallas_call(
        pack_kernel,
        grid=(width // chunk,),
        in_specs=[
            pl.BlockSpec(chosen.shape, lambda k: (0, 0)),
            pl.BlockSpec((count, chunk), lambda k: (0, k)),
        ],
        out_specs=[pl.BlockSpec((slots, chunk), lambda k: (0, k))] * planes,
        out_shape=[jax.ShapeDtypeStruct((slots, width), jnp.bfloat16)] * planes,
        compiler_params=pltpu.CompilerParams(vmem_limit_bytes=SMALL_BYTES),
        cost_estimate=pl.CostEstimate(
            flops=2 * chosen.size * width,
            bytes_accessed=2 * width * (count + planes * slots),
            transcendentals=0,
        ),
    )(chosen, rows)


def hidden_kernel(count, *refs):
    units, weights = refs[:count], refs[count : count + 8]
    gate_o, gate_c, gate_x, gate_xc, up_o, up_c, up_x, up_xc = weights
    out, near_gate, far_gate, near_up, far_up = refs[count + 8 :]
    step = pl.program_id(0)

    @pl.when(step == 0)
    def _():
        for total in (near_gate, far_gate, near_up, far_up):
            total[...] = jnp.zeros_like(total)

    rows = jnp.concatenate([unit[...] for unit in units], axis=0)
    near_gate[...] += pair_dot(rows, gate_o, gate_c)
    near_up[...] += pair_dot(rows, up_o, up_c)
    far_gate[...] += pair_dot(rows, gate_x, gate_xc)
    far_up[...] += pair_dot(rows, up_x, up_xc)

    @pl.when(step == pl.num_programs(0) - 1)
    def _():
        two = near_up.shape[1]
        out[:, :two] = gated(near_gate[...], near_up[...])
        out[:, two:] = gated(far_gate[...], far_up[...])


def hidden_units(units, weights, chunk):
    width, wide = weights[0].shape
    count = sum(unit.shape[0] for unit in units)
    return pl.pallas_call(
        partial(hidden_kernel, len(units)),
        grid=(width // chunk,),
        in_specs=[pl.BlockSpec((unit.shape[0], chunk), lambda k: (0, k)) for unit in units]
        + [pl.BlockSpec((chunk, wide), lambda k: (k, 0)) for _ in weights],
        out_specs=pl.BlockSpec((count, 4 * wide), lambda k: (0, 0)),
        out_shape=jax.ShapeDtypeStruct((count, 4 * wide), jnp.bfloat16),
        scratch_shapes=[pltpu.VMEM((count, 2 * wide), jnp.float32)] * 4,
        compiler_params=pltpu.CompilerParams(vmem_limit_bytes=VMEM_BYTES),
        cost_estimate=pl.CostEstimate(
            flops=2 * count * width * wide * 8,
            bytes_accessed=2 * width * (count + wide * 8),
            transcendentals=0,
        ),
    )(*units, *weights)


def down_kernel(mine, other, own, own_c, side_0, side_0c, side_1, side_1c, *outs):
    deep = own.shape[0] // 2
    count = mine.shape[0] // 2
    rows = 2 * count // len(outs)

    def fill(side, side_c):
        parts = (own, own_c, side, side_c)
        table = jnp.concatenate(
            [part[:deep, :] for part in parts] + [part[deep:, :] for part in parts], axis=0
        )
        joined = jnp.concatenate(
            [
                jnp.concatenate([mine[:count, :], other[count:, :]], axis=1),
                jnp.concatenate([mine[count:, :], other[:count, :]], axis=1),
            ],
            axis=0,
        )
        value = jnp.dot(joined, table, preferred_element_type=jnp.float32).astype(jnp.bfloat16)
        for at, out in enumerate(outs):
            out[...] = value[at * rows : (at + 1) * rows]

    first = pl.program_id(0) < pl.num_programs(0) // 2

    @pl.when(first)
    def _():
        fill(side_0, side_0c)

    @pl.when(jnp.logical_not(first))
    def _():
        fill(side_1, side_1c)


def down_values(mine, other, own, firsts, seconds, planes, chunk):
    count, inner = mine.shape
    deep, width = own[0].shape
    rows = count // (2 * planes)
    steps = width // chunk
    half = steps // 2
    return pl.pallas_call(
        down_kernel,
        grid=(steps,),
        in_specs=[pl.BlockSpec((count, inner), lambda k: (0, 0))] * 2
        + [pl.BlockSpec((deep, chunk), lambda k: (0, k)) for _ in own]
        + [pl.BlockSpec((deep, chunk), lambda k: (0, jnp.minimum(k, half - 1))) for _ in firsts]
        + [pl.BlockSpec((deep, chunk), lambda k: (0, jnp.maximum(k - half, 0))) for _ in seconds],
        out_specs=[pl.BlockSpec((rows, chunk), lambda k: (0, k))] * (2 * planes),
        out_shape=[jax.ShapeDtypeStruct((rows, width), jnp.bfloat16)] * (2 * planes),
        compiler_params=pltpu.CompilerParams(vmem_limit_bytes=VMEM_BYTES),
        cost_estimate=pl.CostEstimate(
            flops=2 * count * 2 * inner * width,
            bytes_accessed=8 * deep * width + 2 * count * width,
            transcendentals=0,
        ),
    )(mine, other, *own, *firsts, *seconds)


ARRIVAL = (4, 1, 2, 6, 7, 5, 3, 0)


def combine_kernel(upper, high, low, *refs):
    out = refs[-1]
    planes = len(ARRIVAL) // 2
    parts = [refs[ARRIVAL.index(at)] for at in range(2 * planes)]

    def mix(chosen):
        values = jnp.concatenate([part[...] for part in chosen], axis=0)
        total = jnp.dot(high[...], values, preferred_element_type=jnp.float32)
        total = total + jnp.dot(low[...], values, preferred_element_type=jnp.float32)
        out[...] = total.astype(jnp.bfloat16)

    side = pl.program_id(0)

    @pl.when(side == 0)
    def _():
        mix(parts[:planes])

    @pl.when(side == 1)
    def _():
        mix(parts[planes:])


def combine(upper, high, low, mine, theirs, chunk):
    rows, width = mine[0].shape
    count = high.shape[0]
    steps = width // chunk

    def own_block(g, k, upper):
        return 0, jnp.where(g == 0, k, steps - 1)

    def other_block(g, k, upper):
        return 0, jnp.where(g == 0, 0, k)

    def out_block(g, k, upper):
        return 0, (upper[0] + g) % 2 * steps + k

    return pl.pallas_call(
        combine_kernel,
        grid_spec=pltpu.PrefetchScalarGridSpec(
            num_scalar_prefetch=1,
            grid=(2, steps),
            in_specs=[pl.BlockSpec(high.shape, lambda g, k, upper: (0, 0))] * 2
            + [
                pl.BlockSpec((rows, chunk), own_block if at < len(mine) else other_block)
                for at in ARRIVAL
            ],
            out_specs=pl.BlockSpec((count, chunk), out_block),
        ),
        out_shape=jax.ShapeDtypeStruct((count, 2 * width), jnp.bfloat16),
        compiler_params=pltpu.CompilerParams(vmem_limit_bytes=SMALL_BYTES),
        cost_estimate=pl.CostEstimate(
            flops=8 * high.size * width,
            bytes_accessed=4 * width * (len(mine) * rows + count),
            transcendentals=0,
        ),
    )(upper.reshape(1), high, low, *[(*mine, *theirs)[at] for at in ARRIVAL])


def places(picks, planes, split):
    count = picks.shape[0]
    plane = lax.axis_index("ep") // split
    experts = (plane + jnp.arange(planes, dtype=jnp.int32)) % planes
    named = jnp.any(picks[None] == experts[:, None, None], axis=2)
    order = jnp.arange(count, dtype=jnp.int32)
    before = order[:, None] < order[None, :]
    rank = jnp.sum((named[:, :, None] & before[None]).astype(jnp.int32), axis=1)
    return experts, named, rank


def gate_table(picks, gates, planes, split, slots):
    experts, named, rank = places(picks, planes, split)
    weight = jnp.sum(
        jnp.where(picks[None] == experts[:, None, None], gates[None], jnp.zeros_like(gates)[None]),
        axis=2,
    )
    at = jnp.arange(slots, dtype=jnp.int32)
    found = (rank.T[:, :, None] == at[None, None, :]) & named.T[:, :, None]
    return jnp.where(found, weight.T[:, :, None], 0.0)


def layer(
    rows,
    picks,
    gates,
    latents,
    owners,
    requests,
    queries,
    cache_latents,
    cache_lens,
    gate_proj,
    up_proj,
    down_proj,
):
    n_ep = lax.axis_size("ep")
    split = FF_WIN // gate_proj.shape[1]
    planes = n_ep // split
    count, width = rows.shape
    slots = -(-3 * count * picks.shape[1] // (2 * planes * 16)) * 16
    chunk = width // 4
    upper = lax.axis_index("ep") // YBIT % 2
    span = width // 4

    gate_x = swap(gate_proj, XBIT)
    _, named, rank = places(picks, planes, split)
    at = jnp.arange(slots, dtype=jnp.int32)
    chosen = (rank[:, None, :] == at[None, :, None]) & named[:, None, :]
    chosen = chosen.astype(jnp.bfloat16)

    pack_0, out_1, out_2, out_3 = packs(
        chosen.reshape(planes * slots, count), rows, planes, span
    )
    pack_0, out_1, out_3, latents, owners, requests, down_proj = together(
        pack_0, out_1, out_3, latents, owners, requests, down_proj
    )
    own_1, own_3, peer_0 = shift(out_1, split), shift(out_3, 3 * split), swap(pack_0, YBIT)
    send = lax.dynamic_slice_in_dim(down_proj, (2 - 2 * upper) * span, 2 * span, 1)
    down_y = swap(send, YBIT)
    outgoing = hand_over(latents, owners, requests)

    own_1, own_3, peer_0, down_y, gate_x, out_2, outgoing, down_proj, gate_proj = together(
        own_1, own_3, peer_0, down_y, gate_x, out_2, outgoing, down_proj, gate_proj
    )
    own_2, peer_1, peer_3 = shift(out_2, 2 * split), swap(own_1, YBIT), swap(own_3, YBIT)
    up_x, gate_c = swap(up_proj, XBIT), swap(gate_proj, CORE)
    keep = lax.dynamic_slice_in_dim(down_proj, 2 * upper * span, 2 * span, 1)
    own = jnp.concatenate([keep, down_y], axis=0)
    begin, rest = own[:, :span], own[:, span:]

    own_2, peer_1, peer_3, up_x, gate_x, gate_c, up_proj, own, begin, rest = together(
        own_2, peer_1, peer_3, up_x, gate_x, gate_c, up_proj, own, begin, rest
    )
    outgoing, own_2 = together(outgoing, own_2)
    peer_2, side_0 = swap(own_2, YBIT), swap(begin, XBIT)
    up_c, gate_xc, up_xc = swap(up_proj, CORE), swap(gate_x, CORE), swap(up_x, CORE)
    incoming = lax.all_to_all(outgoing, "ep", split_axis=0, concat_axis=0, tiled=True)
    peer_2, up_c, gate_xc, up_xc, side_0, rest, own, picks, gates, incoming = together(
        peer_2, up_c, gate_xc, up_xc, side_0, rest, own, picks, gates, incoming
    )
    own_c, side_0c, side_1 = swap(own, CORE), swap(side_0, CORE), swap(rest, XBIT)
    units = (pack_0, own_1, own_2, own_3, peer_0, peer_1, peer_2, peer_3)
    weights = (gate_proj, gate_c, gate_x, gate_xc, up_proj, up_c, up_x, up_xc)
    hidden = hidden_units(units, weights, chunk)
    hidden, own_c, side_0c, picks, gates = together(hidden, own_c, side_0c, picks, gates)
    table = gate_table(picks, gates, planes, split, slots).reshape(count, planes * slots)
    high = lax.reduce_precision(table, 8, 7)
    high, low = high.astype(jnp.bfloat16), (table - high).astype(jnp.bfloat16)
    other, side_1, high, low = together(swap(hidden, YBIT), side_1, high, low)
    firsts, seconds = (side_0, side_0c), (side_1, swap(side_1, CORE))
    values = down_values(hidden, other, (own, own_c), firsts, seconds, planes, span // 2)
    mine, theirs = list(values[:planes]), list(values[planes:])
    theirs[0] = swap(theirs[0], YBIT)
    mine[1] = shift(mine[1], n_ep - split)
    mine[2], theirs[2] = shift(mine[2], n_ep - 2 * split), cross(theirs[2], n_ep - 2 * split)
    theirs[3] = cross(theirs[3], n_ep - 3 * split)
    theirs[1] = cross(theirs[1], n_ep - split)
    mine[3] = shift(mine[3], n_ep - 3 * split)
    handed = incoming.reshape(-1, incoming.shape[2])
    mine[0], handed = together(mine[0], handed)
    marks = handed[:, latents.shape[1]].astype(jnp.float32)[None, :]
    attended = attend(queries, cache_latents, cache_lens, handed, marks)
    theirs[0], attended = together(theirs[0], attended)
    return combine(upper, high, low, mine, theirs, span), attended


def attend_kernel(lens, query, cache, handed, marks, out):
    request = pl.program_id(0)
    heads = query.shape[2]
    wide = out.shape[2]
    lat = query.shape[1]
    asked = query[0].astype(jnp.float32).T.astype(jnp.bfloat16)
    given = handed[:, :lat]
    near = jnp.dot(asked, cache[0], preferred_element_type=jnp.float32) * score_scale
    over_last = (((1,), (1,)), ((), ()))
    far = lax.dot_general(asked, given, over_last, preferred_element_type=jnp.float32)
    far = far * score_scale
    place = lax.broadcasted_iota(jnp.int32, (heads, near.shape[1]), 1)
    near = jnp.where(place < lens[request], near, -jnp.inf)
    mark = (request + 1).astype(jnp.float32)
    far = jnp.where(jnp.broadcast_to(marks[...], far.shape) == mark, far, -jnp.inf)
    top = jnp.maximum(
        jnp.max(near, axis=1, keepdims=True), jnp.max(far, axis=1, keepdims=True)
    )
    near, far = jnp.exp(near - top), jnp.exp(far - top)
    total = jnp.sum(near, axis=1, keepdims=True) + jnp.sum(far, axis=1, keepdims=True)
    near, far = (near / total).astype(jnp.bfloat16), (far / total).astype(jnp.bfloat16)
    result = lax.dot_general(near, cache[0, :wide], over_last, preferred_element_type=jnp.float32)
    result = result + jnp.dot(far, given[:, :wide], preferred_element_type=jnp.float32)
    out[0] = result.astype(jnp.bfloat16)


def attend(queries, cache_latents, cache_lens, handed, marks):
    requests, heads, lat = queries.shape
    cached = cache_latents.shape[1]
    return pl.pallas_call(
        attend_kernel,
        grid=(requests,),
        in_specs=[
            pl.BlockSpec(memory_space=pltpu.SMEM),
            pl.BlockSpec((1, lat, heads), lambda k: (k, 0, 0)),
            pl.BlockSpec((1, lat, cached), lambda k: (k, 0, 0)),
            pl.BlockSpec(handed.shape, lambda k: (0, 0)),
            pl.BlockSpec(marks.shape, lambda k: (0, 0)),
        ],
        out_specs=pl.BlockSpec((1, heads, VDIM), lambda k: (k, 0, 0)),
        out_shape=jax.ShapeDtypeStruct((requests, heads, VDIM), jnp.bfloat16),
        compiler_params=pltpu.CompilerParams(vmem_limit_bytes=VMEM_BYTES),
        cost_estimate=pl.CostEstimate(
            flops=2 * requests * heads * (cached + handed.shape[0]) * (lat + VDIM),
            bytes_accessed=2 * requests * (heads * (lat + VDIM) + cached * lat),
            transcendentals=requests * heads * (cached + handed.shape[0]),
        ),
    )(
        cache_lens,
        jnp.swapaxes(queries, 1, 2),
        jnp.swapaxes(cache_latents, 1, 2),
        handed,
        marks,
    )


def hand_over(prompt_latents, owners, requests):
    n_ep = lax.axis_size("ep")
    stretch, lat = prompt_latents.shape
    cap = 2 * stretch // n_ep
    places_at = jnp.arange(stretch, dtype=jnp.int32)
    earlier = (owners[:, None] == owners[None, :]) & (places_at[None, :] < places_at[:, None])
    target = owners * cap + jnp.sum(earlier.astype(jnp.int32), axis=1)
    slots = jnp.arange(n_ep * cap, dtype=jnp.int32)
    chosen = slots[:, None] == target[None, :]
    packed = jnp.dot(
        chosen.astype(jnp.bfloat16), prompt_latents, preferred_element_type=jnp.float32
    ).astype(jnp.bfloat16)
    mark = jnp.sum(jnp.where(chosen, requests[None, :] + 1, 0), axis=1).astype(jnp.bfloat16)
    fill = -(lat + 1) % 128
    outgoing = jnp.concatenate(
        [packed, mark[:, None], jnp.zeros((n_ep * cap, fill), jnp.bfloat16)], axis=1
    )
    return outgoing.reshape(n_ep, cap, lat + 1 + fill)


def on_device(
    moe_rows,
    routes,
    route_gates,
    gate_proj,
    up_proj,
    down_proj,
    queries,
    cache_latents,
    cache_lens,
    prompt_latents,
    kv_owner,
    kv_request,
):
    sections, count, width = moe_rows.shape
    top = routes.shape[2]
    expert_out, attended = layer(
        moe_rows.reshape(sections * count, width),
        routes.reshape(sections * count, top),
        route_gates.reshape(sections * count, top),
        prompt_latents,
        kv_owner[:, 0],
        kv_request,
        queries,
        cache_latents,
        cache_lens,
        gate_proj,
        up_proj,
        down_proj,
    )
    expert_out = expert_out.reshape(moe_rows.shape)
    return (expert_out, attended)


def solution(mesh):
    placed = (
        P("section", ("groups", "ep"), None),
        P("section", ("groups", "ep"), None),
        P("section", ("groups", "ep"), None),
        P(None, "ep"),
        P(None, "ep"),
        P("ep", None),
        P(("groups", "ep"), None, None),
        P(("groups", "ep"), None, None),
        P(("groups", "ep")),
        P(("groups", "ep"), None),
        P(("groups", "ep"), None),
        P(("groups", "ep")),
    )
    return jax.shard_map(
        on_device,
        mesh=mesh,
        in_specs=placed,
        out_specs=(P("section", ("groups", "ep"), None), P(("groups", "ep"), None, None)),
        check_vma=False,
    )
```

```python
from functools import partial

import jax
import jax.numpy as jnp
from jax import lax
from jax.experimental import pallas as pl
from jax.experimental.pallas import tpu as pltpu
from jax.sharding import PartitionSpec as P

VDIM = 512
FF_WIN = 1024
CORE, XBIT, YBIT = 1, 2, 4
VMEM_BYTES = 60 * 1024 * 1024
SMALL_BYTES = 14 * 1024 * 1024


score_scale = 0.07216878364870323


def swap(value, bit):
    count = lax.axis_size("ep")
    return lax.ppermute(value, "ep", [(i, i ^ bit) for i in range(count)])


def shift(value, step):
    count = lax.axis_size("ep")
    return lax.ppermute(value, "ep", [(i, (i + step) % count) for i in range(count)])


def cross(value, step):
    count = lax.axis_size("ep")
    pairs = [(i, (i + step) % count ^ YBIT) for i in range(count)]
    return lax.ppermute(value, "ep", pairs)


def together(*values):
    return lax.optimization_barrier(values)


def pair_dot(rows, left, right):
    both = jnp.concatenate([left[...], right[...]], axis=1)
    return jnp.dot(rows, both, preferred_element_type=jnp.float32)


def gated(gate, up):
    return (gate / (1.0 + jnp.exp(-gate)) * up).astype(jnp.bfloat16)


def pack_kernel(chosen, rows, *outs):
    picked = jnp.dot(chosen[...], rows[...], preferred_element_type=jnp.float32)
    picked = picked.astype(jnp.bfloat16)
    slots = outs[0].shape[0]
    for at, out in enumerate(outs):
        out[...] = picked[at * slots : (at + 1) * slots]


def packs(chosen, rows, planes, chunk):
    count, width = rows.shape
    slots = chosen.shape[0] // planes
    return pl.pallas_call(
        pack_kernel,
        grid=(width // chunk,),
        in_specs=[
            pl.BlockSpec(chosen.shape, lambda k: (0, 0)),
            pl.BlockSpec((count, chunk), lambda k: (0, k)),
        ],
        out_specs=[pl.BlockSpec((slots, chunk), lambda k: (0, k))] * planes,
        out_shape=[jax.ShapeDtypeStruct((slots, width), jnp.bfloat16)] * planes,
        compiler_params=pltpu.CompilerParams(vmem_limit_bytes=SMALL_BYTES),
        cost_estimate=pl.CostEstimate(
            flops=2 * chosen.size * width,
            bytes_accessed=2 * width * (count + planes * slots),
            transcendentals=0,
        ),
    )(chosen, rows)


def hidden_kernel(count, *refs):
    units, weights = refs[:count], refs[count : count + 8]
    gate_o, gate_c, gate_x, gate_xc, up_o, up_c, up_x, up_xc = weights
    out, near_gate, far_gate, near_up, far_up = refs[count + 8 :]
    step = pl.program_id(0)

    @pl.when(step == 0)
    def _():
        for total in (near_gate, far_gate, near_up, far_up):
            total[...] = jnp.zeros_like(total)

    rows = jnp.concatenate([unit[...] for unit in units], axis=0)
    near_gate[...] += pair_dot(rows, gate_o, gate_c)
    near_up[...] += pair_dot(rows, up_o, up_c)
    far_gate[...] += pair_dot(rows, gate_x, gate_xc)
    far_up[...] += pair_dot(rows, up_x, up_xc)

    @pl.when(step == pl.num_programs(0) - 1)
    def _():
        two = near_up.shape[1]
        out[:, :two] = gated(near_gate[...], near_up[...])
        out[:, two:] = gated(far_gate[...], far_up[...])


def hidden_units(units, weights, chunk):
    width, wide = weights[0].shape
    count = sum(unit.shape[0] for unit in units)
    return pl.pallas_call(
        partial(hidden_kernel, len(units)),
        grid=(width // chunk,),
        in_specs=[pl.BlockSpec((unit.shape[0], chunk), lambda k: (0, k)) for unit in units]
        + [pl.BlockSpec((chunk, wide), lambda k: (k, 0)) for _ in weights],
        out_specs=pl.BlockSpec((count, 4 * wide), lambda k: (0, 0)),
        out_shape=jax.ShapeDtypeStruct((count, 4 * wide), jnp.bfloat16),
        scratch_shapes=[pltpu.VMEM((count, 2 * wide), jnp.float32)] * 4,
        compiler_params=pltpu.CompilerParams(vmem_limit_bytes=VMEM_BYTES),
        cost_estimate=pl.CostEstimate(
            flops=2 * count * width * wide * 8,
            bytes_accessed=2 * width * (count + wide * 8),
            transcendentals=0,
        ),
    )(*units, *weights)


def down_kernel(mine, other, own, own_c, side_0, side_0c, side_1, side_1c, *outs):
    deep = own.shape[0] // 2
    count = mine.shape[0] // 2
    rows = 2 * count // len(outs)

    def fill(side, side_c):
        parts = (own, own_c, side, side_c)
        table = jnp.concatenate(
            [part[:deep, :] for part in parts] + [part[deep:, :] for part in parts], axis=0
        )
        joined = jnp.concatenate(
            [
                jnp.concatenate([mine[:count, :], other[count:, :]], axis=1),
                jnp.concatenate([mine[count:, :], other[:count, :]], axis=1),
            ],
            axis=0,
        )
        value = jnp.dot(joined, table, preferred_element_type=jnp.float32).astype(jnp.bfloat16)
        for at, out in enumerate(outs):
            out[...] = value[at * rows : (at + 1) * rows]

    first = pl.program_id(0) < pl.num_programs(0) // 2

    @pl.when(first)
    def _():
        fill(side_0, side_0c)

    @pl.when(jnp.logical_not(first))
    def _():
        fill(side_1, side_1c)


def down_values(mine, other, own, firsts, seconds, planes, chunk):
    count, inner = mine.shape
    deep, width = own[0].shape
    rows = count // (2 * planes)
    steps = width // chunk
    half = steps // 2
    return pl.pallas_call(
        down_kernel,
        grid=(steps,),
        in_specs=[pl.BlockSpec((count, inner), lambda k: (0, 0))] * 2
        + [pl.BlockSpec((deep, chunk), lambda k: (0, k)) for _ in own]
        + [pl.BlockSpec((deep, chunk), lambda k: (0, jnp.minimum(k, half - 1))) for _ in firsts]
        + [pl.BlockSpec((deep, chunk), lambda k: (0, jnp.maximum(k - half, 0))) for _ in seconds],
        out_specs=[pl.BlockSpec((rows, chunk), lambda k: (0, k))] * (2 * planes),
        out_shape=[jax.ShapeDtypeStruct((rows, width), jnp.bfloat16)] * (2 * planes),
        compiler_params=pltpu.CompilerParams(vmem_limit_bytes=VMEM_BYTES),
        cost_estimate=pl.CostEstimate(
            flops=2 * count * 2 * inner * width,
            bytes_accessed=8 * deep * width + 2 * count * width,
            transcendentals=0,
        ),
    )(mine, other, *own, *firsts, *seconds)


ARRIVAL = (4, 1, 2, 6, 7, 5, 3, 0)


def combine_kernel(upper, high, low, *refs):
    out = refs[-1]
    planes = len(ARRIVAL) // 2
    parts = [refs[ARRIVAL.index(at)] for at in range(2 * planes)]

    def mix(chosen):
        values = jnp.concatenate([part[...] for part in chosen], axis=0)
        total = jnp.dot(high[...], values, preferred_element_type=jnp.float32)
        total = total + jnp.dot(low[...], values, preferred_element_type=jnp.float32)
        out[...] = total.astype(jnp.bfloat16)

    side = pl.program_id(0)

    @pl.when(side == 0)
    def _():
        mix(parts[:planes])

    @pl.when(side == 1)
    def _():
        mix(parts[planes:])


def combine(upper, high, low, mine, theirs, chunk):
    rows, width = mine[0].shape
    count = high.shape[0]
    steps = width // chunk

    def own_block(g, k, upper):
        return 0, jnp.where(g == 0, k, steps - 1)

    def other_block(g, k, upper):
        return 0, jnp.where(g == 0, 0, k)

    def out_block(g, k, upper):
        return 0, (upper[0] + g) % 2 * steps + k

    return pl.pallas_call(
        combine_kernel,
        grid_spec=pltpu.PrefetchScalarGridSpec(
            num_scalar_prefetch=1,
            grid=(2, steps),
            in_specs=[pl.BlockSpec(high.shape, lambda g, k, upper: (0, 0))] * 2
            + [
                pl.BlockSpec((rows, chunk), own_block if at < len(mine) else other_block)
                for at in ARRIVAL
            ],
            out_specs=pl.BlockSpec((count, chunk), out_block),
        ),
        out_shape=jax.ShapeDtypeStruct((count, 2 * width), jnp.bfloat16),
        compiler_params=pltpu.CompilerParams(vmem_limit_bytes=SMALL_BYTES),
        cost_estimate=pl.CostEstimate(
            flops=8 * high.size * width,
            bytes_accessed=4 * width * (len(mine) * rows + count),
            transcendentals=0,
        ),
    )(upper.reshape(1), high, low, *[(*mine, *theirs)[at] for at in ARRIVAL])


def places(picks, planes, split):
    count = picks.shape[0]
    plane = lax.axis_index("ep") // split
    experts = (plane + jnp.arange(planes, dtype=jnp.int32)) % planes
    named = jnp.any(picks[None] == experts[:, None, None], axis=2)
    order = jnp.arange(count, dtype=jnp.int32)
    before = order[:, None] < order[None, :]
    rank = jnp.sum((named[:, :, None] & before[None]).astype(jnp.int32), axis=1)
    return experts, named, rank


def gate_table(picks, gates, planes, split, slots):
    experts, named, rank = places(picks, planes, split)
    weight = jnp.sum(
        jnp.where(picks[None] == experts[:, None, None], gates[None], jnp.zeros_like(gates)[None]),
        axis=2,
    )
    at = jnp.arange(slots, dtype=jnp.int32)
    found = (rank.T[:, :, None] == at[None, None, :]) & named.T[:, :, None]
    return jnp.where(found, weight.T[:, :, None], 0.0)


def layer(
    rows,
    picks,
    gates,
    latents,
    owners,
    requests,
    queries,
    cache_latents,
    cache_lens,
    gate_proj,
    up_proj,
    down_proj,
):
    n_ep = lax.axis_size("ep")
    split = FF_WIN // gate_proj.shape[1]
    planes = n_ep // split
    count, width = rows.shape
    slots = -(-3 * count * picks.shape[1] // (2 * planes * 16)) * 16
    chunk = width // 4
    upper = lax.axis_index("ep") // YBIT % 2
    span = width // 4

    gate_x = swap(gate_proj, XBIT)
    _, named, rank = places(picks, planes, split)
    at = jnp.arange(slots, dtype=jnp.int32)
    chosen = (rank[:, None, :] == at[None, :, None]) & named[:, None, :]
    chosen = chosen.astype(jnp.bfloat16)

    pack_0, out_1, out_2, out_3 = packs(
        chosen.reshape(planes * slots, count), rows, planes, span
    )
    pack_0, out_1, out_3, latents, owners, requests, down_proj = together(
        pack_0, out_1, out_3, latents, owners, requests, down_proj
    )
    own_1, own_3, peer_0 = shift(out_1, split), shift(out_3, 3 * split), swap(pack_0, YBIT)
    send = lax.dynamic_slice_in_dim(down_proj, (2 - 2 * upper) * span, 2 * span, 1)
    down_y = swap(send, YBIT)
    outgoing = hand_over(latents, owners, requests)

    own_1, own_3, peer_0, down_y, gate_x, out_2, outgoing, down_proj, gate_proj = together(
        own_1, own_3, peer_0, down_y, gate_x, out_2, outgoing, down_proj, gate_proj
    )
    own_2, peer_1, peer_3 = shift(out_2, 2 * split), swap(own_1, YBIT), swap(own_3, YBIT)
    up_x, gate_c = swap(up_proj, XBIT), swap(gate_proj, CORE)
    keep = lax.dynamic_slice_in_dim(down_proj, 2 * upper * span, 2 * span, 1)
    own = jnp.concatenate([keep, down_y], axis=0)
    begin, rest = own[:, :span], own[:, span:]

    own_2, peer_1, peer_3, up_x, gate_x, gate_c, up_proj, own, begin, rest = together(
        own_2, peer_1, peer_3, up_x, gate_x, gate_c, up_proj, own, begin, rest
    )
    outgoing, own_2 = together(outgoing, own_2)
    peer_2, side_0 = swap(own_2, YBIT), swap(begin, XBIT)
    up_c, gate_xc, up_xc = swap(up_proj, CORE), swap(gate_x, CORE), swap(up_x, CORE)
    incoming = lax.all_to_all(outgoing, "ep", split_axis=0, concat_axis=0, tiled=True)
    peer_2, up_c, gate_xc, up_xc, side_0, rest, own, picks, gates, incoming = together(
        peer_2, up_c, gate_xc, up_xc, side_0, rest, own, picks, gates, incoming
    )
    own_c, side_0c, side_1 = swap(own, CORE), swap(side_0, CORE), swap(rest, XBIT)
    units = (pack_0, own_1, own_2, own_3, peer_0, peer_1, peer_2, peer_3)
    weights = (gate_proj, gate_c, gate_x, gate_xc, up_proj, up_c, up_x, up_xc)
    hidden = hidden_units(units, weights, chunk)
    hidden, own_c, side_0c, picks, gates = together(hidden, own_c, side_0c, picks, gates)
    table = gate_table(picks, gates, planes, split, slots).reshape(count, planes * slots)
    high = lax.reduce_precision(table, 8, 7)
    high, low = high.astype(jnp.bfloat16), (table - high).astype(jnp.bfloat16)
    other, side_1, high, low = together(swap(hidden, YBIT), side_1, high, low)
    firsts, seconds = (side_0, side_0c), (side_1, swap(side_1, CORE))
    values = down_values(hidden, other, (own, own_c), firsts, seconds, planes, span)
    mine, theirs = list(values[:planes]), list(values[planes:])
    theirs[0] = swap(theirs[0], YBIT)
    mine[1] = shift(mine[1], n_ep - split)
    mine[2], theirs[2] = shift(mine[2], n_ep - 2 * split), cross(theirs[2], n_ep - 2 * split)
    theirs[3] = cross(theirs[3], n_ep - 3 * split)
    theirs[1] = cross(theirs[1], n_ep - split)
    mine[3] = shift(mine[3], n_ep - 3 * split)
    handed = incoming.reshape(-1, incoming.shape[2])
    mine[0], handed = together(mine[0], handed)
    marks = handed[:, latents.shape[1]].astype(jnp.float32)[None, :]
    attended = attend(queries, cache_latents, cache_lens, handed, marks)
    theirs[0], attended = together(theirs[0], attended)
    return combine(upper, high, low, mine, theirs, 2 * span), attended


def attend_kernel(lens, query, cache, handed, marks, out):
    request = pl.program_id(0)
    heads = query.shape[2]
    wide = out.shape[2]
    lat = query.shape[1]
    asked = query[0].astype(jnp.float32).T.astype(jnp.bfloat16)
    given = handed[:, :lat]
    near = jnp.dot(asked, cache[0], preferred_element_type=jnp.float32) * score_scale
    over_last = (((1,), (1,)), ((), ()))
    far = lax.dot_general(asked, given, over_last, preferred_element_type=jnp.float32)
    far = far * score_scale
    place = lax.broadcasted_iota(jnp.int32, (heads, near.shape[1]), 1)
    near = jnp.where(place < lens[request], near, -jnp.inf)
    mark = (request + 1).astype(jnp.float32)
    far = jnp.where(jnp.broadcast_to(marks[...], far.shape) == mark, far, -jnp.inf)
    top = jnp.maximum(
        jnp.max(near, axis=1, keepdims=True), jnp.max(far, axis=1, keepdims=True)
    )
    near, far = jnp.exp(near - top), jnp.exp(far - top)
    total = jnp.sum(near, axis=1, keepdims=True) + jnp.sum(far, axis=1, keepdims=True)
    near, far = (near / total).astype(jnp.bfloat16), (far / total).astype(jnp.bfloat16)
    result = lax.dot_general(near, cache[0, :wide], over_last, preferred_element_type=jnp.float32)
    result = result + jnp.dot(far, given[:, :wide], preferred_element_type=jnp.float32)
    out[0] = result.astype(jnp.bfloat16)


def attend(queries, cache_latents, cache_lens, handed, marks):
    requests, heads, lat = queries.shape
    cached = cache_latents.shape[1]
    return pl.pallas_call(
        attend_kernel,
        grid=(requests,),
        in_specs=[
            pl.BlockSpec(memory_space=pltpu.SMEM),
            pl.BlockSpec((1, lat, heads), lambda k: (k, 0, 0)),
            pl.BlockSpec((1, lat, cached), lambda k: (k, 0, 0)),
            pl.BlockSpec(handed.shape, lambda k: (0, 0)),
            pl.BlockSpec(marks.shape, lambda k: (0, 0)),
        ],
        out_specs=pl.BlockSpec((1, heads, VDIM), lambda k: (k, 0, 0)),
        out_shape=jax.ShapeDtypeStruct((requests, heads, VDIM), jnp.bfloat16),
        compiler_params=pltpu.CompilerParams(vmem_limit_bytes=VMEM_BYTES),
        cost_estimate=pl.CostEstimate(
            flops=2 * requests * heads * (cached + handed.shape[0]) * (lat + VDIM),
            bytes_accessed=2 * requests * (heads * (lat + VDIM) + cached * lat),
            transcendentals=requests * heads * (cached + handed.shape[0]),
        ),
    )(
        cache_lens,
        jnp.swapaxes(queries, 1, 2),
        jnp.swapaxes(cache_latents, 1, 2),
        handed,
        marks,
    )


def hand_over(prompt_latents, owners, requests):
    n_ep = lax.axis_size("ep")
    stretch, lat = prompt_latents.shape
    cap = 2 * stretch // n_ep
    places_at = jnp.arange(stretch, dtype=jnp.int32)
    earlier = (owners[:, None] == owners[None, :]) & (places_at[None, :] < places_at[:, None])
    target = owners * cap + jnp.sum(earlier.astype(jnp.int32), axis=1)
    slots = jnp.arange(n_ep * cap, dtype=jnp.int32)
    chosen = slots[:, None] == target[None, :]
    packed = jnp.dot(
        chosen.astype(jnp.bfloat16), prompt_latents, preferred_element_type=jnp.float32
    ).astype(jnp.bfloat16)
    mark = jnp.sum(jnp.where(chosen, requests[None, :] + 1, 0), axis=1).astype(jnp.bfloat16)
    fill = -(lat + 1) % 128
    outgoing = jnp.concatenate(
        [packed, mark[:, None], jnp.zeros((n_ep * cap, fill), jnp.bfloat16)], axis=1
    )
    return outgoing.reshape(n_ep, cap, lat + 1 + fill)


def on_device(
    moe_rows,
    routes,
    route_gates,
    gate_proj,
    up_proj,
    down_proj,
    queries,
    cache_latents,
    cache_lens,
    prompt_latents,
    kv_owner,
    kv_request,
):
    sections, count, width = moe_rows.shape
    top = routes.shape[2]
    expert_out, attended = layer(
        moe_rows.reshape(sections * count, width),
        routes.reshape(sections * count, top),
        route_gates.reshape(sections * count, top),
        prompt_latents,
        kv_owner[:, 0],
        kv_request,
        queries,
        cache_latents,
        cache_lens,
        gate_proj,
        up_proj,
        down_proj,
    )
    expert_out = expert_out.reshape(moe_rows.shape)
    return (expert_out, attended)


def solution(mesh):
    placed = (
        P("section", ("groups", "ep"), None),
        P("section", ("groups", "ep"), None),
        P("section", ("groups", "ep"), None),
        P(None, "ep"),
        P(None, "ep"),
        P("ep", None),
        P(("groups", "ep"), None, None),
        P(("groups", "ep"), None, None),
        P(("groups", "ep")),
        P(("groups", "ep"), None),
        P(("groups", "ep"), None),
        P(("groups", "ep")),
    )
    return jax.shard_map(
        on_device,
        mesh=mesh,
        in_specs=placed,
        out_specs=(P("section", ("groups", "ep"), None), P(("groups", "ep"), None, None)),
        check_vma=False,
    )
```

```python
from functools import partial

import jax
import jax.numpy as jnp
from jax import lax
from jax.experimental import pallas as pl
from jax.experimental.pallas import tpu as pltpu
from jax.sharding import PartitionSpec as P

VDIM = 512
FF_WIN = 1024
CORE, XBIT, YBIT = 1, 2, 4
VMEM_BYTES = 60 * 1024 * 1024
SMALL_BYTES = 14 * 1024 * 1024


score_scale = 0.07216878364870323


def swap(value, bit):
    count = lax.axis_size("ep")
    return lax.ppermute(value, "ep", [(i, i ^ bit) for i in range(count)])


def shift(value, step):
    count = lax.axis_size("ep")
    return lax.ppermute(value, "ep", [(i, (i + step) % count) for i in range(count)])


def cross(value, step):
    count = lax.axis_size("ep")
    pairs = [(i, (i + step) % count ^ YBIT) for i in range(count)]
    return lax.ppermute(value, "ep", pairs)


def together(*values):
    return lax.optimization_barrier(values)


def pair_dot(rows, left, right):
    both = jnp.concatenate([left[...], right[...]], axis=1)
    return jnp.dot(rows, both, preferred_element_type=jnp.float32)


def gated(gate, up):
    return (gate / (1.0 + jnp.exp(-gate)) * up).astype(jnp.bfloat16)


def pack_kernel(chosen, rows, *outs):
    picked = jnp.dot(chosen[...], rows[...], preferred_element_type=jnp.float32)
    picked = picked.astype(jnp.bfloat16)
    slots = outs[0].shape[0]
    for at, out in enumerate(outs):
        out[...] = picked[at * slots : (at + 1) * slots]


def packs(chosen, rows, planes, chunk):
    count, width = rows.shape
    slots = chosen.shape[0] // planes
    return pl.pallas_call(
        pack_kernel,
        grid=(width // chunk,),
        in_specs=[
            pl.BlockSpec(chosen.shape, lambda k: (0, 0)),
            pl.BlockSpec((count, chunk), lambda k: (0, k)),
        ],
        out_specs=[pl.BlockSpec((slots, chunk), lambda k: (0, k))] * planes,
        out_shape=[jax.ShapeDtypeStruct((slots, width), jnp.bfloat16)] * planes,
        compiler_params=pltpu.CompilerParams(vmem_limit_bytes=SMALL_BYTES),
        cost_estimate=pl.CostEstimate(
            flops=2 * chosen.size * width,
            bytes_accessed=2 * width * (count + planes * slots),
            transcendentals=0,
        ),
    )(chosen, rows)


def hidden_kernel(count, *refs):
    units, weights = refs[:count], refs[count : count + 8]
    gate_o, gate_c, gate_x, gate_xc, up_o, up_c, up_x, up_xc = weights
    out, near_gate, far_gate, near_up, far_up = refs[count + 8 :]
    step = pl.program_id(0)

    @pl.when(step == 0)
    def _():
        for total in (near_gate, far_gate, near_up, far_up):
            total[...] = jnp.zeros_like(total)

    rows = jnp.concatenate([unit[...] for unit in units], axis=0)
    near_gate[...] += pair_dot(rows, gate_o, gate_c)
    near_up[...] += pair_dot(rows, up_o, up_c)
    far_gate[...] += pair_dot(rows, gate_x, gate_xc)
    far_up[...] += pair_dot(rows, up_x, up_xc)

    @pl.when(step == pl.num_programs(0) - 1)
    def _():
        two = near_up.shape[1]
        out[:, :two] = gated(near_gate[...], near_up[...])
        out[:, two:] = gated(far_gate[...], far_up[...])


def hidden_units(units, weights, chunk):
    width, wide = weights[0].shape
    count = sum(unit.shape[0] for unit in units)
    return pl.pallas_call(
        partial(hidden_kernel, len(units)),
        grid=(width // chunk,),
        in_specs=[pl.BlockSpec((unit.shape[0], chunk), lambda k: (0, k)) for unit in units]
        + [pl.BlockSpec((chunk, wide), lambda k: (k, 0)) for _ in weights],
        out_specs=pl.BlockSpec((count, 4 * wide), lambda k: (0, 0)),
        out_shape=jax.ShapeDtypeStruct((count, 4 * wide), jnp.bfloat16),
        scratch_shapes=[pltpu.VMEM((count, 2 * wide), jnp.float32)] * 4,
        compiler_params=pltpu.CompilerParams(vmem_limit_bytes=VMEM_BYTES),
        cost_estimate=pl.CostEstimate(
            flops=2 * count * width * wide * 8,
            bytes_accessed=2 * width * (count + wide * 8),
            transcendentals=0,
        ),
    )(*units, *weights)


def down_kernel(mine, other, own, own_c, side_0, side_0c, side_1, side_1c, *outs):
    deep = own.shape[0] // 2
    count = mine.shape[0] // 2
    rows = 2 * count // len(outs)

    def fill(side, side_c):
        parts = (own, own_c, side, side_c)
        table = jnp.concatenate(
            [part[:deep, :] for part in parts] + [part[deep:, :] for part in parts], axis=0
        )
        joined = jnp.concatenate(
            [
                jnp.concatenate([mine[:count, :], other[count:, :]], axis=1),
                jnp.concatenate([mine[count:, :], other[:count, :]], axis=1),
            ],
            axis=0,
        )
        value = jnp.dot(joined, table, preferred_element_type=jnp.float32).astype(jnp.bfloat16)
        for at, out in enumerate(outs):
            out[...] = value[at * rows : (at + 1) * rows]

    first = pl.program_id(0) < pl.num_programs(0) // 2

    @pl.when(first)
    def _():
        fill(side_0, side_0c)

    @pl.when(jnp.logical_not(first))
    def _():
        fill(side_1, side_1c)


def down_values(mine, other, own, firsts, seconds, planes, chunk):
    count, inner = mine.shape
    deep, width = own[0].shape
    rows = count // (2 * planes)
    steps = width // chunk
    half = steps // 2
    return pl.pallas_call(
        down_kernel,
        grid=(steps,),
        in_specs=[pl.BlockSpec((count, inner), lambda k: (0, 0))] * 2
        + [pl.BlockSpec((deep, chunk), lambda k: (0, k)) for _ in own]
        + [pl.BlockSpec((deep, chunk), lambda k: (0, jnp.minimum(k, half - 1))) for _ in firsts]
        + [pl.BlockSpec((deep, chunk), lambda k: (0, jnp.maximum(k - half, 0))) for _ in seconds],
        out_specs=[pl.BlockSpec((rows, chunk), lambda k: (0, k))] * (2 * planes),
        out_shape=[jax.ShapeDtypeStruct((rows, width), jnp.bfloat16)] * (2 * planes),
        compiler_params=pltpu.CompilerParams(vmem_limit_bytes=VMEM_BYTES),
        cost_estimate=pl.CostEstimate(
            flops=2 * count * 2 * inner * width,
            bytes_accessed=8 * deep * width + 2 * count * width,
            transcendentals=0,
        ),
    )(mine, other, *own, *firsts, *seconds)


ARRIVAL = (4, 1, 2, 6, 7, 5, 3, 0)


def combine_kernel(upper, high, low, *refs):
    out = refs[-1]
    planes = len(ARRIVAL) // 2
    parts = [refs[ARRIVAL.index(at)] for at in range(2 * planes)]

    def mix(chosen):
        values = jnp.concatenate([part[...] for part in chosen], axis=0)
        total = jnp.dot(high[...], values, preferred_element_type=jnp.float32)
        total = total + jnp.dot(low[...], values, preferred_element_type=jnp.float32)
        out[...] = total.astype(jnp.bfloat16)

    side = pl.program_id(0)

    @pl.when(side == 0)
    def _():
        mix(parts[:planes])

    @pl.when(side == 1)
    def _():
        mix(parts[planes:])


def combine(upper, high, low, mine, theirs, chunk):
    rows, width = mine[0].shape
    count = high.shape[0]
    steps = width // chunk

    def own_block(g, k, upper):
        return 0, jnp.where(g == 0, k, steps - 1)

    def other_block(g, k, upper):
        return 0, jnp.where(g == 0, 0, k)

    def out_block(g, k, upper):
        return 0, (upper[0] + g) % 2 * steps + k

    return pl.pallas_call(
        combine_kernel,
        grid_spec=pltpu.PrefetchScalarGridSpec(
            num_scalar_prefetch=1,
            grid=(2, steps),
            in_specs=[pl.BlockSpec(high.shape, lambda g, k, upper: (0, 0))] * 2
            + [
                pl.BlockSpec((rows, chunk), own_block if at < len(mine) else other_block)
                for at in ARRIVAL
            ],
            out_specs=pl.BlockSpec((count, chunk), out_block),
        ),
        out_shape=jax.ShapeDtypeStruct((count, 2 * width), jnp.bfloat16),
        compiler_params=pltpu.CompilerParams(vmem_limit_bytes=SMALL_BYTES),
        cost_estimate=pl.CostEstimate(
            flops=8 * high.size * width,
            bytes_accessed=4 * width * (len(mine) * rows + count),
            transcendentals=0,
        ),
    )(upper.reshape(1), high, low, *[(*mine, *theirs)[at] for at in ARRIVAL])


def places(picks, planes, split):
    count = picks.shape[0]
    plane = lax.axis_index("ep") // split
    experts = (plane + jnp.arange(planes, dtype=jnp.int32)) % planes
    named = jnp.any(picks[None] == experts[:, None, None], axis=2)
    order = jnp.arange(count, dtype=jnp.int32)
    before = order[:, None] < order[None, :]
    rank = jnp.sum((named[:, :, None] & before[None]).astype(jnp.int32), axis=1)
    return experts, named, rank


def gate_table(picks, gates, planes, split, slots):
    experts, named, rank = places(picks, planes, split)
    weight = jnp.sum(
        jnp.where(picks[None] == experts[:, None, None], gates[None], jnp.zeros_like(gates)[None]),
        axis=2,
    )
    at = jnp.arange(slots, dtype=jnp.int32)
    found = (rank.T[:, :, None] == at[None, None, :]) & named.T[:, :, None]
    return jnp.where(found, weight.T[:, :, None], 0.0)


def layer(
    rows,
    picks,
    gates,
    latents,
    owners,
    requests,
    queries,
    cache_latents,
    cache_lens,
    gate_proj,
    up_proj,
    down_proj,
):
    n_ep = lax.axis_size("ep")
    split = FF_WIN // gate_proj.shape[1]
    planes = n_ep // split
    count, width = rows.shape
    slots = -(-3 * count * picks.shape[1] // (2 * planes * 16)) * 16
    chunk = width // 4
    upper = lax.axis_index("ep") // YBIT % 2
    span = width // 4

    gate_x = swap(gate_proj, XBIT)
    _, named, rank = places(picks, planes, split)
    at = jnp.arange(slots, dtype=jnp.int32)
    chosen = (rank[:, None, :] == at[None, :, None]) & named[:, None, :]
    chosen = chosen.astype(jnp.bfloat16)

    pack_0, out_1, out_2, out_3 = packs(
        chosen.reshape(planes * slots, count), rows, planes, span
    )
    pack_0, out_1, out_3, latents, owners, requests = together(
        pack_0, out_1, out_3, latents, owners, requests
    )
    own_1, own_3, peer_0 = shift(out_1, split), shift(out_3, 3 * split), swap(pack_0, YBIT)
    send = lax.dynamic_slice_in_dim(down_proj, (2 - 2 * upper) * span, 2 * span, 1)
    down_y = swap(send, YBIT)
    outgoing = hand_over(latents, owners, requests)

    own_1, own_3, peer_0, down_y, gate_x, out_2, outgoing, down_proj, gate_proj = together(
        own_1, own_3, peer_0, down_y, gate_x, out_2, outgoing, down_proj, gate_proj
    )
    own_2, peer_1, peer_3 = shift(out_2, 2 * split), swap(own_1, YBIT), swap(own_3, YBIT)
    up_x, gate_c = swap(up_proj, XBIT), swap(gate_proj, CORE)
    keep = lax.dynamic_slice_in_dim(down_proj, 2 * upper * span, 2 * span, 1)
    own = jnp.concatenate([keep, down_y], axis=0)
    begin, rest = own[:, :span], own[:, span:]

    own_2, peer_1, peer_3, up_x, gate_x, gate_c, up_proj, own, begin, rest = together(
        own_2, peer_1, peer_3, up_x, gate_x, gate_c, up_proj, own, begin, rest
    )
    outgoing, own_2 = together(outgoing, own_2)
    peer_2, side_0 = swap(own_2, YBIT), swap(begin, XBIT)
    up_c, gate_xc, up_xc = swap(up_proj, CORE), swap(gate_x, CORE), swap(up_x, CORE)
    incoming = lax.all_to_all(outgoing, "ep", split_axis=0, concat_axis=0, tiled=True)
    peer_2, up_c, gate_xc, up_xc, side_0, rest, own, picks, gates, incoming = together(
        peer_2, up_c, gate_xc, up_xc, side_0, rest, own, picks, gates, incoming
    )
    own_c, side_0c, side_1 = swap(own, CORE), swap(side_0, CORE), swap(rest, XBIT)
    units = (pack_0, own_1, own_2, own_3, peer_0, peer_1, peer_2, peer_3)
    weights = (gate_proj, gate_c, gate_x, gate_xc, up_proj, up_c, up_x, up_xc)
    hidden = hidden_units(units, weights, chunk)
    hidden, own_c, side_0c, picks, gates = together(hidden, own_c, side_0c, picks, gates)
    table = gate_table(picks, gates, planes, split, slots).reshape(count, planes * slots)
    high = lax.reduce_precision(table, 8, 7)
    high, low = high.astype(jnp.bfloat16), (table - high).astype(jnp.bfloat16)
    other, side_1, high, low = together(swap(hidden, YBIT), side_1, high, low)
    firsts, seconds = (side_0, side_0c), (side_1, swap(side_1, CORE))
    values = down_values(hidden, other, (own, own_c), firsts, seconds, planes, span)
    mine, theirs = list(values[:planes]), list(values[planes:])
    theirs[0] = swap(theirs[0], YBIT)
    mine[1] = shift(mine[1], n_ep - split)
    mine[2], theirs[2] = shift(mine[2], n_ep - 2 * split), cross(theirs[2], n_ep - 2 * split)
    theirs[3] = cross(theirs[3], n_ep - 3 * split)
    theirs[1] = cross(theirs[1], n_ep - split)
    mine[3] = shift(mine[3], n_ep - 3 * split)
    handed = incoming.reshape(-1, incoming.shape[2])
    mine[0], handed = together(mine[0], handed)
    marks = handed[:, latents.shape[1]].astype(jnp.float32)[None, :]
    attended = attend(queries, cache_latents, cache_lens, handed, marks)
    theirs[0], attended = together(theirs[0], attended)
    return combine(upper, high, low, mine, theirs, 2 * span), attended


def attend_kernel(lens, query, cache, handed, marks, out):
    request = pl.program_id(0)
    heads = query.shape[2]
    wide = out.shape[2]
    lat = query.shape[1]
    asked = query[0].astype(jnp.float32).T.astype(jnp.bfloat16)
    given = handed[:, :lat]
    near = jnp.dot(asked, cache[0], preferred_element_type=jnp.float32) * score_scale
    over_last = (((1,), (1,)), ((), ()))
    far = lax.dot_general(asked, given, over_last, preferred_element_type=jnp.float32)
    far = far * score_scale
    place = lax.broadcasted_iota(jnp.int32, (heads, near.shape[1]), 1)
    near = jnp.where(place < lens[request], near, -jnp.inf)
    mark = (request + 1).astype(jnp.float32)
    far = jnp.where(jnp.broadcast_to(marks[...], far.shape) == mark, far, -jnp.inf)
    top = jnp.maximum(
        jnp.max(near, axis=1, keepdims=True), jnp.max(far, axis=1, keepdims=True)
    )
    near, far = jnp.exp(near - top), jnp.exp(far - top)
    total = jnp.sum(near, axis=1, keepdims=True) + jnp.sum(far, axis=1, keepdims=True)
    near, far = (near / total).astype(jnp.bfloat16), (far / total).astype(jnp.bfloat16)
    result = lax.dot_general(near, cache[0, :wide], over_last, preferred_element_type=jnp.float32)
    result = result + jnp.dot(far, given[:, :wide], preferred_element_type=jnp.float32)
    out[0] = result.astype(jnp.bfloat16)


def attend(queries, cache_latents, cache_lens, handed, marks):
    requests, heads, lat = queries.shape
    cached = cache_latents.shape[1]
    return pl.pallas_call(
        attend_kernel,
        grid=(requests,),
        in_specs=[
            pl.BlockSpec(memory_space=pltpu.SMEM),
            pl.BlockSpec((1, lat, heads), lambda k: (k, 0, 0)),
            pl.BlockSpec((1, lat, cached), lambda k: (k, 0, 0)),
            pl.BlockSpec(handed.shape, lambda k: (0, 0)),
            pl.BlockSpec(marks.shape, lambda k: (0, 0)),
        ],
        out_specs=pl.BlockSpec((1, heads, VDIM), lambda k: (k, 0, 0)),
        out_shape=jax.ShapeDtypeStruct((requests, heads, VDIM), jnp.bfloat16),
        compiler_params=pltpu.CompilerParams(vmem_limit_bytes=VMEM_BYTES),
        cost_estimate=pl.CostEstimate(
            flops=2 * requests * heads * (cached + handed.shape[0]) * (lat + VDIM),
            bytes_accessed=2 * requests * (heads * (lat + VDIM) + cached * lat),
            transcendentals=requests * heads * (cached + handed.shape[0]),
        ),
    )(
        cache_lens,
        jnp.swapaxes(queries, 1, 2),
        jnp.swapaxes(cache_latents, 1, 2),
        handed,
        marks,
    )


def hand_over(prompt_latents, owners, requests):
    n_ep = lax.axis_size("ep")
    stretch, lat = prompt_latents.shape
    cap = 2 * stretch // n_ep
    places_at = jnp.arange(stretch, dtype=jnp.int32)
    earlier = (owners[:, None] == owners[None, :]) & (places_at[None, :] < places_at[:, None])
    target = owners * cap + jnp.sum(earlier.astype(jnp.int32), axis=1)
    slots = jnp.arange(n_ep * cap, dtype=jnp.int32)
    chosen = slots[:, None] == target[None, :]
    packed = jnp.dot(
        chosen.astype(jnp.bfloat16), prompt_latents, preferred_element_type=jnp.float32
    ).astype(jnp.bfloat16)
    mark = jnp.sum(jnp.where(chosen, requests[None, :] + 1, 0), axis=1).astype(jnp.bfloat16)
    fill = -(lat + 1) % 128
    outgoing = jnp.concatenate(
        [packed, mark[:, None], jnp.zeros((n_ep * cap, fill), jnp.bfloat16)], axis=1
    )
    return outgoing.reshape(n_ep, cap, lat + 1 + fill)


def on_device(
    moe_rows,
    routes,
    route_gates,
    gate_proj,
    up_proj,
    down_proj,
    queries,
    cache_latents,
    cache_lens,
    prompt_latents,
    kv_owner,
    kv_request,
):
    sections, count, width = moe_rows.shape
    top = routes.shape[2]
    expert_out, attended = layer(
        moe_rows.reshape(sections * count, width),
        routes.reshape(sections * count, top),
        route_gates.reshape(sections * count, top),
        prompt_latents,
        kv_owner[:, 0],
        kv_request,
        queries,
        cache_latents,
        cache_lens,
        gate_proj,
        up_proj,
        down_proj,
    )
    expert_out = expert_out.reshape(moe_rows.shape)
    return (expert_out, attended)


def solution(mesh):
    placed = (
        P("section", ("groups", "ep"), None),
        P("section", ("groups", "ep"), None),
        P("section", ("groups", "ep"), None),
        P(None, "ep"),
        P(None, "ep"),
        P("ep", None),
        P(("groups", "ep"), None, None),
        P(("groups", "ep"), None, None),
        P(("groups", "ep")),
        P(("groups", "ep"), None),
        P(("groups", "ep"), None),
        P(("groups", "ep")),
    )
    return jax.shard_map(
        on_device,
        mesh=mesh,
        in_specs=placed,
        out_specs=(P("section", ("groups", "ep"), None), P(("groups", "ep"), None, None)),
        check_vma=False,
    )
```

```python
from functools import partial

import jax
import jax.numpy as jnp
from jax import lax
from jax.experimental import pallas as pl
from jax.experimental.pallas import tpu as pltpu
from jax.sharding import PartitionSpec as P

VDIM = 512
FF_WIN = 1024
CORE, XBIT, YBIT = 1, 2, 4
VMEM_BYTES = 60 * 1024 * 1024
SMALL_BYTES = 14 * 1024 * 1024


score_scale = 0.07216878364870323


def swap(value, bit):
    count = lax.axis_size("ep")
    return lax.ppermute(value, "ep", [(i, i ^ bit) for i in range(count)])


def shift(value, step):
    count = lax.axis_size("ep")
    return lax.ppermute(value, "ep", [(i, (i + step) % count) for i in range(count)])


def cross(value, step):
    count = lax.axis_size("ep")
    pairs = [(i, (i + step) % count ^ YBIT) for i in range(count)]
    return lax.ppermute(value, "ep", pairs)


def together(*values):
    return lax.optimization_barrier(values)


def pair_dot(rows, left, right):
    both = jnp.concatenate([left[...], right[...]], axis=1)
    return jnp.dot(rows, both, preferred_element_type=jnp.float32)


def gated(gate, up):
    return (gate / (1.0 + jnp.exp(-gate)) * up).astype(jnp.bfloat16)


def pack_kernel(chosen, rows, *outs):
    picked = jnp.dot(chosen[...], rows[...], preferred_element_type=jnp.float32)
    picked = picked.astype(jnp.bfloat16)
    slots = outs[0].shape[0]
    for at, out in enumerate(outs):
        out[...] = picked[at * slots : (at + 1) * slots]


def packs(chosen, rows, planes, chunk):
    count, width = rows.shape
    slots = chosen.shape[0] // planes
    return pl.pallas_call(
        pack_kernel,
        grid=(width // chunk,),
        in_specs=[
            pl.BlockSpec(chosen.shape, lambda k: (0, 0)),
            pl.BlockSpec((count, chunk), lambda k: (0, k)),
        ],
        out_specs=[pl.BlockSpec((slots, chunk), lambda k: (0, k))] * planes,
        out_shape=[jax.ShapeDtypeStruct((slots, width), jnp.bfloat16)] * planes,
        compiler_params=pltpu.CompilerParams(vmem_limit_bytes=SMALL_BYTES),
        cost_estimate=pl.CostEstimate(
            flops=2 * chosen.size * width,
            bytes_accessed=2 * width * (count + planes * slots),
            transcendentals=0,
        ),
    )(chosen, rows)


def hidden_kernel(count, *refs):
    units, weights = refs[:count], refs[count : count + 8]
    gate_o, gate_c, gate_x, gate_xc, up_o, up_c, up_x, up_xc = weights
    out, near_gate, far_gate, near_up, far_up = refs[count + 8 :]
    step = pl.program_id(0)

    @pl.when(step == 0)
    def _():
        for total in (near_gate, far_gate, near_up, far_up):
            total[...] = jnp.zeros_like(total)

    rows = jnp.concatenate([unit[...] for unit in units], axis=0)
    near_gate[...] += pair_dot(rows, gate_o, gate_c)
    near_up[...] += pair_dot(rows, up_o, up_c)
    far_gate[...] += pair_dot(rows, gate_x, gate_xc)
    far_up[...] += pair_dot(rows, up_x, up_xc)

    @pl.when(step == pl.num_programs(0) - 1)
    def _():
        two = near_up.shape[1]
        out[:, :two] = gated(near_gate[...], near_up[...])
        out[:, two:] = gated(far_gate[...], far_up[...])


def hidden_units(units, weights, chunk):
    width, wide = weights[0].shape
    count = sum(unit.shape[0] for unit in units)
    return pl.pallas_call(
        partial(hidden_kernel, len(units)),
        grid=(width // chunk,),
        in_specs=[pl.BlockSpec((unit.shape[0], chunk), lambda k: (0, k)) for unit in units]
        + [pl.BlockSpec((chunk, wide), lambda k: (k, 0)) for _ in weights],
        out_specs=pl.BlockSpec((count, 4 * wide), lambda k: (0, 0)),
        out_shape=jax.ShapeDtypeStruct((count, 4 * wide), jnp.bfloat16),
        scratch_shapes=[pltpu.VMEM((count, 2 * wide), jnp.float32)] * 4,
        compiler_params=pltpu.CompilerParams(vmem_limit_bytes=VMEM_BYTES),
        cost_estimate=pl.CostEstimate(
            flops=2 * count * width * wide * 8,
            bytes_accessed=2 * width * (count + wide * 8),
            transcendentals=0,
        ),
    )(*units, *weights)


def down_kernel(mine, other, own, own_c, side_0, side_0c, side_1, side_1c, *outs):
    deep = own.shape[0] // 2
    count = mine.shape[0] // 2
    rows = 2 * count // len(outs)

    def fill(side, side_c):
        parts = (own, own_c, side, side_c)
        table = jnp.concatenate(
            [part[:deep, :] for part in parts] + [part[deep:, :] for part in parts], axis=0
        )
        joined = jnp.concatenate(
            [
                jnp.concatenate([mine[:count, :], other[count:, :]], axis=1),
                jnp.concatenate([mine[count:, :], other[:count, :]], axis=1),
            ],
            axis=0,
        )
        value = jnp.dot(joined, table, preferred_element_type=jnp.float32).astype(jnp.bfloat16)
        for at, out in enumerate(outs):
            out[...] = value[at * rows : (at + 1) * rows]

    first = pl.program_id(0) < pl.num_programs(0) // 2

    @pl.when(first)
    def _():
        fill(side_0, side_0c)

    @pl.when(jnp.logical_not(first))
    def _():
        fill(side_1, side_1c)


def down_values(mine, other, own, firsts, seconds, planes, chunk):
    count, inner = mine.shape
    deep, width = own[0].shape
    rows = count // (2 * planes)
    steps = width // chunk
    half = steps // 2
    return pl.pallas_call(
        down_kernel,
        grid=(steps,),
        in_specs=[pl.BlockSpec((count, inner), lambda k: (0, 0))] * 2
        + [pl.BlockSpec((deep, chunk), lambda k: (0, k)) for _ in own]
        + [pl.BlockSpec((deep, chunk), lambda k: (0, jnp.minimum(k, half - 1))) for _ in firsts]
        + [pl.BlockSpec((deep, chunk), lambda k: (0, jnp.maximum(k - half, 0))) for _ in seconds],
        out_specs=[pl.BlockSpec((rows, chunk), lambda k: (0, k))] * (2 * planes),
        out_shape=[jax.ShapeDtypeStruct((rows, width), jnp.bfloat16)] * (2 * planes),
        compiler_params=pltpu.CompilerParams(vmem_limit_bytes=VMEM_BYTES),
        cost_estimate=pl.CostEstimate(
            flops=2 * count * 2 * inner * width,
            bytes_accessed=8 * deep * width + 2 * count * width,
            transcendentals=0,
        ),
    )(mine, other, *own, *firsts, *seconds)


ARRIVAL = (4, 1, 2, 6, 7, 5, 3, 0)


def combine_kernel(upper, high, low, *refs):
    out = refs[-1]
    planes = len(ARRIVAL) // 2
    parts = [refs[ARRIVAL.index(at)] for at in range(2 * planes)]

    def mix(chosen):
        values = jnp.concatenate([part[...] for part in chosen], axis=0)
        total = jnp.dot(high[...], values, preferred_element_type=jnp.float32)
        total = total + jnp.dot(low[...], values, preferred_element_type=jnp.float32)
        out[...] = total.astype(jnp.bfloat16)

    side = pl.program_id(0)

    @pl.when(side == 0)
    def _():
        mix(parts[:planes])

    @pl.when(side == 1)
    def _():
        mix(parts[planes:])


def combine(upper, high, low, mine, theirs, chunk):
    rows, width = mine[0].shape
    count = high.shape[0]
    steps = width // chunk

    def own_block(g, k, upper):
        return 0, jnp.where(g == 0, k, steps - 1)

    def other_block(g, k, upper):
        return 0, jnp.where(g == 0, 0, k)

    def out_block(g, k, upper):
        return 0, (upper[0] + g) % 2 * steps + k

    return pl.pallas_call(
        combine_kernel,
        grid_spec=pltpu.PrefetchScalarGridSpec(
            num_scalar_prefetch=1,
            grid=(2, steps),
            in_specs=[pl.BlockSpec(high.shape, lambda g, k, upper: (0, 0))] * 2
            + [
                pl.BlockSpec((rows, chunk), own_block if at < len(mine) else other_block)
                for at in ARRIVAL
            ],
            out_specs=pl.BlockSpec((count, chunk), out_block),
        ),
        out_shape=jax.ShapeDtypeStruct((count, 2 * width), jnp.bfloat16),
        compiler_params=pltpu.CompilerParams(vmem_limit_bytes=SMALL_BYTES),
        cost_estimate=pl.CostEstimate(
            flops=8 * high.size * width,
            bytes_accessed=4 * width * (len(mine) * rows + count),
            transcendentals=0,
        ),
    )(upper.reshape(1), high, low, *[(*mine, *theirs)[at] for at in ARRIVAL])


def places(picks, planes, split):
    count = picks.shape[0]
    plane = lax.axis_index("ep") // split
    experts = (plane + jnp.arange(planes, dtype=jnp.int32)) % planes
    named = jnp.any(picks[None] == experts[:, None, None], axis=2)
    order = jnp.arange(count, dtype=jnp.int32)
    before = order[:, None] < order[None, :]
    rank = jnp.sum((named[:, :, None] & before[None]).astype(jnp.int32), axis=1)
    return experts, named, rank


def gate_table(picks, gates, planes, split, slots):
    experts, named, rank = places(picks, planes, split)
    weight = jnp.sum(
        jnp.where(picks[None] == experts[:, None, None], gates[None], jnp.zeros_like(gates)[None]),
        axis=2,
    )
    at = jnp.arange(slots, dtype=jnp.int32)
    found = (rank.T[:, :, None] == at[None, None, :]) & named.T[:, :, None]
    return jnp.where(found, weight.T[:, :, None], 0.0)


def layer(
    rows,
    picks,
    gates,
    latents,
    owners,
    requests,
    queries,
    cache_latents,
    cache_lens,
    gate_proj,
    up_proj,
    down_proj,
):
    n_ep = lax.axis_size("ep")
    split = FF_WIN // gate_proj.shape[1]
    planes = n_ep // split
    count, width = rows.shape
    slots = -(-3 * count * picks.shape[1] // (2 * planes * 16)) * 16
    chunk = width // 2
    upper = lax.axis_index("ep") // YBIT % 2
    span = width // 4

    gate_x = swap(gate_proj, XBIT)
    _, named, rank = places(picks, planes, split)
    at = jnp.arange(slots, dtype=jnp.int32)
    chosen = (rank[:, None, :] == at[None, :, None]) & named[:, None, :]
    chosen = chosen.astype(jnp.bfloat16)

    pack_0, out_1, out_2, out_3 = packs(
        chosen.reshape(planes * slots, count), rows, planes, span
    )
    pack_0, out_1, out_3, latents, owners, requests = together(
        pack_0, out_1, out_3, latents, owners, requests
    )
    own_1, own_3, peer_0 = shift(out_1, split), shift(out_3, 3 * split), swap(pack_0, YBIT)
    send = lax.dynamic_slice_in_dim(down_proj, (2 - 2 * upper) * span, 2 * span, 1)
    down_y = swap(send, YBIT)
    outgoing = hand_over(latents, owners, requests)

    own_1, own_3, peer_0, down_y, gate_x, out_2, outgoing, down_proj, gate_proj = together(
        own_1, own_3, peer_0, down_y, gate_x, out_2, outgoing, down_proj, gate_proj
    )
    own_2, peer_1, peer_3 = shift(out_2, 2 * split), swap(own_1, YBIT), swap(own_3, YBIT)
    up_x, gate_c = swap(up_proj, XBIT), swap(gate_proj, CORE)
    keep = lax.dynamic_slice_in_dim(down_proj, 2 * upper * span, 2 * span, 1)
    own = jnp.concatenate([keep, down_y], axis=0)
    begin, rest = own[:, :span], own[:, span:]

    own_2, peer_1, peer_3, up_x, gate_x, gate_c, up_proj, own, begin, rest = together(
        own_2, peer_1, peer_3, up_x, gate_x, gate_c, up_proj, own, begin, rest
    )
    outgoing, own_2 = together(outgoing, own_2)
    peer_2, side_0 = swap(own_2, YBIT), swap(begin, XBIT)
    up_c, gate_xc, up_xc = swap(up_proj, CORE), swap(gate_x, CORE), swap(up_x, CORE)
    incoming = lax.all_to_all(outgoing, "ep", split_axis=0, concat_axis=0, tiled=True)
    peer_2, up_c, gate_xc, up_xc, side_0, rest, own, picks, gates, incoming = together(
        peer_2, up_c, gate_xc, up_xc, side_0, rest, own, picks, gates, incoming
    )
    own_c, side_0c, side_1 = swap(own, CORE), swap(side_0, CORE), swap(rest, XBIT)
    units = (pack_0, own_1, own_2, own_3, peer_0, peer_1, peer_2, peer_3)
    weights = (gate_proj, gate_c, gate_x, gate_xc, up_proj, up_c, up_x, up_xc)
    hidden = hidden_units(units, weights, chunk)
    hidden, own_c, side_0c, picks, gates = together(hidden, own_c, side_0c, picks, gates)
    table = gate_table(picks, gates, planes, split, slots).reshape(count, planes * slots)
    high = lax.reduce_precision(table, 8, 7)
    high, low = high.astype(jnp.bfloat16), (table - high).astype(jnp.bfloat16)
    other, side_1, high, low = together(swap(hidden, YBIT), side_1, high, low)
    firsts, seconds = (side_0, side_0c), (side_1, swap(side_1, CORE))
    values = down_values(hidden, other, (own, own_c), firsts, seconds, planes, span)
    mine, theirs = list(values[:planes]), list(values[planes:])
    theirs[0] = swap(theirs[0], YBIT)
    mine[1] = shift(mine[1], n_ep - split)
    mine[2], theirs[2] = shift(mine[2], n_ep - 2 * split), cross(theirs[2], n_ep - 2 * split)
    theirs[3] = cross(theirs[3], n_ep - 3 * split)
    theirs[1] = cross(theirs[1], n_ep - split)
    mine[3] = shift(mine[3], n_ep - 3 * split)
    handed = incoming.reshape(-1, incoming.shape[2])
    mine[0], handed = together(mine[0], handed)
    marks = handed[:, latents.shape[1]].astype(jnp.float32)[None, :]
    attended = attend(queries, cache_latents, cache_lens, handed, marks)
    theirs[0], attended = together(theirs[0], attended)
    return combine(upper, high, low, mine, theirs, 2 * span), attended


def attend_kernel(lens, query, cache, handed, marks, out):
    request = pl.program_id(0)
    heads = query.shape[2]
    wide = out.shape[2]
    lat = query.shape[1]
    asked = query[0].astype(jnp.float32).T.astype(jnp.bfloat16)
    given = handed[:, :lat]
    near = jnp.dot(asked, cache[0], preferred_element_type=jnp.float32) * score_scale
    over_last = (((1,), (1,)), ((), ()))
    far = lax.dot_general(asked, given, over_last, preferred_element_type=jnp.float32)
    far = far * score_scale
    place = lax.broadcasted_iota(jnp.int32, (heads, near.shape[1]), 1)
    near = jnp.where(place < lens[request], near, -jnp.inf)
    mark = (request + 1).astype(jnp.float32)
    far = jnp.where(jnp.broadcast_to(marks[...], far.shape) == mark, far, -jnp.inf)
    top = jnp.maximum(
        jnp.max(near, axis=1, keepdims=True), jnp.max(far, axis=1, keepdims=True)
    )
    near, far = jnp.exp(near - top), jnp.exp(far - top)
    total = jnp.sum(near, axis=1, keepdims=True) + jnp.sum(far, axis=1, keepdims=True)
    near, far = (near / total).astype(jnp.bfloat16), (far / total).astype(jnp.bfloat16)
    result = lax.dot_general(near, cache[0, :wide], over_last, preferred_element_type=jnp.float32)
    result = result + jnp.dot(far, given[:, :wide], preferred_element_type=jnp.float32)
    out[0] = result.astype(jnp.bfloat16)


def attend(queries, cache_latents, cache_lens, handed, marks):
    requests, heads, lat = queries.shape
    cached = cache_latents.shape[1]
    return pl.pallas_call(
        attend_kernel,
        grid=(requests,),
        in_specs=[
            pl.BlockSpec(memory_space=pltpu.SMEM),
            pl.BlockSpec((1, lat, heads), lambda k: (k, 0, 0)),
            pl.BlockSpec((1, lat, cached), lambda k: (k, 0, 0)),
            pl.BlockSpec(handed.shape, lambda k: (0, 0)),
            pl.BlockSpec(marks.shape, lambda k: (0, 0)),
        ],
        out_specs=pl.BlockSpec((1, heads, VDIM), lambda k: (k, 0, 0)),
        out_shape=jax.ShapeDtypeStruct((requests, heads, VDIM), jnp.bfloat16),
        compiler_params=pltpu.CompilerParams(vmem_limit_bytes=VMEM_BYTES),
        cost_estimate=pl.CostEstimate(
            flops=2 * requests * heads * (cached + handed.shape[0]) * (lat + VDIM),
            bytes_accessed=2 * requests * (heads * (lat + VDIM) + cached * lat),
            transcendentals=requests * heads * (cached + handed.shape[0]),
        ),
    )(
        cache_lens,
        jnp.swapaxes(queries, 1, 2),
        jnp.swapaxes(cache_latents, 1, 2),
        handed,
        marks,
    )


def hand_over(prompt_latents, owners, requests):
    n_ep = lax.axis_size("ep")
    stretch, lat = prompt_latents.shape
    cap = 2 * stretch // n_ep
    places_at = jnp.arange(stretch, dtype=jnp.int32)
    earlier = (owners[:, None] == owners[None, :]) & (places_at[None, :] < places_at[:, None])
    target = owners * cap + jnp.sum(earlier.astype(jnp.int32), axis=1)
    slots = jnp.arange(n_ep * cap, dtype=jnp.int32)
    chosen = slots[:, None] == target[None, :]
    packed = jnp.dot(
        chosen.astype(jnp.bfloat16), prompt_latents, preferred_element_type=jnp.float32
    ).astype(jnp.bfloat16)
    mark = jnp.sum(jnp.where(chosen, requests[None, :] + 1, 0), axis=1).astype(jnp.bfloat16)
    fill = -(lat + 1) % 128
    outgoing = jnp.concatenate(
        [packed, mark[:, None], jnp.zeros((n_ep * cap, fill), jnp.bfloat16)], axis=1
    )
    return outgoing.reshape(n_ep, cap, lat + 1 + fill)


def on_device(
    moe_rows,
    routes,
    route_gates,
    gate_proj,
    up_proj,
    down_proj,
    queries,
    cache_latents,
    cache_lens,
    prompt_latents,
    kv_owner,
    kv_request,
):
    sections, count, width = moe_rows.shape
    top = routes.shape[2]
    expert_out, attended = layer(
        moe_rows.reshape(sections * count, width),
        routes.reshape(sections * count, top),
        route_gates.reshape(sections * count, top),
        prompt_latents,
        kv_owner[:, 0],
        kv_request,
        queries,
        cache_latents,
        cache_lens,
        gate_proj,
        up_proj,
        down_proj,
    )
    expert_out = expert_out.reshape(moe_rows.shape)
    return (expert_out, attended)


def solution(mesh):
    placed = (
        P("section", ("groups", "ep"), None),
        P("section", ("groups", "ep"), None),
        P("section", ("groups", "ep"), None),
        P(None, "ep"),
        P(None, "ep"),
        P("ep", None),
        P(("groups", "ep"), None, None),
        P(("groups", "ep"), None, None),
        P(("groups", "ep")),
        P(("groups", "ep"), None),
        P(("groups", "ep"), None),
        P(("groups", "ep")),
    )
    return jax.shard_map(
        on_device,
        mesh=mesh,
        in_specs=placed,
        out_specs=(P("section", ("groups", "ep"), None), P(("groups", "ep"), None, None)),
        check_vma=False,
    )
```
